32 devices in a mesh: dp: 8 (over z, y), tensor: 4 (over x, core).
Axes of the slice: x: 2, y: 2, z: 4, core: 2. Of those that a mesh axis runs over, the one named last changes fastest.
Arguments:
- tokens: bfloat16 [8192, 1024], P(('dp', 'tensor')), may hold values from -6 to 6
- qkv_weight: bfloat16 [3, 1024, 1024], P(None, None, 'tensor'), may hold values from -0.25 to 0.25
- qv_bias: bfloat16 [2, 1024], P(None, 'tensor'), may hold values from -2 to 2
- out_weight: bfloat16 [1024, 1024], P('tensor'), may hold values from -0.5 to 0.5
- out_bias: bfloat16 [1024], replicated, may hold values from -2 to 2
- norm1_gain: bfloat16 [1024], replicated, may hold values from 0.099609375 to 1.8984375
- norm1_bias: bfloat16 [1024], replicated, may hold values from -2 to 2
- up_weight: bfloat16 [1024, 4096], P(None, 'tensor'), may hold values from -0.1875 to 0.1875
- up_bias: bfloat16 [4096], P('tensor'), may hold values from -2 to 2
- down_weight: bfloat16 [4096, 1024], P('tensor'), may hold values from -0.09375 to 0.09375
- down_bias: bfloat16 [1024], replicated, may hold values from -2 to 2
- norm2_gain: bfloat16 [1024], replicated, may hold values from 0.099609375 to 1.8984375
- norm2_bias: bfloat16 [1024], replicated, may hold values from -2 to 2
- cotangent: bfloat16 [8192, 1024], P(('dp', 'tensor')), may hold values from -7 to 7
Outputs:
- layer_out: bfloat16 [8192, 1024], P(('dp', 'tensor'))
- token_grad: float32 [8192, 1024], P(('dp', 'tensor'))
- qkv_grad: float32 [3, 1024, 1024], P(None, None, 'tensor')
- qv_bias_grad: float32 [2, 1024], P(None, 'tensor')
- out_weight_grad: float32 [1024, 1024], P('tensor')
- out_bias_grad: float32 [1024], replicated
- norm1_gain_grad: float32 [1024], replicated
- norm1_bias_grad: float32 [1024], replicated
- up_weight_grad: float32 [1024, 4096], P(None, 'tensor')
- up_bias_grad: float32 [4096], P('tensor')
- down_weight_grad: float32 [4096, 1024], P('tensor')
- down_bias_grad: float32 [1024], replicated
- norm2_gain_grad: float32 [1024], replicated
- norm2_bias_grad: float32 [1024], replicated
The draws below stay inside these ranges and needn't reach their ends.
All inputs are finite; a program needn't handle non-finite values.
Results may differ from the reference program's by a relative error of at most 0.014.
The reference program's roundings to bfloat16 on the way count: a program that leaves them out, or rounds other values in their place, can miss the bound.
Values may be sent and summed in bfloat16 or wider, within the bound.
No kernel may reach another device: no remote copies, remote signals or barrier semaphores. Data moves between devices by JAX's collectives and lax.ppermute only.
A program may use at most 128 MiB of HBM per device.

```python
import math
import jax
import jax.numpy as jnp
from jax import lax

D = 1024
HEADS = 16
HEAD_SIZE = 64
FF = 4096
LENGTH = 512
TOKENS = 8192


def draw_cotangent(key, part):
    key = jax.random.fold_in(key, 7)
    row_rise = jnp.arange(TOKENS, dtype=jnp.float32)[:, None] / max(TOKENS - 1, 1)
    base_draw = jax.random.truncated_normal(key, -3.5, 3.5, (TOKENS, D), jnp.float32)
    return (base_draw * (0.6 + 1.2 * row_rise)).astype(jnp.bfloat16)


def block_levels(stream_key, extent, split, least, top_value):
    def one(dim, shards_of):
        draws = jax.random.uniform(jax.random.fold_in(jax.random.fold_in(stream_key, 6), dim), (shards_of,), jnp.float32, least / len(split), top_value / len(split))
        return jnp.repeat(jnp.exp(draws), extent[dim] // shards_of).reshape((-1,) + (1,) * (len(extent) - dim - 1))

    level = one(*split[0])
    for cut in split[1:]:
        level = level * one(*cut)
    return level


def centred(key, extent, deviation, limit, split=(), kind=jnp.bfloat16):
    loudness = block_levels(key, extent, split, -0.22, 0.18) if split else 1.0
    entries = jax.random.normal(key, extent, jnp.float32) * deviation * loudness
    return jnp.minimum(jnp.maximum(entries, -limit), limit).astype(kind)


def setup_inputs(seed: int = 0) -> dict:
    seeds = jax.random.split(jax.random.key(seed), 15)
    tokens = centred(seeds[0], (TOKENS, D), 1.0, 6.0, ((0, 32),))
    qkv_weight = centred(seeds[1], (3, D, D), (D // 2) ** -0.5, 0.25, ((2, 4),))
    qv_bias = centred(seeds[2], (2, D), 0.3, 2.0, ((1, 4),))
    out_weight = centred(seeds[3], (D, D), (D // 8) ** -0.5, 0.5, ((0, 4),))
    out_bias = centred(seeds[4], (D,), 0.3, 2.0)
    norm1_gain = jnp.clip(1.0 + 0.18 * jax.random.normal(seeds[5], (D,), jnp.float32), 0.099609375, 1.8984375).astype(jnp.bfloat16)
    norm1_bias = centred(seeds[6], (D,), 0.3, 2.0)
    up_weight = centred(seeds[7], (D, FF), D ** -0.5, 0.1875, ((1, 4),))
    up_bias = centred(seeds[8], (FF,), 0.3, 2.0, ((0, 4),))
    down_weight = centred(seeds[9], (FF, D), FF ** -0.5, 0.09375, ((0, 4),))
    down_bias = centred(seeds[10], (D,), 0.3, 2.0)
    norm2_gain = jnp.clip(1.0 + 0.18 * jax.random.normal(seeds[11], (D,), jnp.float32), 0.099609375, 1.8984375).astype(jnp.bfloat16)
    norm2_bias = centred(seeds[12], (D,), 0.3, 2.0)
    cotangent = draw_cotangent(jax.random.fold_in(seeds[14], 71), 0)
    return {"tokens": tokens, "qkv_weight": qkv_weight, "qv_bias": qv_bias, "out_weight": out_weight, "out_bias": out_bias, "norm1_gain": norm1_gain, "norm1_bias": norm1_bias, "up_weight": up_weight, "up_bias": up_bias, "down_weight": down_weight, "down_bias": down_bias, "norm2_gain": norm2_gain, "norm2_bias": norm2_bias, "cotangent": cotangent}


@jax.custom_vjp
def low(v):
    return lax.optimization_barrier(v.astype(jnp.bfloat16)).astype(jnp.float32)

@jax.custom_vjp
def low_back(v):
    return v

def low_keep(v):
    return (low(v), None)

def low_pass(kept, grad):
    return (grad,)

def back_keep(v):
    return (v, None)

def back_low(kept, grad):
    return (low(grad),)
low.defvjp(low_keep, low_pass)
low_back.defvjp(back_keep, back_low)
EPSILON = 1e-05
PRECISE = lax.Precision.HIGHEST

def normalize(values, gain, shift):
    center = values - lax.optimization_barrier(jnp.mean(values, -1, keepdims=True))
    spread = lax.optimization_barrier(jnp.mean(center * center, -1, keepdims=True))
    return center * lax.rsqrt(spread + EPSILON) * gain + shift

def group_forward(params, seq_group):
    qkv_weight, qv_bias, out_weight, out_bias, norm1_gain, norm1_bias, up_weight, up_bias, down_weight, down_bias, norm2_gain, norm2_bias = params
    flat_rows = seq_group.reshape(-1, D)
    query_rows = low_back(low((jnp.dot(flat_rows, qkv_weight[0], precision=PRECISE) + qv_bias[0]) * 0.125))
    key_rows = low_back(low(jnp.dot(flat_rows, qkv_weight[1], precision=PRECISE)))
    value_rows = low_back(low(jnp.dot(flat_rows, qkv_weight[2], precision=PRECISE) + qv_bias[1]))
    head_shape = (seq_group.shape[0], LENGTH, HEADS, HEAD_SIZE)
    scores = low_back(jnp.einsum('gqhe,gkhe->ghqk', query_rows.reshape(head_shape), key_rows.reshape(head_shape), precision=PRECISE))
    attn_probs = low(jax.nn.softmax(scores, axis=-1))
    head_mixed = jnp.einsum('ghqk,gkhe->gqhe', attn_probs, value_rows.reshape(head_shape), precision=PRECISE)
    head_mixed = low_back(low(head_mixed.reshape(-1, D)))
    attended = low_back(jnp.dot(head_mixed, out_weight, precision=PRECISE))
    normed = normalize(flat_rows + attended + out_bias, norm1_gain, norm1_bias)
    hidden_pre = low_back(jnp.dot(low(normed), up_weight, precision=PRECISE) + up_bias)
    hidden_act = low(jax.nn.gelu(hidden_pre, approximate=False))
    branch_out = low_back(jnp.dot(hidden_act, down_weight, precision=PRECISE))
    result = normalize(normed + branch_out + down_bias, norm2_gain, norm2_bias)
    return result.reshape(seq_group.shape)

def reference(tokens, qkv_weight, qv_bias, out_weight, out_bias, norm1_gain, norm1_bias, up_weight, up_bias, down_weight, down_bias, norm2_gain, norm2_bias, cotangent):
    params = tuple((item.astype(jnp.float32) for item in (qkv_weight, qv_bias, out_weight, out_bias, norm1_gain, norm1_bias, up_weight, up_bias, down_weight, down_bias, norm2_gain, norm2_bias)))
    inputs = tokens.astype(jnp.float32)
    seq_total = TOKENS // LENGTH
    per_group = math.gcd(seq_total, max(1, 4096 // LENGTH))
    checked = jax.checkpoint(group_forward)

    def forward_all(params, inputs):
        grouped = inputs.reshape(seq_total // per_group, per_group, LENGTH, D)

        def scan_step(carried, seq_group):
            return (carried, checked(params, seq_group))
        _, outputs = lax.scan(scan_step, jnp.zeros((), jnp.float32), grouped)
        return outputs.reshape(TOKENS, D)
    output_full, pullback = jax.vjp(forward_all, params, inputs)
    grad_params, grad_inputs = pullback(cotangent.astype(jnp.float32))
    return (output_full.astype(jnp.bfloat16), grad_inputs, grad_params[0], grad_params[1], grad_params[2], grad_params[3], grad_params[4], grad_params[5], grad_params[6], grad_params[7], grad_params[8], grad_params[9], grad_params[10], grad_params[11])
```

```python
import functools

import jax
import jax.numpy as jnp
import numpy as np
from jax import lax
from jax.experimental import pallas as pl
from jax.experimental.pallas import tpu as pltpu
from jax.sharding import PartitionSpec as P

HEAD_SIZE = 64
LENGTH = 512
EPSILON = 1e-05
BF16 = jnp.bfloat16
F32 = jnp.float32
RING = 8


def dot(a, b):
    return jnp.dot(a, b, preferred_element_type=F32)


def dot_t(a, b):
    return lax.dot_general(a, b, (((1,), (1,)), ((), ())), preferred_element_type=F32)


def dot_l(a, b):
    return lax.dot_general(a, b, (((0,), (0,)), ((), ())), preferred_element_type=F32)


def attend_kernel(first, second, weight, bias, query, key, value, mixed_first, mixed_second):
    rows = first.shape[0]
    width = query.shape[1]
    bias_wide = bias[...].astype(F32)
    for half, part in enumerate((first, second)):
        block = pl.ds(half * rows, rows)
        part = part[...]
        query[block, :] = ((dot(part, weight[0]) + bias_wide[0:1, :]) * 0.125).astype(BF16)
        key[block, :] = dot(part, weight[1]).astype(BF16)
        value[block, :] = (dot(part, weight[2]) + bias_wide[1:2, :]).astype(BF16)
    lane = lax.broadcasted_iota(jnp.int32, (rows, 128), 1)
    low_half = lane < HEAD_SIZE
    for half, mixed in enumerate((mixed_first, mixed_second)):
        block = pl.ds(half * rows, rows)
        for pair in range(width // 128):
            cols = pl.ds(pair * 128, 128)
            q_pair = query[block, cols]
            k_pair = key[:, cols]
            v_pair = value[:, cols]
            outs = []
            for side in range(2):
                keep = low_half if side == 0 else ~low_half
                scores = dot_t(jnp.where(keep, q_pair, jnp.zeros_like(q_pair)), k_pair)
                peak = jnp.max(scores, -1, keepdims=True)
                weights = jnp.exp(scores - peak)
                total = jnp.sum(weights, -1, keepdims=True)
                probs = (weights * (1.0 / total)).astype(BF16)
                outs.append(dot(probs, v_pair))
            mixed[:, cols] = jnp.where(low_half, outs[0], outs[1]).astype(BF16)


def attend(first, second, weight, bias):
    rows = first.shape[0]
    width = weight.shape[2]
    whole = jax.ShapeDtypeStruct((2 * rows, width), BF16)
    half = jax.ShapeDtypeStruct((rows, width), BF16)
    return pl.pallas_call(
        attend_kernel,
        out_shape=(whole, whole, whole, half, half),
        compiler_params=pltpu.CompilerParams(vmem_limit_bytes=40 * 2**20),
        cost_estimate=pl.CostEstimate(
            flops=2 * 2 * rows * first.shape[1] * width * 3 + 16 * rows * rows * width * 4,
            bytes_accessed=6 * 2**20,
            transcendentals=0,
        ),
    )(first, second, weight, bias)


def attend_back_kernel(query, key, value, grad_first, grad_second, out, key_sum, value_sum):
    rows = grad_first.shape[0]
    width = query.shape[1]
    lane = lax.broadcasted_iota(jnp.int32, (rows, 128), 1)
    low_half = lane < HEAD_SIZE
    lane_all = lax.broadcasted_iota(jnp.int32, (2 * rows, 128), 1)
    low_all = lane_all < HEAD_SIZE
    for pair in range(width // 128):
        cols = pl.ds(pair * 128, 128)
        k_pair = key[:, cols]
        v_pair = value[:, cols]
        for half, grads in enumerate((grad_first, grad_second)):
            block = pl.ds(half * rows, rows)
            q_pair = query[block, cols]
            g_pair = grads[:, cols]
            dq, dk, dv = [], [], []
            for side in range(2):
                keep = low_half if side == 0 else ~low_half
                scores = dot_t(jnp.where(keep, q_pair, jnp.zeros_like(q_pair)), k_pair)
                peak = jnp.max(scores, -1, keepdims=True)
                weights = jnp.exp(scores - peak)
                total = jnp.sum(weights, -1, keepdims=True)
                probs = weights * (1.0 / total)
                grad_probs = dot_t(jnp.where(keep, g_pair, jnp.zeros_like(g_pair)), v_pair)
                inner = probs * grad_probs
                grad_scores = (
                    inner - probs * jnp.sum(inner, -1, keepdims=True)
                ).astype(BF16)
                dv.append(dot_l(probs.astype(BF16), g_pair))
                dq.append(dot(grad_scores, k_pair))
                dk.append(dot_l(grad_scores, q_pair))
            out[0, block, cols] = (
                jnp.where(low_half, dq[0], dq[1]).astype(BF16).astype(F32) * 0.125
            ).astype(BF16)
            dk_pair = jnp.where(low_all, dk[0], dk[1])
            dv_pair = jnp.where(low_all, dv[0], dv[1])
            if half == 0:
                key_sum[...] = dk_pair
                value_sum[...] = dv_pair
            else:
                out[1, :, cols] = (key_sum[...] + dk_pair).astype(BF16)
                out[2, :, cols] = (value_sum[...] + dv_pair).astype(BF16)


def attend_back(query, key, value, grad_first, grad_second):
    length, width = query.shape
    return pl.pallas_call(
        attend_back_kernel,
        out_shape=jax.ShapeDtypeStruct((3, length, width), BF16),
        scratch_shapes=[pltpu.VMEM((length, 128), F32), pltpu.VMEM((length, 128), F32)],
        compiler_params=pltpu.CompilerParams(vmem_limit_bytes=40 * 2**20),
        cost_estimate=pl.CostEstimate(
            flops=4 * length * length * width * 2 * 5,
            bytes_accessed=2 * 2**20,
            transcendentals=0,
        ),
    )(query, key, value, grad_first, grad_second)


def center_scale(values):
    center = values - jnp.mean(values, -1, keepdims=True)
    spread = jnp.mean(center * center, -1, keepdims=True)
    scale = lax.rsqrt(spread + EPSILON)
    return center * scale, scale


def norm_back(grad, unit, scale, gain):
    grad_unit = grad * gain
    return scale * (
        grad_unit
        - jnp.mean(grad_unit, -1, keepdims=True)
        - unit * jnp.mean(grad_unit * unit, -1, keepdims=True)
    )


def gate(pre):
    cdf = 0.5 * (1.0 + lax.erf(pre * np.float32(np.sqrt(0.5))))
    return pre * cdf


def gate_slope(pre):
    cdf = 0.5 * (1.0 + lax.erf(pre * np.float32(np.sqrt(0.5))))
    return cdf + pre * (np.float32(1 / np.sqrt(2 * np.pi)) * jnp.exp(-0.5 * pre * pre))


def swap(values, bit, tensor):
    return lax.ppermute(values, "tensor", [(i, i ^ bit) for i in range(tensor)])


def ring_sum(grad, dp, forward):
    order = list(range(0, dp, 2)) + list(range(dp - 1, 0, -2))
    place = [0] * dp
    for at, device in enumerate(order):
        place[device] = at
    pairs = [(order[i], order[(i + 1) % dp]) for i in range(dp)]
    sign = 1
    if not forward:
        pairs = [(b, a) for a, b in pairs]
        sign = -1
    pos = jnp.asarray(np.array(place, np.int32))[lax.axis_index("dp")]
    rows, columns = grad.shape[0] // dp, grad.shape[1]

    def chunk(step):
        first = lax.rem(pos + (sign * step) % dp, dp) * rows
        return first

    def own(step):
        return lax.dynamic_slice(grad, (chunk(step), 0), (rows, columns))

    moving = own(0).astype(BF16)
    for step in range(1, dp):
        moving = lax.ppermute(moving, "dp", pairs)
        moving = (moving.astype(F32) + own(-step)).astype(BF16)
    out = jnp.zeros(grad.shape, F32)
    out = lax.dynamic_update_slice(out, moving.astype(F32), (chunk(1), 0))
    for step in range(1, dp):
        moving = lax.ppermute(moving, "dp", pairs)
        out = lax.dynamic_update_slice(out, moving.astype(F32), (chunk(1 - step), 0))
    return out


def dp_sum(grad, dp):
    if dp != RING:
        return lax.psum(grad, "dp")
    half = grad.shape[0] // 2
    return jnp.concatenate([ring_sum(grad[:half], dp, True), ring_sum(grad[half:], dp, False)], 0)


def cube_sum(values, axis, size):
    bit = 1
    while bit < size:
        values = values + lax.ppermute(values, axis, [(i, i ^ bit) for i in range(size)])
        bit *= 2
    return values


def on_device(
    dp,
    tensor,
    tokens,
    qkv_weight,
    qv_bias,
    out_weight,
    out_bias,
    norm1_gain,
    norm1_bias,
    up_weight,
    up_bias,
    down_weight,
    down_bias,
    norm2_gain,
    norm2_bias,
    cotangent,
):
    core = functools.partial(swap, bit=1, tensor=tensor)
    chip = functools.partial(swap, bit=2, tensor=tensor)
    rows, model = tokens.shape
    tok_a = tokens
    tok_c = chip(tok_a)
    tok_b = core(tok_a)
    out_peer = core(out_weight)
    up_peer = core(up_weight)
    down_peer = core(down_weight)
    up_bias_peer = core(up_bias)
    qkv_peer = core(qkv_weight)
    gain1, shift1 = norm1_gain.astype(F32), norm1_bias.astype(F32)
    gain2, shift2 = norm2_gain.astype(F32), norm2_bias.astype(F32)

    q_ab, k_ab, v_ab, mix_a, mix_b = attend(tok_a, tok_b, qkv_weight, qv_bias)
    sum_a = dot(mix_a, out_weight) + dot(core(mix_b), out_peer)
    tok_d = core(tok_c)
    q_cd, k_cd, v_cd, mix_c, mix_d = attend(tok_c, tok_d, qkv_weight, qv_bias)
    sum_c = dot(mix_c, out_weight) + dot(core(mix_d), out_peer)
    low_a, low_c = sum_a.astype(BF16), sum_c.astype(BF16)
    far_c = chip(low_a)
    far_a = chip(low_c)
    out_bias_wide = out_bias.astype(F32)
    first_a = tok_a.astype(F32) + low_a.astype(F32) + far_a.astype(F32) + out_bias_wide
    first_c = tok_c.astype(F32) + low_c.astype(F32) + far_c.astype(F32) + out_bias_wide
    unit1_a, scale1_a = center_scale(first_a)
    unit1_c, _ = center_scale(first_c)
    normed_a = unit1_a * gain1 + shift1
    nrm_a = normed_a.astype(BF16)
    nrm_c = (unit1_c * gain1 + shift1).astype(BF16)

    up_bias_wide = up_bias.astype(F32)
    up_bias_peer_wide = up_bias_peer.astype(F32)

    def feed(nrm):
        pre = dot(nrm, up_weight) + up_bias_wide
        pre_peer = dot(nrm, up_peer) + up_bias_peer_wide
        act, act_peer = gate(pre).astype(BF16), gate(pre_peer).astype(BF16)
        return pre, pre_peer, act, act_peer, dot(act, down_weight) + dot(act_peer, down_peer)

    pre_c, pre_peer_c, act_c, act_peer_c, feed_c = feed(nrm_c)
    far_feed = chip(feed_c.astype(BF16))
    pre_a, pre_peer_a, act_a, act_peer_a, feed_a = feed(nrm_a)
    second_a = normed_a + feed_a + far_feed.astype(F32) + down_bias.astype(F32)
    unit2, scale2 = center_scale(second_a)
    layer_out = (unit2 * gain2 + shift2).astype(BF16)
    cot = cotangent.astype(F32)
    grad_second = norm_back(cot, unit2, scale2, gain2)
    gs_a = grad_second.astype(BF16)
    gs_c = chip(gs_a)
    gs_b, gs_d = core(gs_a), core(gs_c)
    act_b, act_d = core(act_peer_a), core(act_peer_c)
    nrm_b, nrm_d = core(nrm_a), core(nrm_c)

    def stack(*parts):
        return jnp.concatenate(parts, 0)

    def feed_back(gs, pre, pre_peer):
        gp = (gate_slope(pre) * dot_t(gs, down_weight)).astype(BF16)
        gp_peer = (gate_slope(pre_peer) * dot_t(gs, down_peer)).astype(BF16)
        return gp, gp_peer, dot_t(gp, up_weight) + dot_t(gp_peer, up_peer)

    gp_c, gp_peer_c, back_c = feed_back(gs_c, pre_c, pre_peer_c)
    far_back = chip(back_c.astype(BF16))
    gp_a, gp_peer_a, back_a = feed_back(gs_a, pre_a, pre_peer_a)
    gp_b, gp_d = core(gp_peer_a), core(gp_peer_c)
    grad_down = dot_l(stack(act_a, act_b, act_c, act_d), stack(gs_a, gs_b, gs_c, gs_d))
    grad_down = dp_sum(grad_down, dp)
    gp_all = stack(gp_a, gp_b, gp_c, gp_d)
    grad_up = dot_l(stack(nrm_a, nrm_b, nrm_c, nrm_d), gp_all)
    grad_up = dp_sum(grad_up, dp)
    grad_up_bias = jnp.sum(gp_all.astype(F32), 0)

    grad_normed = grad_second + back_a + far_back.astype(F32)
    grad_first = norm_back(grad_normed, unit1_a, scale1_a, gain1)
    gf_a = grad_first.astype(BF16)
    gf_c = chip(gf_a)
    gf_b, gf_d = core(gf_a), core(gf_c)

    def heads_back(gf):
        return dot_t(gf, out_weight).astype(BF16), dot_t(gf, out_peer).astype(BF16)

    gh_a, gh_peer_a = heads_back(gf_a)
    gp_ab = attend_back(q_ab, k_ab, v_ab, gh_a, core(gh_peer_a))
    gh_c, gh_peer_c = heads_back(gf_c)
    gp_cd = attend_back(q_cd, k_cd, v_cd, gh_c, core(gh_peer_c))
    grad_out = dot_l(stack(mix_a, mix_b, mix_c, mix_d), stack(gf_a, gf_b, gf_c, gf_d))

    def proj_back(grads):
        near, far = grads[:, :rows], core(grads[:, rows:])
        total = 0.0
        for i in range(3):
            total = total + dot_t(near[i], qkv_weight[i]) + dot_t(far[i], qkv_peer[i])
        return total

    rows_c = proj_back(gp_cd)
    far_rows = chip(rows_c.astype(BF16))
    token_grad = grad_first + proj_back(gp_ab) + far_rows.astype(F32)
    tok_all = stack(tok_a, tok_b, tok_c, tok_d)
    proj_all = jnp.concatenate([gp_ab, gp_cd], 1)
    grad_qkv = jnp.concatenate([dot_l(tok_all, proj_all[i]) for i in range(3)], 0)
    grad_qkv = dp_sum(grad_qkv, dp).reshape(qkv_weight.shape)
    grad_out = dp_sum(grad_out, dp)
    grad_qv_bias = jnp.sum(proj_all.astype(F32), 1)

    small = jnp.stack(
        [
            jnp.sum(grad_normed * unit1_a, 0),
            jnp.sum(grad_normed, 0),
            jnp.sum(grad_first, 0),
            jnp.sum(cot * unit2, 0),
            jnp.sum(cot, 0),
            jnp.sum(grad_second, 0),
        ]
    )
    small = cube_sum(small, "tensor", tensor)
    flat = jnp.concatenate(
        [small.reshape(-1), grad_up_bias, grad_qv_bias[0], grad_qv_bias[2]]
    )
    flat = cube_sum(flat.reshape(-1, 128), "dp", dp).reshape(-1)
    small = flat[: 6 * model].reshape(6, model)
    hidden = grad_up_bias.shape[0]
    grad_up_bias = flat[6 * model : 6 * model + hidden]
    grad_qv = flat[6 * model + hidden :].reshape(2, -1)
    return (
        layer_out,
        token_grad,
        grad_qkv,
        grad_qv,
        grad_out,
        small[2],
        small[0],
        small[1],
        grad_up,
        grad_up_bias,
        grad_down,
        small[5],
        small[3],
        small[4],
    )


def solution(mesh):
    dp, tensor = mesh.shape["dp"], mesh.shape["tensor"]
    placed = (
        P(("dp", "tensor"), None),
        P(None, None, "tensor"),
        P(None, "tensor"),
        P("tensor", None),
        P(),
        P(),
        P(),
        P(None, "tensor"),
        P("tensor"),
        P("tensor", None),
        P(),
        P(),
        P(),
        P(("dp", "tensor"), None),
    )
    return jax.shard_map(
        functools.partial(on_device, dp, tensor),
        mesh=mesh,
        in_specs=placed,
        out_specs=(
            P(("dp", "tensor"), None),
            P(("dp", "tensor"), None),
            P(None, None, "tensor"),
            P(None, "tensor"),
            P("tensor", None),
            P(),
            P(),
            P(),
            P(None, "tensor"),
            P("tensor"),
            P("tensor", None),
            P(),
            P(),
            P(),
        ),
        check_vma=False,
    )
```

```python
import functools

import jax
import jax.numpy as jnp
import numpy as np
from jax import lax
from jax.experimental import pallas as pl
from jax.experimental.pallas import tpu as pltpu
from jax.sharding import PartitionSpec as P

HEAD_SIZE = 64
LENGTH = 512
EPSILON = 1e-05
BF16 = jnp.bfloat16
F32 = jnp.float32
RING = 8
MIB = 2**20


def dot(a, b):
    return jnp.dot(a, b, preferred_element_type=F32)


def dot_t(a, b):
    return lax.dot_general(a, b, (((1,), (1,)), ((), ())), preferred_element_type=F32)


def dot_l(a, b):
    return lax.dot_general(a, b, (((0,), (0,)), ((), ())), preferred_element_type=F32)


def shape(dims, kind):
    return jax.ShapeDtypeStruct(dims, kind)


def call(body, out_shape, args, vmem, scratch=(), outside=False):
    whole = pl.BlockSpec(memory_space=pltpu.VMEM)
    there = pl.BlockSpec(memory_space=pl.ANY)
    return pl.pallas_call(
        body,
        out_shape=out_shape,
        in_specs=[whole] * len(args),
        out_specs=jax.tree.map(lambda _: there if outside else whole, out_shape),
        scratch_shapes=list(scratch),
        compiler_params=pltpu.CompilerParams(vmem_limit_bytes=vmem * MIB),
        cost_estimate=pl.CostEstimate(flops=1024, bytes_accessed=1024, transcendentals=0),
    )(*args)


def attend_kernel(first, second, weight, bias, query, key, value, mixed_first, mixed_second):
    rows = first.shape[0]
    width = query.shape[1]
    bias_wide = bias[...].astype(F32)
    for half, part in enumerate((first, second)):
        block = pl.ds(half * rows, rows)
        part = part[...]
        query[block, :] = ((dot(part, weight[0]) + bias_wide[0:1, :]) * 0.125).astype(BF16)
        key[block, :] = dot(part, weight[1]).astype(BF16)
        value[block, :] = (dot(part, weight[2]) + bias_wide[1:2, :]).astype(BF16)
    low_half = lax.broadcasted_iota(jnp.int32, (rows, 128), 1) < HEAD_SIZE
    for half, mixed in enumerate((mixed_first, mixed_second)):
        block = pl.ds(half * rows, rows)
        for pair in range(width // 128):
            cols = pl.ds(pair * 128, 128)
            q_pair = query[block, cols]
            k_pair = key[:, cols]
            v_pair = value[:, cols]
            outs = []
            for side in range(2):
                keep = low_half if side == 0 else ~low_half
                scores = dot_t(jnp.where(keep, q_pair, jnp.zeros_like(q_pair)), k_pair)
                weights = jnp.exp(scores - jnp.max(scores, -1, keepdims=True))
                total = jnp.sum(weights, -1, keepdims=True)
                probs = (weights * (1.0 / total)).astype(BF16)
                outs.append(dot(probs, v_pair))
            mixed[:, cols] = jnp.where(low_half, outs[0], outs[1]).astype(BF16)


def attend(first, second, weight, bias):
    rows, model = first.shape
    width = weight.shape[2]
    whole = shape((2 * rows, width), BF16)
    half = shape((rows, width), BF16)
    return call(attend_kernel, (whole, whole, whole, half, half), (first, second, weight, bias), 12)


def attend_back_kernel(query, key, value, grad_first, grad_second, out, key_sum, value_sum):
    rows = grad_first.shape[0]
    width = query.shape[1]
    low_half = lax.broadcasted_iota(jnp.int32, (rows, 128), 1) < HEAD_SIZE
    low_all = lax.broadcasted_iota(jnp.int32, (2 * rows, 128), 1) < HEAD_SIZE
    for pair in range(width // 128):
        cols = pl.ds(pair * 128, 128)
        k_pair = key[:, cols]
        v_pair = value[:, cols]
        for half, grads in enumerate((grad_first, grad_second)):
            block = pl.ds(half * rows, rows)
            q_pair = query[block, cols]
            g_pair = grads[:, cols]
            dq, dk, dv = [], [], []
            for side in range(2):
                keep = low_half if side == 0 else ~low_half
                scores = dot_t(jnp.where(keep, q_pair, jnp.zeros_like(q_pair)), k_pair)
                weights = jnp.exp(scores - jnp.max(scores, -1, keepdims=True))
                total = jnp.sum(weights, -1, keepdims=True)
                probs = weights * (1.0 / total)
                grad_probs = dot_t(jnp.where(keep, g_pair, jnp.zeros_like(g_pair)), v_pair)
                inner = probs * grad_probs
                grad_scores = (inner - probs * jnp.sum(inner, -1, keepdims=True)).astype(BF16)
                dv.append(dot_l(probs.astype(BF16), g_pair))
                dq.append(dot(grad_scores, k_pair))
                dk.append(dot_l(grad_scores, q_pair))
            out[0, block, cols] = (
                jnp.where(low_half, dq[0], dq[1]).astype(BF16).astype(F32) * 0.125
            ).astype(BF16)
            dk_pair = jnp.where(low_all, dk[0], dk[1])
            dv_pair = jnp.where(low_all, dv[0], dv[1])
            if half == 0:
                key_sum[...] = dk_pair
                value_sum[...] = dv_pair
            else:
                out[1, :, cols] = (key_sum[...] + dk_pair).astype(BF16)
                out[2, :, cols] = (value_sum[...] + dv_pair).astype(BF16)


def attend_back(query, key, value, grad_first, grad_second):
    length, width = query.shape
    return call(
        attend_back_kernel,
        shape((3, length, width), BF16),
        (query, key, value, grad_first, grad_second),
        12,
        [pltpu.VMEM((length, 128), F32), pltpu.VMEM((length, 128), F32)],
    )


def two_dots_kernel(transposed, left, right, weight, weight_peer, out):
    product = dot_t if transposed else dot
    out[...] = (product(left[...], weight[...]) + product(right[...], weight_peer[...])).astype(out.dtype)


def mix_out(mix, mix_peer, weight, weight_peer):
    rows, width = mix.shape
    model = weight.shape[1]
    return call(
        functools.partial(two_dots_kernel, False),
        shape((rows, model), BF16),
        (mix, mix_peer, weight, weight_peer),
        4,
    )


def center_scale(values):
    center = values - jnp.mean(values, -1, keepdims=True)
    spread = jnp.mean(center * center, -1, keepdims=True)
    scale = lax.rsqrt(spread + EPSILON)
    return center * scale, scale


def norm_back(grad, unit, scale, gain):
    grad_unit = grad * gain
    return scale * (
        grad_unit
        - jnp.mean(grad_unit, -1, keepdims=True)
        - unit * jnp.mean(grad_unit * unit, -1, keepdims=True)
    )


def first_sum(tok, low, far, out_bias):
    return tok[...].astype(F32) + low[...].astype(F32) + far[...].astype(F32) + out_bias[...].astype(F32)


def gate(pre):
    cdf = 0.5 * (1.0 + lax.erf(pre * np.float32(np.sqrt(0.5))))
    density = np.float32(1 / np.sqrt(2 * np.pi)) * jnp.exp(-0.5 * pre * pre)
    return pre * cdf, cdf + pre * density


def feed_kernel(keep_wide, tok, low, far, out_bias, gain, shift, bias, bias_peer, *refs):
    weights, refs = refs[:4], refs[4:]
    if keep_wide:
        wide, refs = refs[0], refs[1:]
    normed, act, act_peer, slope, slope_peer, out = refs
    unit, _ = center_scale(first_sum(tok, low, far, out_bias))
    value = unit * gain[...].astype(F32) + shift[...].astype(F32)
    if keep_wide:
        wide[...] = value
    normed[...] = value.astype(BF16)
    hidden = act.shape[1]
    step = 256
    for side, (bias_of, act_of, slope_of) in enumerate(((bias, act, slope), (bias_peer, act_peer, slope_peer))):
        for first in range(0, hidden, step):
            cols = pl.ds(first, step)
            pre = dot(normed[...], weights[side][:, cols]) + bias_of[:, cols].astype(F32)
            gated, slant = gate(pre)
            act_of[:, cols] = gated.astype(BF16)
            slope_of[:, cols] = slant
    out[...] = (dot(act[...], weights[2][...]) + dot(act_peer[...], weights[3][...])).astype(out.dtype)


def feed(keep_wide, tok, low, far, out_bias, gain, shift, bias, bias_peer, weights):
    rows, model = tok.shape
    hidden = weights[0].shape[1]
    outs = [shape((rows, model), F32)] if keep_wide else []
    outs += [shape((rows, model), BF16)] + [shape((rows, hidden), BF16)] * 2 + [shape((rows, hidden), F32)] * 2
    outs.append(shape((rows, model), F32 if keep_wide else BF16))
    return call(
        functools.partial(feed_kernel, keep_wide),
        tuple(outs),
        (tok, low, far, out_bias, gain, shift, bias, bias_peer, *weights),
        8,
    )


def second_kernel(normed, feed_sum, far, down_bias, gain, shift, cotangent, layer_out, grad, grad_low, sums):
    second = normed[...] + feed_sum[...] + far[...].astype(F32) + down_bias[...].astype(F32)
    unit, scale = center_scale(second)
    gain_wide = gain[...].astype(F32)
    layer_out[...] = (unit * gain_wide + shift[...].astype(F32)).astype(BF16)
    cot = cotangent[...].astype(F32)
    grad_second = norm_back(cot, unit, scale, gain_wide)
    grad[...] = grad_second
    grad_low[...] = grad_second.astype(BF16)
    sums[...] = jnp.zeros_like(sums)
    sums[0:1, :] = jnp.sum(cot * unit, 0, keepdims=True)
    sums[1:2, :] = jnp.sum(cot, 0, keepdims=True)
    sums[2:3, :] = jnp.sum(grad_second, 0, keepdims=True)


def second_norm(normed, feed_sum, far, down_bias, gain, shift, cotangent):
    rows, model = normed.shape
    outs = (shape((rows, model), BF16), shape((rows, model), F32), shape((rows, model), BF16), shape((8, model), F32))
    args = (normed, feed_sum, far, down_bias, gain, shift, cotangent)
    return call(second_kernel, outs, args, 8)


def feed_back_kernel(grad, slope, slope_peer, up, up_peer, down, down_peer, pre, pre_peer, out):
    hidden = pre.shape[1]
    step = 256
    for slope_of, pre_of, weight in ((slope, pre, down), (slope_peer, pre_peer, down_peer)):
        for first in range(0, hidden, step):
            cols = pl.ds(first, step)
            pre_of[:, cols] = (slope_of[:, cols] * dot_t(grad[...], weight[cols, :])).astype(BF16)
    out[...] = (dot_t(pre[...], up[...]) + dot_t(pre_peer[...], up_peer[...])).astype(out.dtype)


def feed_back(grad, slope, slope_peer, weights, kind):
    rows, model = grad.shape
    hidden = slope.shape[1]
    outs = (shape((rows, hidden), BF16), shape((rows, hidden), BF16), shape((rows, model), kind))
    return call(
        feed_back_kernel,
        outs,
        (grad, slope, slope_peer, *weights),
        8,
    )


def summed(left, right):
    total = dot_l(left[0], right[0])
    for a, b in zip(left[1:], right[1:]):
        total += dot_l(a, b)
    return total


def weight_grad_kernel(parts, sums, *refs):
    left, right, out = refs[:parts], refs[parts : 2 * parts], refs[2 * parts]
    step = 256
    for first in range(0, out.shape[1], step):
        cols = pl.ds(first, step)
        out[:, cols] = summed([part[...] for part in left], [part[:, cols] for part in right])
    if sums:
        ones = jnp.ones((left[0].shape[0], 8), BF16)
        refs[-1][...] = summed([ones] * parts, [part[...] for part in right])


def weight_grad(left, right, sums=False):
    parts = len(left)
    wide, tall = right[0].shape[1], left[0].shape[1]
    outs = [shape((tall, wide), F32)] + ([shape((8, wide), F32)] if sums else [])
    return call(functools.partial(weight_grad_kernel, parts, sums), tuple(outs), (*left, *right), 12)


def first_back_kernel(tok, low, far, out_bias, gain, grad_second, near, far_back, weight, weight_peer, *outs):
    grad, grad_low, heads, heads_peer, sums = outs
    unit, scale = center_scale(first_sum(tok, low, far, out_bias))
    grad_normed = grad_second[...] + near[...] + far_back[...].astype(F32)
    grad_first = norm_back(grad_normed, unit, scale, gain[...].astype(F32))
    grad[...] = grad_first
    grad_low[...] = grad_first.astype(BF16)
    heads[...] = dot_t(grad_low[...], weight[...]).astype(BF16)
    heads_peer[...] = dot_t(grad_low[...], weight_peer[...]).astype(BF16)
    sums[...] = jnp.zeros_like(sums)
    sums[0:1, :] = jnp.sum(grad_normed * unit, 0, keepdims=True)
    sums[1:2, :] = jnp.sum(grad_normed, 0, keepdims=True)
    sums[2:3, :] = jnp.sum(grad_first, 0, keepdims=True)


def first_back(tok, low, far, out_bias, gain, grad_second, near, far_back, weight, weight_peer):
    rows, model = tok.shape
    width = weight.shape[0]
    outs = (
        shape((rows, model), F32),
        shape((rows, model), BF16),
        shape((rows, width), BF16),
        shape((rows, width), BF16),
        shape((8, model), F32),
    )
    args = (tok, low, far, out_bias, gain, grad_second, near, far_back, weight, weight_peer)
    return call(first_back_kernel, outs, args, 8)


def heads_back_kernel(grad, weight, weight_peer, heads, heads_peer):
    heads[...] = dot_t(grad[...], weight[...]).astype(BF16)
    heads_peer[...] = dot_t(grad[...], weight_peer[...]).astype(BF16)


def heads_back(grad, weight, weight_peer):
    rows, model = grad.shape
    width = weight.shape[0]
    outs = (shape((rows, width), BF16), shape((rows, width), BF16))
    return call(heads_back_kernel, outs, (grad, weight, weight_peer), 4)


def proj_back_kernel(near, far, weight, weight_peer, out):
    total = dot_t(near[0], weight[0]) + dot_t(far[0], weight_peer[0])
    for i in (1, 2):
        total += dot_t(near[i], weight[i]) + dot_t(far[i], weight_peer[i])
    out[...] = total.astype(out.dtype)


def proj_back(near, far, weight, weight_peer, kind):
    _, rows, width = near.shape
    model = weight.shape[1]
    args = (near, far, weight, weight_peer)
    return call(proj_back_kernel, shape((rows, model), kind), args, 8)


def ring_grad_kernel(tok_a, tok_b, tok_c, tok_d, near, far, *refs):
    mixes, grads, (out, bias, total) = refs[:4], refs[4:8], refs[8:]
    rows, model = tok_a.shape
    width = near.shape[2]
    chunks = out.shape[0]
    share = width // chunks
    tall = out.shape[1] - model // width * share
    mixed = [part[...] for part in mixes]
    for j in range(model // width):
        block = summed(mixed, [part[:, pl.ds(j * width, width)] for part in grads])
        out[:, pl.ds(tall + j * share, share), :] = block.reshape(chunks, share, width)
    toks = [part[...] for part in (tok_a, tok_b, tok_c, tok_d)]
    ones = [jnp.ones((rows, 8), BF16)] * 4
    for j in range(3):
        right = [part[j, pl.ds(half * rows, rows), :] for part in (near, far) for half in range(2)]
        total[pl.ds(j * model, model), :] = summed(toks, right)
        if j != 1:
            bias[:, pl.ds(j // 2 * width, width)] = summed(ones, right)
    for i in range(chunks):
        out[i, pl.ds(0, tall), :] = total[pl.ds(i * tall, tall), :]


def ring_grad(toks, near, far, mixes, grads, chunks):
    model = toks[0].shape[1]
    width = near.shape[2]
    tall = 4 * model // chunks
    outs = (shape((chunks, tall, width), F32), shape((8, 2 * width), F32))
    return call(ring_grad_kernel, outs, (*toks, near, far, *mixes, *grads), 16, [pltpu.VMEM((3 * model, width), F32)])


def place_kernel(parts, index, *refs):
    chunks, out, wide, semaphores = refs[:parts], refs[parts], refs[-2], refs[-1]
    rows = chunks[0].shape[0]
    copies = []
    for i, chunk in enumerate(chunks):
        wide[i] = chunk[...].astype(F32)
        first = pl.multiple_of(index[i] * rows, 8)
        copies.append(pltpu.make_async_copy(wide.at[i], out.at[pl.ds(first, rows)], semaphores.at[i]))
        copies[-1].start()
    for copy in copies:
        copy.wait()


def place_mixed_kernel(parts, model, index, *refs):
    chunks, out, out_last, wide, last, semaphores, semaphores_last = refs[:parts], *refs[parts:]
    width = chunks[0].shape[1]
    blocks = model // width
    tall = wide.shape[1]
    share = last.shape[1]
    copies = []
    for i, chunk in enumerate(chunks):
        wide[i] = chunk[pl.ds(0, tall), :].astype(F32)
        for j in range(blocks):
            last[i, :, pl.ds(j * width, width)] = chunk[pl.ds(tall + j * share, share), :].astype(F32)
        first = pl.multiple_of(index[i] * tall, 8)
        copies.append(pltpu.make_async_copy(wide.at[i], out.at[pl.ds(first, tall)], semaphores.at[i]))
        first = pl.multiple_of(index[i] * share, 8)
        copies.append(pltpu.make_async_copy(last.at[i], out_last.at[pl.ds(first, share)], semaphores_last.at[i]))
        copies[-2].start()
        copies[-1].start()
    for copy in copies:
        copy.wait()


def place(kernel, outs, chunks, index, vmem, scratch):
    parts = len(chunks)
    there = pl.BlockSpec(memory_space=pl.ANY)
    return pl.pallas_call(
        functools.partial(kernel, parts),
        out_shape=outs,
        in_specs=[pl.BlockSpec(memory_space=pltpu.SMEM)] + [pl.BlockSpec(memory_space=pltpu.VMEM)] * parts,
        out_specs=jax.tree.map(lambda _: there, outs),
        scratch_shapes=scratch,
        compiler_params=pltpu.CompilerParams(vmem_limit_bytes=vmem * MIB),
        cost_estimate=pl.CostEstimate(flops=1024, bytes_accessed=1024, transcendentals=0),
    )(index, *chunks)


def place_rows(chunks, index):
    parts = len(chunks)
    rows, columns = chunks[0].shape
    scratch = [pltpu.VMEM((parts, rows, columns), F32), pltpu.SemaphoreType.DMA((parts,))]
    return place(place_kernel, shape((parts * rows, columns), F32), chunks, index, 8, scratch)


def place_mixed(chunks, index, model, share):
    parts = len(chunks)
    width = chunks[0].shape[1]
    tall = chunks[0].shape[0] - model // width * share
    outs = (shape((parts * tall, width), F32), shape((parts * share, model), F32))
    scratch = [
        pltpu.VMEM((parts, tall, width), F32),
        pltpu.VMEM((parts, share, model), F32),
        pltpu.SemaphoreType.DMA((parts,)),
        pltpu.SemaphoreType.DMA((parts,)),
    ]

    def kernel(count, *refs):
        place_mixed_kernel(count, model, *refs)

    return place(kernel, outs, chunks, index, 8, scratch)


def swap(values, bit, tensor):
    return lax.ppermute(values, "tensor", [(i, i ^ bit) for i in range(tensor)])


class Line:
    def __init__(self):
        self.last = None

    def run(self, body, *args):
        if self.last is not None:
            args, _ = lax.optimization_barrier((args, self.last))
        out = body(*args)
        self.last = jax.tree.leaves(out)[0]
        return out

    def land(self, values):
        return lax.optimization_barrier((values, self.last))[0]


class Ring:
    def __init__(self, line, dp, grad, forward):
        order = list(range(0, dp, 2)) + list(range(dp - 1, 0, -2))
        at = [0] * dp
        for index, device in enumerate(order):
            at[device] = index
        self.pairs = [(order[i], order[(i + 1) % dp]) for i in range(dp)]
        self.sign = 1
        if not forward:
            self.pairs = [(b, a) for a, b in self.pairs]
            self.sign = -1
        self.pos = jnp.asarray(np.array(at, np.int32))[lax.axis_index("dp")]
        self.line, self.dp, self.grad = line, dp, grad
        self.step = 0
        self.chunks, self.places = [], []
        self.send(line.run(lambda g: self.own(g, 0).astype(BF16), grad))

    def index(self, step):
        return lax.rem(self.pos + (self.sign * step) % self.dp, self.dp)

    def own(self, grad, step):
        return lax.dynamic_index_in_dim(grad, self.index(step), 0, keepdims=False)

    def send(self, moving):
        self.flying = lax.ppermute(moving, "dp", self.pairs)

    def keep(self, chunk, step):
        self.chunks.append(chunk)
        self.places.append(self.index(step))

    def tick(self):
        dp = self.dp
        if self.step >= 2 * (dp - 1):
            return False
        self.step += 1
        if self.step < dp:
            moving = self.line.run(
                lambda f, g: (f.astype(F32) + self.own(g, -self.step)).astype(BF16), self.flying, self.grad
            )
            self.send(moving)
            if self.step == dp - 1:
                self.keep(moving, 1)
        else:
            step = self.step - (dp - 1)
            moving = self.line.land(self.flying)
            if step < dp - 1:
                self.send(moving)
            self.keep(moving, 1 - step)
            self.line.last = moving
        return True

    def done(self):
        return self.step >= 2 * (self.dp - 1)


def on_device(
    dp,
    tensor,
    tokens,
    qkv_weight,
    qv_bias,
    out_weight,
    out_bias,
    norm1_gain,
    norm1_bias,
    up_weight,
    up_bias,
    down_weight,
    down_bias,
    norm2_gain,
    norm2_bias,
    cotangent,
):
    core = functools.partial(swap, bit=1, tensor=tensor)
    chip = functools.partial(swap, bit=2, tensor=tensor)
    rows, model = tokens.shape
    width = qkv_weight.shape[2]
    hidden = up_weight.shape[1]
    line = Line()
    run, land = line.run, line.land

    def row(values):
        return values.reshape(1, -1)

    out_bias, down_bias = row(out_bias), row(down_bias)
    gain1, shift1, gain2, shift2 = (row(v) for v in (norm1_gain, norm1_bias, norm2_gain, norm2_bias))
    tok_a = tokens
    tok_c = chip(tok_a)
    tok_b = core(tok_a)
    out_peer = core(out_weight)
    q_ab, k_ab, v_ab, mix_a, mix_b = run(attend, tok_a, tok_b, qkv_weight, qv_bias)
    mix_b_peer = core(mix_b)
    up_peer = core(land(up_weight))
    down_peer = core(land(down_weight))
    up_bias_peer = core(land(up_bias))
    up_bias, up_bias_peer = row(up_bias), row(up_bias_peer)
    low_a = run(mix_out, mix_a, mix_b_peer, out_weight, out_peer)
    far_c = chip(low_a)
    tok_c = land(tok_c)
    tok_d = core(tok_c)
    q_cd, k_cd, v_cd, mix_c, mix_d = run(attend, tok_c, tok_d, qkv_weight, qv_bias)
    low_c = run(mix_out, mix_c, core(mix_d), out_weight, out_peer)
    far_a = chip(low_c)
    qkv_peer = core(land(qkv_weight))
    weights = (up_weight, up_peer, down_weight, down_peer)
    nrm_c, act_c, act_peer_c, slope_c, slope_peer_c, feed_c = run(
        functools.partial(feed, False), tok_c, low_c, far_c, out_bias, gain1, shift1, up_bias, up_bias_peer, weights
    )
    far_feed = chip(feed_c)
    act_d, nrm_d = core(land(act_peer_c)), core(land(nrm_c))
    wide_a, nrm_a, act_a, act_peer_a, slope_a, slope_peer_a, feed_a = run(
        functools.partial(feed, True), tok_a, low_a, far_a, out_bias, gain1, shift1, up_bias, up_bias_peer, weights
    )
    act_b, nrm_b = core(land(act_peer_a)), core(land(nrm_a))
    layer_out, grad_second, gs_a, sums2 = run(
        second_norm, wide_a, feed_a, far_feed, down_bias, gain2, shift2, cotangent
    )
    gs_c = chip(gs_a)
    gs_b = core(gs_a)
    gp_a, gp_peer_a, back_a = run(
        functools.partial(feed_back, kind=F32), gs_a, slope_a, slope_peer_a, weights
    )
    gp_b = core(gp_peer_a)
    gs_c = land(gs_c)
    gs_d = core(gs_c)
    gp_c, gp_peer_c, back_c = run(
        functools.partial(feed_back, kind=BF16), gs_c, slope_c, slope_peer_c, weights
    )
    far_back = chip(back_c)
    gp_d = core(gp_peer_c)
    ring = dp == RING
    (grad_down,) = run(weight_grad, (act_a, act_b, act_c, act_d), (gs_a, gs_b, gs_c, gs_d))
    if ring:
        ring_down = Ring(line, dp, grad_down.reshape(dp, -1, model), True)
    grad_up, up_sum = run(
        functools.partial(weight_grad, sums=True), (nrm_a, nrm_b, nrm_c, nrm_d), (gp_a, gp_b, gp_c, gp_d)
    )
    rings = []
    if ring:
        ring_up = Ring(line, dp, grad_up.reshape(dp, -1, hidden), False)
        rings = [ring_down, ring_up]

    def tick():
        return any([item.tick() for item in rings])

    tick()
    far_back = land(far_back)
    grad_first, gf_a, gh_a, gh_peer_a, sums1 = run(
        first_back, tok_a, low_a, far_a, out_bias, gain1, grad_second, back_a, far_back, out_weight, out_peer
    )
    gf_c = chip(gf_a)
    gh_b = core(gh_peer_a)
    gf_b = core(gf_a)
    tick()
    gr_ab = run(attend_back, q_ab, k_ab, v_ab, gh_a, land(gh_b))
    far_ab = core(gr_ab[:, rows:])
    tick()
    rows_a = run(
        functools.partial(proj_back, kind=F32), gr_ab[:, :rows], land(far_ab), qkv_weight, qkv_peer
    )
    gf_c = land(gf_c)
    gf_d = core(gf_c)
    gh_c, gh_peer_c = run(heads_back, gf_c, out_weight, out_peer)
    gh_d = core(gh_peer_c)
    tick()
    gr_cd = run(attend_back, q_cd, k_cd, v_cd, gh_c, land(gh_d))
    far_cd = core(gr_cd[:, rows:])
    tick()
    chunks = 2 * dp if ring else 2 * RING
    grad_mixed, qv_sum = run(
        functools.partial(ring_grad, chunks=chunks),
        (tok_a, tok_b, tok_c, tok_d),
        gr_ab,
        gr_cd,
        (mix_a, mix_b, mix_c, mix_d),
        (gf_a, gf_b, gf_c, gf_d),
    )
    share = width // chunks
    if ring:
        mixed = [Ring(line, dp, grad_mixed[:dp], True), Ring(line, dp, grad_mixed[dp:], False)]
        rings.extend(mixed)
    rows_c = run(functools.partial(proj_back, kind=BF16), gr_cd[:, :rows], land(far_cd), qkv_weight, qkv_peer)
    far_rows = chip(rows_c)
    tick()
    tick()
    token_grad = run(lambda a, b, c: a + b + c.astype(F32), grad_first, rows_a, land(far_rows))
    small = jnp.concatenate([sums1[:3], sums2[:3]], 0)
    flat = jnp.concatenate([up_sum[0], qv_sum[0]])

    bits = [("tensor", tensor, 1), ("tensor", tensor, 2)]
    bit = 1
    while bit < dp:
        bits.append(("dp", dp, bit))
        bit *= 2
    for axis, size, bit in bits:
        if axis == "dp" and bit == 1:
            flat = jnp.concatenate([small.reshape(-1), flat]).reshape(-1, 128)
        values = small if axis == "tensor" else flat
        flying = lax.ppermute(values, axis, [(i, i ^ bit) for i in range(size)])
        tick()
        values = run(lambda a, b: a + b, values, flying)
        if axis == "tensor":
            small = values
        else:
            flat = values
    flat = flat.reshape(-1)
    small = flat[: 6 * model].reshape(6, model)
    grad_up_bias = flat[6 * model : 6 * model + hidden]
    grad_qv = flat[6 * model + hidden :].reshape(2, -1)
    if ring:
        while not (ring_down.done() and ring_up.done()):
            tick()

        def placed(item):
            return run(lambda chunks, index: place_rows(chunks, index), item.chunks, jnp.stack(item.places))

        grad_down = placed(ring_down).reshape(grad_down.shape)
        tick()
        grad_up = placed(ring_up).reshape(grad_up.shape)
        while tick():
            pass
        index = jnp.stack(mixed[0].places + [dp + at for at in mixed[1].places])
        grad_qkv, grad_out = run(
            lambda chunks, index: place_mixed(chunks, index, model, share), mixed[0].chunks + mixed[1].chunks, index
        )
    else:
        grad_down, grad_up, grad_mixed = lax.psum((grad_down, grad_up, grad_mixed), "dp")
        grad_qkv, grad_out = place_mixed(list(grad_mixed), jnp.arange(chunks, dtype=jnp.int32), model, share)
    grad_qkv = grad_qkv.reshape(qkv_weight.shape)
    grad_out = grad_out.reshape(out_weight.shape)
    return (
        layer_out,
        token_grad,
        grad_qkv,
        grad_qv,
        grad_out,
        small[2],
        small[0],
        small[1],
        grad_up,
        grad_up_bias,
        grad_down,
        small[5],
        small[3],
        small[4],
    )


def solution(mesh):
    dp, tensor = mesh.shape["dp"], mesh.shape["tensor"]
    rows = P(("dp", "tensor"), None)
    placed = (
        rows,
        P(None, None, "tensor"),
        P(None, "tensor"),
        P("tensor", None),
        P(),
        P(),
        P(),
        P(None, "tensor"),
        P("tensor"),
        P("tensor", None),
        P(),
        P(),
        P(),
        rows,
    )
    given = (rows, rows) + placed[1:13]
    return jax.shard_map(
        functools.partial(on_device, dp, tensor),
        mesh=mesh,
        in_specs=placed,
        out_specs=given,
        check_vma=False,
    )
```

```python
import functools

import jax
import jax.numpy as jnp
import numpy as np
from jax import lax
from jax.experimental import pallas as pl
from jax.experimental.pallas import tpu as pltpu
from jax.sharding import PartitionSpec as P

HEAD_SIZE = 64
LENGTH = 512
EPSILON = 1e-05
BF16 = jnp.bfloat16
F32 = jnp.float32
RING = 8
MIB = 2**20


def dot(a, b):
    return jnp.dot(a, b, preferred_element_type=F32)


def dot_t(a, b):
    return lax.dot_general(a, b, (((1,), (1,)), ((), ())), preferred_element_type=F32)


def dot_l(a, b):
    return lax.dot_general(a, b, (((0,), (0,)), ((), ())), preferred_element_type=F32)


class Given:
    def __init__(self, ref, copy=None):
        self.ref, self.copy = ref, copy

    def __call__(self):
        if self.copy is not None:
            self.copy.wait()
            self.copy = None
        return self.ref


class Result:
    def __init__(self, ref, copy=None):
        self.ref, self.copy, self.sent = ref, copy, False

    def send(self):
        if self.copy is not None and not self.sent:
            self.copy.start()
            self.sent = True

    def finish(self):
        self.send()
        if self.copy is not None:
            self.copy.wait()


VM = (6, 6, 8, 8, 8, 8, 8, 4)
HERE, THERE = "vmem", "hbm"


COSTS = {
    "attend": 18.4,
    "attend_back": 0.88,
    "mix_out": 2.4,
    "feed": 0.8,
    "second_grad": 1.0,
    "second_rest": 8.0,
    "feed_back": 22.0,
    "weight_grad": 0.64,
    "first_back": 0.4,
    "heads_back": 0.6,
    "proj_back": 0.384,
    "mixed_grad": 0.48,
    "token_sum": 0.4,
    "add": 4.0,
    "place": 0.16,
    "ring": 2.8,
}


def cost(us):
    return pl.CostEstimate(flops=int(us * 1e9), bytes_accessed=1024, transcendentals=0)


def keep(array):
    return pltpu.with_memory_space_constraint(array, pltpu.HBM)


def call(body, args, outs, vmem, us, scratch=(), index=None, aliases=None):
    spaces = {HERE: pltpu.VMEM, THERE: pltpu.HBM}
    far_in = [i for i, (_, place) in enumerate(args) if place == THERE]
    far_out = [i for i, (_, _, place) in enumerate(outs) if place == THERE]
    scalars = [] if index is None else [index]

    def kernel(*refs):
        scalar, refs = refs[: len(scalars)], refs[len(scalars) :]
        given, refs = list(refs[: len(args)]), refs[len(args) :]
        result, refs = list(refs[: len(outs)]), refs[len(outs) :]
        slots_in, refs = refs[: len(far_in)], refs[len(far_in) :]
        slots_out, refs = refs[: len(far_out)], refs[len(far_out) :]
        if far_in:
            done_in, refs = refs[0], refs[1:]
        if far_out:
            done_out, refs = refs[0], refs[1:]
        given = [Given(ref) for ref in given]
        for slot, i in enumerate(far_in):
            copy = pltpu.make_async_copy(given[i].ref, slots_in[slot], done_in.at[slot])
            copy.start()
            given[i] = Given(slots_in[slot], copy)
        result = [Result(ref) for ref in result]
        for slot, i in enumerate(far_out):
            copy = pltpu.make_async_copy(slots_out[slot], result[i].ref, done_out.at[slot])
            result[i] = Result(slots_out[slot], copy)
        body(given, result, *scalar, *refs)
        for item in given:
            item()
        for item in result:
            item.send()
        for item in result:
            item.finish()

    room = [pltpu.VMEM(args[i][0].shape, args[i][0].dtype) for i in far_in]
    room += [pltpu.VMEM(outs[i][0], outs[i][1]) for i in far_out]
    room += [pltpu.SemaphoreType.DMA((len(far),)) for far in (far_in, far_out) if far]
    return pl.pallas_call(
        kernel,
        out_shape=tuple(
            (pltpu.HBM if place == THERE else jax.ShapeDtypeStruct)(dims, kind) for dims, kind, place in outs
        ),
        in_specs=[pl.BlockSpec(memory_space=pltpu.SMEM)] * len(scalars)
        + [pl.BlockSpec(memory_space=spaces[place]) for _, place in args],
        out_specs=tuple(pl.BlockSpec(memory_space=spaces[place]) for _, _, place in outs),
        scratch_shapes=room + list(scratch),
        input_output_aliases={len(scalars) + i: o for i, o in (aliases or {}).items()},
        compiler_params=pltpu.CompilerParams(vmem_limit_bytes=vmem * MIB),
        cost_estimate=cost(us),
    )(*scalars, *(keep(array) if place == THERE else array for array, place in args))


def attend_kernel(given, result):
    first, second, weight, bias = given
    query, key, value, mixed_first, mixed_second = result
    bias_wide = bias()[...].astype(F32)
    rows = first.ref.shape[0]
    width = query.ref.shape[1]
    weight = weight()
    for half, part in enumerate((first, second)):
        block = pl.ds(half * rows, rows)
        part = part()[...]
        query.ref[block, :] = ((dot(part, weight[0]) + bias_wide[0:1, :]) * 0.125).astype(BF16)
        key.ref[block, :] = dot(part, weight[1]).astype(BF16)
        value.ref[block, :] = (dot(part, weight[2]) + bias_wide[1:2, :]).astype(BF16)
    for item in (query, key, value):
        item.send()
    low_half = lax.broadcasted_iota(jnp.int32, (rows, 128), 1) < HEAD_SIZE
    for half, mixed in enumerate((mixed_second, mixed_first)):
        block = pl.ds((1 - half) * rows, rows)
        for pair in range(width // 128):
            cols = pl.ds(pair * 128, 128)
            q_pair = query.ref[block, cols]
            k_pair = key.ref[:, cols]
            v_pair = value.ref[:, cols]
            outs = []
            for side in range(2):
                keep = low_half if side == 0 else ~low_half
                scores = dot_t(jnp.where(keep, q_pair, jnp.zeros_like(q_pair)), k_pair)
                weights = jnp.exp(scores - jnp.max(scores, -1, keepdims=True))
                total = jnp.sum(weights, -1, keepdims=True)
                probs = (weights * (1.0 / total)).astype(BF16)
                outs.append(dot(probs, v_pair))
            mixed.ref[:, cols] = jnp.where(low_half, outs[0], outs[1]).astype(BF16)


def attend(first, second, weight, bias):
    rows, width = first.shape[0], weight.shape[2]
    args = [(v, HERE) for v in (first, second, weight, bias)]
    outs = [((2 * rows, width), BF16, THERE)] * 3 + [((rows, width), BF16, HERE)] * 2
    return call(attend_kernel, args, outs, VM[0], COSTS["attend"])


def attend_back_kernel(given, result, key_sum, value_sum):
    query, key, value, grad_first, grad_second = given
    query, key, value = query(), key(), value()
    near, far = (item.ref for item in result)
    rows = near.shape[1]
    width = near.shape[2]
    low_half = lax.broadcasted_iota(jnp.int32, (rows, 128), 1) < HEAD_SIZE
    low_all = lax.broadcasted_iota(jnp.int32, (2 * rows, 128), 1) < HEAD_SIZE
    for pair in range(width // 128):
        cols = pl.ds(pair * 128, 128)
        k_pair = key[:, cols]
        v_pair = value[:, cols]
        for half, (grads, out) in enumerate(((grad_first(), near), (grad_second(), far))):
            q_pair = query[pl.ds(half * rows, rows), cols]
            g_pair = grads[:, cols]
            dq, dk, dv = [], [], []
            for side in range(2):
                keep = low_half if side == 0 else ~low_half
                scores = dot_t(jnp.where(keep, q_pair, jnp.zeros_like(q_pair)), k_pair)
                weights = jnp.exp(scores - jnp.max(scores, -1, keepdims=True))
                total = jnp.sum(weights, -1, keepdims=True)
                probs = weights * (1.0 / total)
                grad_probs = dot_t(jnp.where(keep, g_pair, jnp.zeros_like(g_pair)), v_pair)
                inner = probs * grad_probs
                grad_scores = (inner - probs * jnp.sum(inner, -1, keepdims=True)).astype(BF16)
                dv.append(dot_l(probs.astype(BF16), g_pair))
                dq.append(dot(grad_scores, k_pair))
                dk.append(dot_l(grad_scores, q_pair))
            out[0, :, cols] = (jnp.where(low_half, dq[0], dq[1]).astype(BF16).astype(F32) * 0.125).astype(BF16)
            dk_pair = jnp.where(low_all, dk[0], dk[1])
            dv_pair = jnp.where(low_all, dv[0], dv[1])
            if half == 0:
                key_sum[...] = dk_pair
                value_sum[...] = dv_pair
        for i, (part, last) in enumerate(((key_sum, dk_pair), (value_sum, dv_pair))):
            total = (part[...] + last).astype(BF16)
            near[1 + i, :, cols] = total[:rows]
            far[1 + i, :, cols] = total[rows:]


def attend_back(query, key, value, grad_first, grad_second):
    length, width = query.shape
    args = [(query, THERE), (key, THERE), (value, THERE), (grad_first, HERE), (grad_second, HERE)]
    outs = [((3, length // 2, width), BF16, HERE)] * 2
    return call(attend_back_kernel, args, outs, VM[1], COSTS["attend_back"], [pltpu.VMEM((length, 128), F32), pltpu.VMEM((length, 128), F32)])


def mix_out_kernel(given, result):
    mix, mix_peer, weight, weight_peer = given
    out = dot(mix()[...], weight()[...]) + dot(mix_peer()[...], weight_peer()[...])
    result[0].ref[...] = out
    result[1].ref[...] = out.astype(BF16)


def mix_out(mix, mix_peer, weight, weight_peer):
    args = [(mix, HERE), (mix_peer, HERE), (weight, HERE), (weight_peer, HERE)]
    dims = (mix.shape[0], weight.shape[1])
    return call(mix_out_kernel, args, [(dims, F32, HERE), (dims, BF16, HERE)], 4, COSTS["mix_out"])


def center_scale(values):
    center = values - jnp.mean(values, -1, keepdims=True)
    spread = jnp.mean(center * center, -1, keepdims=True)
    scale = lax.rsqrt(spread + EPSILON)
    return center * scale, scale


def norm_back(grad, unit, scale, gain):
    grad_unit = grad * gain
    return scale * (
        grad_unit
        - jnp.mean(grad_unit, -1, keepdims=True)
        - unit * jnp.mean(grad_unit * unit, -1, keepdims=True)
    )


def gate(pre):
    cdf = 0.5 * (1.0 + lax.erf(pre * np.float32(np.sqrt(0.5))))
    density = np.float32(1 / np.sqrt(2 * np.pi)) * jnp.exp(-0.5 * pre * pre)
    return pre * cdf, cdf + pre * density


def feed_kernel(own, given, result):
    tok, low, far, out_bias, gain, shift, bias, bias_peer = (item()[...].astype(F32) for item in given[:8])
    weights = given[8:]
    if own:
        first, wide, result = result[0], result[1], result[2:]
    normed, act, act_peer, slope, slope_peer, out = result
    first_sum = tok + low + far + out_bias
    unit, _ = center_scale(first_sum)
    value = unit * gain + shift
    if own:
        first.ref[...] = first_sum
        first.send()
        wide.ref[...] = value
    normed.ref[...] = value.astype(BF16)
    normed.send()
    step = 256
    for weight, bias_of, act_of, slope_of in ((weights[0], bias, act, slope), (weights[1], bias_peer, act_peer, slope_peer)):
        for start in range(0, act_of.ref.shape[1], step):
            cols = pl.ds(start, step)
            pre = dot(normed.ref[...], weight()[:, cols]) + bias_of[:, start : start + step]
            act_of.ref[:, cols], slope_of.ref[:, cols] = (
                part.astype(kind) for part, kind in zip(gate(pre), (BF16, F32))
            )
        act_of.send()
        slope_of.send()
    total = dot(act.ref[...], weights[2]()[...]) + dot(act_peer.ref[...], weights[3]()[...])
    out.ref[...] = total.astype(out.ref.dtype)


def feed(own, tok, low, far, out_bias, gain, shift, bias, bias_peer, weights):
    rows, model = tok.shape
    hidden = weights[0].shape[1]
    outs = [((rows, model), F32, THERE), ((rows, model), F32, HERE)] if own else []
    outs += [((rows, model), BF16, HERE), ((rows, hidden), BF16, THERE), ((rows, hidden), BF16, HERE)]
    outs += [((rows, hidden), F32, THERE)] * 2
    outs.append(((rows, model), F32 if own else BF16, HERE))
    args = [(v, HERE) for v in (tok, low, far, out_bias, gain, shift, bias, bias_peer, *weights)]
    return call(functools.partial(feed_kernel, own), args, outs, VM[2], COSTS["feed"])


def second_parts(given):
    wide, feed_sum, far, down_bias, gain, shift, cot = (item()[...].astype(F32) for item in given)
    unit, scale = center_scale(wide + feed_sum + far + down_bias)
    return unit, scale, gain, shift, cot


def second_grad_kernel(given, result):
    unit, scale, gain, _, cot = second_parts(given)
    result[0].ref[...] = norm_back(cot, unit, scale, gain).astype(BF16)


def second_rest_kernel(given, result):
    unit, scale, gain, shift, cot = second_parts(given)
    layer_out, grad, sums = result
    layer_out.ref[...] = (unit * gain + shift).astype(BF16)
    layer_out.send()
    grad_second = norm_back(cot, unit, scale, gain)
    grad.ref[...] = grad_second
    grad.send()
    sums.ref[...] = jnp.zeros_like(sums.ref)
    sums.ref[3:4, :] = jnp.sum(cot * unit, 0, keepdims=True)
    sums.ref[4:5, :] = jnp.sum(cot, 0, keepdims=True)
    sums.ref[5:6, :] = jnp.sum(grad_second, 0, keepdims=True)


def second_grad(*values):
    return call(second_grad_kernel, [(v, HERE) for v in values], [(values[0].shape, BF16, HERE)], 6, COSTS["second_grad"])[0]


def second_rest(*values):
    dims = values[0].shape
    outs = [(dims, BF16, THERE), (dims, F32, THERE), ((8, dims[1]), F32, HERE)]
    return call(second_rest_kernel, [(v, HERE) for v in values], outs, 8, COSTS["second_rest"])


def feed_back_kernel(given, result):
    grad, slope, slope_peer, up, up_peer, down, down_peer, *more = given
    pre, pre_peer, out = result
    step = 256
    for slope_of, pre_of, weight in ((slope, pre, down), (slope_peer, pre_peer, down_peer)):
        for first in range(0, pre.ref.shape[1], step):
            cols = pl.ds(first, step)
            grad_act = dot_t(grad()[...], weight()[cols, :])
            pre_of.ref[:, cols] = (slope_of()[:, cols] * grad_act).astype(BF16)
        pre_of.send()
    total = dot_t(pre.ref[...], up()[...]) + dot_t(pre_peer.ref[...], up_peer()[...])
    for part in more:
        total += part()[...]
    out.ref[...] = total.astype(out.ref.dtype)


def feed_back(grad, slope, slope_peer, weights, wide=None):
    own = wide is not None
    rows, model = grad.shape
    hidden = slope.shape[1]
    outs = [((rows, hidden), BF16, THERE), ((rows, hidden), BF16, HERE)]
    outs.append(((rows, model), F32, THERE) if own else ((rows, model), BF16, HERE))
    args = [(grad, HERE), (slope, THERE), (slope_peer, THERE)] + [(v, HERE) for v in weights] + [(wide, THERE)] * own
    return call(feed_back_kernel, args, outs, VM[3], COSTS["feed_back"])


def summed(left, right):
    total = dot_l(left[0], right[0])
    for a, b in zip(left[1:], right[1:]):
        total += dot_l(a, b)
    return total


def weight_grad_kernel(second, given, result, index):
    if second:
        given = given[1:]
    parts = len(given) // 2
    left, right = given[:parts], given[parts:]
    out, moving = result[0].ref, result[-1].ref
    chunks = out.shape[0]
    rows = pl.ds(second * moving.shape[0], moving.shape[0])
    step = 256
    for first in range(0, out.shape[2], step):
        cols = pl.ds(first, step)
        block = summed([part()[...] for part in left], [part()[:, cols] for part in right])
        out[:, rows, cols] = block.reshape(chunks, moving.shape[0], step)
    if second:
        ones = jnp.ones((left[0].ref.shape[0], 8), BF16)
        result[1].ref[...] = summed([ones] * parts, [part()[...] for part in right])
    moving[...] = out[index[chunks // 2], rows].astype(BF16)


def weight_grad(left, right, index, vmem, grads=None):
    wide, tall = right[0][0].shape[1], left[0][0].shape[1] // RING
    second = grads is not None
    outs = [((RING, 2 * tall, wide), F32, HERE)] + [((8, wide), F32, HERE)] * second + [((tall, wide), BF16, HERE)]
    args = [(grads, HERE)] * second + [*left, *right]
    body = functools.partial(weight_grad_kernel, int(second))
    return call(body, args, outs, vmem, COSTS["weight_grad"], index=index, aliases={0: 0} if second else None)


def first_back_kernel(given, result):
    first, gain, near, far_back, weight, weight_peer, sums_second = given
    grad, grad_low, sent, heads, sums = result
    unit, scale = center_scale(first()[...])
    grad_normed = near()[...] + far_back()[...].astype(F32)
    grad_first = norm_back(grad_normed, unit, scale, gain()[...].astype(F32))
    grad.ref[...] = grad_first
    grad.send()
    low = grad_first.astype(BF16)
    grad_low.ref[...] = low
    width = heads.ref.shape[1]
    sent.ref[:, width:] = low
    heads.ref[...] = dot_t(low, weight()[...]).astype(BF16)
    sent.ref[:, :width] = dot_t(low, weight_peer()[...]).astype(BF16)
    sums.ref[...] = sums_second()[...]
    sums.ref[0:1, :] = jnp.sum(grad_normed * unit, 0, keepdims=True)
    sums.ref[1:2, :] = jnp.sum(grad_normed, 0, keepdims=True)
    sums.ref[2:3, :] = jnp.sum(grad_first, 0, keepdims=True)


def first_back(first, gain, near, far_back, weight, weight_peer, sums):
    dims, width = first.shape, weight.shape[0]
    args = [(first, THERE), (gain, HERE), (near, THERE)]
    args += [(v, HERE) for v in (far_back, weight, weight_peer, sums)]
    outs = [(dims, F32, THERE), (dims, BF16, HERE)]
    outs += [((dims[0], width + dims[1]), BF16, HERE), ((dims[0], width), BF16, HERE), (sums.shape, F32, HERE)]
    return call(first_back_kernel, args, outs, VM[5], COSTS["first_back"])


def heads_back_kernel(given, result):
    grad, weight, weight_peer = given
    sent, heads = (item.ref for item in result)
    low = grad()[...]
    width = heads.shape[1]
    sent[:, width:] = low
    heads[...] = dot_t(low, weight()[...]).astype(BF16)
    sent[:, :width] = dot_t(low, weight_peer()[...]).astype(BF16)


def heads_back(grad, weight, weight_peer):
    rows, model = grad.shape
    width = weight.shape[0]
    outs = [((rows, width + model), BF16, HERE), ((rows, width), BF16, HERE)]
    return call(heads_back_kernel, [(grad, HERE), (weight, HERE), (weight_peer, HERE)], outs, 4, COSTS["heads_back"])


def proj_back_kernel(given, result):
    near, far, weight, weight_peer = (item() for item in given)
    total = dot_t(near[0], weight[0]) + dot_t(far[0], weight_peer[0])
    for i in (1, 2):
        total += dot_t(near[i], weight[i]) + dot_t(far[i], weight_peer[i])
    result[0].ref[...] = total.astype(result[0].ref.dtype)


def proj_back(near, far, weight, weight_peer, kind, space):
    args = [(v, HERE) for v in (near, far, weight, weight_peer)]
    return call(proj_back_kernel, args, [((near.shape[1], weight.shape[1]), kind, space)], VM[7], COSTS["proj_back"])[0]


def mixed_grad_kernel(given, result, index, total):
    toks, nears, mixes, grads = given[:4], given[4:8], given[8:12], given[12:]
    out, bias, *moving = (item.ref for item in result)
    width = total.shape[1]
    model = total.shape[0] // 3
    chunks = out.shape[0]
    share = width // chunks
    tall = out.shape[1] - model // width * share
    mixed = [part()[...] for part in mixes]
    for j in range(model // width):
        block = summed(mixed, [part()[:, pl.ds(part.ref.shape[1] - model + j * width, width)] for part in grads])
        out[:, pl.ds(tall + j * share, share), :] = block.reshape(chunks, share, width)
    lefts = [part()[...] for part in toks]
    ones = [jnp.ones((lefts[0].shape[0], 8), BF16)] * 4
    for j in range(3):
        right = [part()[j] for part in nears]
        total[pl.ds(j * model, model), :] = summed(lefts, right)
        if j != 1:
            bias[:, pl.ds(j // 2 * width, width)] = summed(ones, right)
    for i in range(chunks):
        out[i, pl.ds(0, tall), :] = total[pl.ds(i * tall, tall), :]
    half = out.shape[1] // 2
    for i, part in enumerate(moving):
        part[...] = out[index[chunks // 2], pl.ds(i * half, half)].astype(BF16)


def mixed_grad(toks, nears, mixes, grads, index, vmem):
    model, width = toks[0].shape[1], mixes[0].shape[1]
    tall = 4 * model // RING
    outs = [((RING, tall, width), F32, HERE), ((8, 2 * width), F32, HERE)] + [((tall // 2, width), BF16, HERE)] * 2
    args = [(v, HERE) for v in (*toks, *nears, *mixes, *grads)]
    return call(mixed_grad_kernel, args, outs, vmem, COSTS["mixed_grad"], [pltpu.VMEM((3 * model, width), F32)], index)


def token_grad_kernel(given, result):
    grad, near, far = given
    result[0].ref[...] = grad()[...] + near()[...] + far()[...].astype(F32)


def token_sum(grad, near, far):
    args = [(grad, THERE), (near, THERE), (far, HERE)]
    return call(token_grad_kernel, args, [(grad.shape, F32, THERE)], 8, COSTS["token_sum"])[0]


def ring_step_kernel(places, given, result, index):
    grad = given[0].ref
    for side, (place, arrived, moving) in enumerate(zip(places, given[1:], result)):
        rows = arrived.ref.shape[0]
        first = side * (grad.shape[1] - rows)
        own = grad[index[place]]
        if rows < grad.shape[1]:
            moving.ref[...] = own.astype(BF16)
        block = pl.ds(first, rows)
        moving.ref[block, :] = (grad[index[place], block] + arrived()[...].astype(F32)).astype(BF16)


def ring_last_kernel(given, result, index):
    grad, ahead, behind = given
    total = grad.ref[index[0]] + ahead()[...].astype(F32) + behind()[...].astype(F32)
    result[0].ref[...] = total
    result[1].ref[...] = total.astype(BF16)


def ring_step(grad, arrived, index, places):
    args = [(v, HERE) for v in (grad, *arrived)]
    outs = [(grad.shape[1:], BF16, HERE)] * 2
    return call(functools.partial(ring_step_kernel, places), args, outs, 3, COSTS["ring"], index=index)


def ring_last(grad, arrived, index):
    args = [(v, HERE) for v in (grad, *arrived)]
    outs = [(grad.shape[1:], kind, HERE) for kind in (F32, BF16)]
    return call(ring_last_kernel, args, outs, 2, COSTS["ring"], index=index)


def place_kernel(bands, order, given, result, index, *scratch):
    wides, semaphores = scratch[:-1], scratch[-1]
    copies = []
    for i, place in enumerate(order):
        parts = given[i:] if i == len(order) - 1 else given[i : i + 1]
        chunk = jnp.concatenate([part()[...] for part in parts], 0).astype(F32)
        for j, ((first, rows, columns), wide, out) in enumerate(zip(bands, wides, result)):
            width = chunk.shape[1]
            for k in range(columns // width):
                wide[i, :, pl.ds(k * width, width)] = chunk[first + k * rows : first + (k + 1) * rows]
            target = pl.ds(pl.multiple_of(index[place] * rows, 8), rows)
            copies.append(pltpu.make_async_copy(wide.at[i], out.at[target], semaphores.at[i, j]))
            copies[-1].start()
    for copy in copies:
        copy.wait()


def place(chunks, held, index, bands, order):
    there = pl.BlockSpec(memory_space=pltpu.HBM)
    count, results, parts = len(chunks), len(bands), len(order)
    held = held or ()

    def kernel(index, *refs):
        given, refs = refs[:count], refs[count + len(held) :]
        place_kernel(bands, order, [Given(ref) for ref in given], refs[:results], index, *refs[results:])

    scratch = [pltpu.VMEM((parts, rows, columns), F32) for _, rows, columns in bands]
    return pl.pallas_call(
        kernel,
        out_shape=tuple(pltpu.HBM((RING * rows, columns), F32) for _, rows, columns in bands),
        in_specs=[pl.BlockSpec(memory_space=pltpu.SMEM)]
        + [pl.BlockSpec(memory_space=pltpu.VMEM)] * count
        + [there] * len(held),
        out_specs=tuple(there for _ in bands),
        scratch_shapes=scratch + [pltpu.SemaphoreType.DMA((parts, results))],
        input_output_aliases={1 + count + i: i for i in range(len(held))},
        compiler_params=pltpu.CompilerParams(vmem_limit_bytes=6 * MIB),
        cost_estimate=cost(COSTS["place"]),
    )(index, *chunks, *(keep(v) for v in held))


def add_kernel(given, result):
    total = given[0]()[...] + given[1]()[...]
    result[0].ref[...] = total


def add(a, b):
    return call(add_kernel, [(a, HERE), (b, HERE)], [(a.shape, a.dtype, HERE)], 2, COSTS["add"])[0]


def add_rows_kernel(given, result):
    a, b, hidden, wide = (item() for item in given)
    out = result[0].ref
    out[...] = a[...] + b[...]
    out[6:7, :] = hidden[0:1, :]
    out[7:8, : wide.shape[1]] = wide[0:1, :]


def add_rows(a, b, hidden, wide):
    return call(add_rows_kernel, [(v, HERE) for v in (a, b, hidden, wide)], [(a.shape, F32, HERE)], 2, COSTS["add"])[0]


def swap(values, bit, tensor):
    return lax.ppermute(values, "tensor", [(i, i ^ bit) for i in range(tensor)])


class Line:
    def __init__(self):
        self.last = None

    def run(self, body, *args):
        if self.last is not None:
            args, _ = lax.optimization_barrier((args, self.last))
        out = body(*args)
        self.last = jax.tree.leaves(out)[-1]
        return out

    def land(self, values):
        return lax.optimization_barrier((values, self.last))[0]

    def settle(self, *values):
        self.last = lax.optimization_barrier((values, self.last))[0]
        return self.last if len(values) > 1 else self.last[0]


def ring_order(dp):
    return list(range(0, dp, 2)) + list(range(dp - 1, 0, -2))


class Ring:
    def __init__(self, line, dp, index, bands):
        self.bands = bands
        order = ring_order(dp)
        self.ways = [[(order[i], order[(i + way) % dp]) for i in range(dp)] for way in (1, -1)]
        self.line, self.dp, self.index = line, dp, index
        self.step, self.half = 0, dp // 2
        self.flying, self.outs = [], None

    def send(self, *moving):
        for part in moving:
            self.flying.append(lax.ppermute(part, "dp", self.ways[len(self.flying)]))

    def tick(self):
        self.step += 1
        step, half, run = self.step, self.half, self.line.run
        arrived, self.flying = tuple(self.flying), []
        if step < half:
            places = (half - step, self.dp + step - half)
            self.send(*run(functools.partial(ring_step, places=places), self.grad, arrived, self.index))
        elif step == half:
            total, moving = run(ring_last, self.grad, arrived, self.index)
            self.send(moving, moving)
            self.put((total,), (0,))
        else:
            step -= half
            arrived = self.line.settle(*arrived)
            if step < half - 1:
                self.send(*arrived)
            elif step < half:
                rows = arrived[0].shape[0] // 2
                self.send(arrived[0][:rows], arrived[1][rows:])
            self.put(arrived, (self.dp - step, step) if step < half else (step,))

    def put(self, chunks, order):
        body = functools.partial(place, bands=self.bands, order=order)
        self.outs = self.line.run(body, chunks, self.outs, self.index)


def on_device(
    dp,
    tensor,
    tokens,
    qkv_weight,
    qv_bias,
    out_weight,
    out_bias,
    norm1_gain,
    norm1_bias,
    up_weight,
    up_bias,
    down_weight,
    down_bias,
    norm2_gain,
    norm2_bias,
    cotangent,
):
    core = functools.partial(swap, bit=1, tensor=tensor)
    chip = functools.partial(swap, bit=2, tensor=tensor)
    rows, model = tokens.shape
    width = qkv_weight.shape[2]
    hidden = up_weight.shape[1]
    ring = dp == RING
    room = 8 if ring else 48
    line = Line()
    run, land, settle = line.run, line.land, line.settle

    def row(values):
        return values.reshape(1, -1)

    index = jnp.arange(RING, dtype=jnp.int32)
    if ring:
        turns = np.zeros((dp, dp), np.int32)
        for at, device in enumerate(ring_order(dp)):
            turns[device] = (at + np.arange(dp)) % dp
        index = lax.dynamic_index_in_dim(jnp.asarray(turns), lax.axis_index("dp"), 0, keepdims=False)
    out_bias, down_bias = row(out_bias), row(down_bias)
    gain1, shift1, gain2, shift2 = (row(v) for v in (norm1_gain, norm1_bias, norm2_gain, norm2_bias))
    tok_a = tokens
    tok_c = chip(tok_a)
    tok_b = core(tok_a)
    out_peer, up_peer = core(out_weight), core(up_weight)
    q_ab, k_ab, v_ab, mix_a, mix_b = run(attend, tok_a, tok_b, qkv_weight, qv_bias)
    mix_b_peer = core(mix_b)
    out_peer, up_peer = settle(out_peer, up_peer)
    part_a, low_a = run(mix_out, mix_a, mix_b_peer, out_weight, out_peer)
    far_c = chip(low_a)
    down_peer = core(land(down_weight))
    tok_c = settle(tok_c)
    tok_d = core(tok_c)
    q_cd, k_cd, v_cd, mix_c, mix_d = run(attend, tok_c, tok_d, qkv_weight, qv_bias)
    part_c, low_c = run(mix_out, mix_c, core(mix_d), out_weight, out_peer)
    far_a = chip(low_c)
    up_bias_peer, down_peer = settle(core(land(up_bias)), down_peer)
    up_bias, up_bias_peer = row(up_bias), row(up_bias_peer)
    weights = (up_weight, up_peer, down_weight, down_peer)
    nrm_c, act_c, act_peer_c, slope_c, slope_peer_c, feed_c = run(
        functools.partial(feed, False), tok_c, part_c, far_c, out_bias, gain1, shift1, up_bias, up_bias_peer, weights
    )
    far_feed = chip(feed_c)
    act_d, nrm_d = core(act_peer_c), core(nrm_c)
    first_a, wide_a, nrm_a, act_a, act_peer_a, slope_a, slope_peer_a, feed_a = run(
        functools.partial(feed, True), tok_a, part_a, far_a, out_bias, gain1, shift1, up_bias, up_bias_peer, weights
    )
    act_d, nrm_d = settle(act_d, nrm_d)
    act_b, nrm_b = core(act_peer_a), core(nrm_a)
    second = (wide_a, feed_a, land(far_feed), down_bias, gain2, shift2, cotangent)
    gs_a = run(second_grad, *second)
    gs_c = chip(gs_a)
    layer_out, grad_second, sums = run(second_rest, *second)
    act_b, nrm_b = settle(act_b, nrm_b)
    qkv_peer = core(land(qkv_weight))
    gs_b = core(gs_a)
    gp_a, gp_peer_a, back_a = run(
        feed_back, gs_a, slope_a, slope_peer_a, weights, grad_second
    )
    gs_b, qkv_peer = settle(gs_b, qkv_peer)
    gp_b = core(gp_peer_a)
    gs_c = settle(gs_c)
    gs_d = core(gs_c)
    gp_c, gp_peer_c, back_c = run(
        feed_back, gs_c, slope_c, slope_peer_c, weights
    )
    far_back = chip(back_c)
    gp_d = core(gp_peer_c)

    def feed_grads(left_here, left_there, right_here, right_there, index, grads=None):
        left = [(v, HERE) for v in left_here] + [(v, THERE) for v in left_there]
        right = [(v, HERE) for v in right_here] + [(v, THERE) for v in right_there]
        return weight_grad(left, right, index, room, grads)

    half, tall, share = model // RING, 3 * model // RING, width // RING
    ring_feed, ring_mixed = (
        Ring(line, dp, index, bands) if ring else None
        for bands in (((0, half, model), (half, half, hidden)), ((0, tall, width), (tall, share, model)))
    )

    def tick(*items):
        for item in items:
            if ring:
                item.tick()

    def send(item, *moving):
        if ring:
            item.send(*moving)

    grads, moving = run(feed_grads, (act_b, act_d), (act_a, act_c), (gs_b, gs_d, gs_a, gs_c), (), index)
    send(ring_feed, moving)
    grads, up_sum, moving = run(
        feed_grads, (nrm_b, nrm_d, nrm_a, nrm_c), (), (gp_b, gp_d), (gp_a, gp_c), index, grads
    )
    send(ring_feed, moving)
    if ring:
        ring_feed.grad = grads
    far_back = settle(far_back)
    grad_first, gf_a, sent_a, gh_a, sums = run(
        first_back, first_a, gain1, back_a, far_back, out_weight, out_peer, sums
    )
    gf_c = chip(gf_a)
    back_b = core(sent_a)
    tick(ring_feed)
    back_b = settle(back_b)
    flying = core(sums)
    gr_a, gr_b = run(attend_back, q_ab, k_ab, v_ab, gh_a, back_b)
    far_gr_b = core(gr_b)
    tick(ring_feed)
    far_gr_b, flying = settle(far_gr_b, flying)
    sums = run(add, sums, flying)
    rows_a = run(functools.partial(proj_back, kind=F32, space=THERE), gr_a, far_gr_b, qkv_weight, qkv_peer)
    gf_c = settle(gf_c)
    flying = chip(sums)
    sent_c, gh_c = run(heads_back, gf_c, out_weight, out_peer)
    back_d = core(sent_c)
    tick(ring_feed)
    back_d = settle(back_d)
    gr_c, gr_d = run(attend_back, q_cd, k_cd, v_cd, gh_c, back_d)
    far_gr_d = core(gr_d)
    flying = settle(flying)
    grad_mixed, qv_sum, *moving = run(
        functools.partial(mixed_grad, vmem=room),
        (tok_a, tok_b, tok_c, tok_d),
        (gr_a, gr_b, gr_c, gr_d),
        (mix_a, mix_b, mix_c, mix_d),
        (gf_a, back_b, gf_c, back_d),
        index,
    )
    send(ring_mixed, *moving)
    if ring:
        ring_mixed.grad = grad_mixed
    sums = run(add_rows, sums, flying, up_sum, qv_sum)
    tick(ring_feed)
    far_gr_d = settle(far_gr_d)
    rows_c = run(functools.partial(proj_back, kind=BF16, space=HERE), gr_c, far_gr_d, qkv_weight, qkv_peer)
    far_rows = chip(rows_c)
    tick(ring_mixed, ring_mixed, ring_feed)
    token_grad = run(token_sum, grad_first, rows_a, land(far_rows))
    turns = [(ring_mixed, ring_mixed), (ring_feed, ring_mixed), (ring_mixed, ring_feed)]
    for place_at in range(dp.bit_length() - 1):
        flying = lax.ppermute(sums, "dp", [(i, i ^ (1 << place_at)) for i in range(dp)])
        tick(*(turns[place_at] if place_at < len(turns) else ()))
        sums = run(add, sums, flying)
    if ring:
        tick(ring_mixed, ring_feed, ring_mixed)
        (grad_down, grad_up), (grad_qkv, grad_out) = ring_feed.outs, ring_mixed.outs
    else:
        grads, grad_mixed = lax.psum((grads, grad_mixed), "dp")
        grad_down, grad_up = grads[:, :half], grads[:, half:]
        grad_qkv = grad_mixed[:, :tall]
        grad_out = grad_mixed[:, tall:].reshape(RING, model // width, share, width).swapaxes(1, 2)
    return (
        layer_out,
        token_grad,
        grad_qkv.reshape(qkv_weight.shape),
        sums[7, : 2 * width].reshape(2, width),
        grad_out.reshape(out_weight.shape),
        sums[2],
        sums[0],
        sums[1],
        grad_up.reshape(up_weight.shape),
        sums[6],
        grad_down.reshape(down_weight.shape),
        sums[5],
        sums[3],
        sums[4],
    )


def solution(mesh):
    dp, tensor = mesh.shape["dp"], mesh.shape["tensor"]
    rows = P(("dp", "tensor"), None)
    placed = (
        rows,
        P(None, None, "tensor"),
        P(None, "tensor"),
        P("tensor", None),
        P(),
        P(),
        P(),
        P(None, "tensor"),
        P("tensor"),
        P("tensor", None),
        P(),
        P(),
        P(),
        rows,
    )
    return jax.shard_map(
        functools.partial(on_device, dp, tensor),
        mesh=mesh,
        in_specs=placed,
        out_specs=(rows, rows) + placed[1:13],
        check_vma=False,
    )
```

```python
import functools

import jax
import jax.numpy as jnp
import numpy as np
from jax import lax
from jax.experimental import pallas as pl
from jax.experimental.pallas import tpu as pltpu
from jax.sharding import PartitionSpec as P

HEAD_SIZE = 64
LENGTH = 512
EPSILON = 1e-05
BF16 = jnp.bfloat16
F32 = jnp.float32
RING = 8
MIB = 2**20


def dot(a, b):
    return jnp.dot(a, b, preferred_element_type=F32)


def dot_t(a, b):
    return lax.dot_general(a, b, (((1,), (1,)), ((), ())), preferred_element_type=F32)


def dot_l(a, b):
    return lax.dot_general(a, b, (((0,), (0,)), ((), ())), preferred_element_type=F32)


class Given:
    def __init__(self, ref, copy=None):
        self.ref, self.copy = ref, copy

    def __call__(self):
        if self.copy is not None:
            self.copy.wait()
            self.copy = None
        return self.ref


class Result:
    def __init__(self, ref, copy=None):
        self.ref, self.copy, self.sent = ref, copy, False

    def send(self):
        if self.copy is not None and not self.sent:
            self.copy.start()
            self.sent = True

    def finish(self):
        self.send()
        if self.copy is not None:
            self.copy.wait()


VM = (6, 6, 8, 8, 8, 8, 8, 4)
HERE, THERE = "vmem", "hbm"


COSTS = {
    "attend": 18.4,
    "attend_back": 0.13,
    "mix_out": 2.4,
    "feed": 0.8,
    "second_grad": 4.0,
    "second_rest": 0.6,
    "feed_back": 22.0,
    "near_grads": 0.64,
    "weight_grad": 0.64,
    "first_back": 0.4,
    "heads_back": 1.2,
    "proj_back": 2.4,
    "mixed_grad": 1.0,
    "token_sum": 0.4,
    "add": 1.0,
    "place": 0.16,
    "ring": 2.8,
}


def cost(us):
    return pl.CostEstimate(flops=int(us * 1e9), bytes_accessed=1024, transcendentals=0)


def keep(array):
    return pltpu.with_memory_space_constraint(array, pltpu.HBM)


def call(body, args, outs, vmem, us, scratch=(), index=None, aliases=None):
    spaces = {HERE: pltpu.VMEM, THERE: pltpu.HBM}
    far_in = [i for i, (_, place) in enumerate(args) if place == THERE]
    far_out = [i for i, (_, _, place) in enumerate(outs) if place == THERE]
    scalars = [] if index is None else [index]

    def kernel(*refs):
        scalar, refs = refs[: len(scalars)], refs[len(scalars) :]
        given, refs = list(refs[: len(args)]), refs[len(args) :]
        result, refs = list(refs[: len(outs)]), refs[len(outs) :]
        slots_in, refs = refs[: len(far_in)], refs[len(far_in) :]
        slots_out, refs = refs[: len(far_out)], refs[len(far_out) :]
        if far_in:
            done_in, refs = refs[0], refs[1:]
        if far_out:
            done_out, refs = refs[0], refs[1:]
        given = [Given(ref) for ref in given]
        for slot, i in enumerate(far_in):
            copy = pltpu.make_async_copy(given[i].ref, slots_in[slot], done_in.at[slot])
            copy.start()
            given[i] = Given(slots_in[slot], copy)
        result = [Result(ref) for ref in result]
        for slot, i in enumerate(far_out):
            copy = pltpu.make_async_copy(slots_out[slot], result[i].ref, done_out.at[slot])
            result[i] = Result(slots_out[slot], copy)
        body(given, result, *scalar, *refs)
        for item in given:
            item()
        for item in result:
            item.send()
        for item in result:
            item.finish()

    room = [pltpu.VMEM(args[i][0].shape, args[i][0].dtype) for i in far_in]
    room += [pltpu.VMEM(outs[i][0], outs[i][1]) for i in far_out]
    room += [pltpu.SemaphoreType.DMA((len(far),)) for far in (far_in, far_out) if far]
    return pl.pallas_call(
        kernel,
        out_shape=tuple(
            (pltpu.HBM if place == THERE else jax.ShapeDtypeStruct)(dims, kind) for dims, kind, place in outs
        ),
        in_specs=[pl.BlockSpec(memory_space=pltpu.SMEM)] * len(scalars)
        + [pl.BlockSpec(memory_space=spaces[place]) for _, place in args],
        out_specs=tuple(pl.BlockSpec(memory_space=spaces[place]) for _, _, place in outs),
        scratch_shapes=room + list(scratch),
        input_output_aliases={len(scalars) + i: o for i, o in (aliases or {}).items()},
        compiler_params=pltpu.CompilerParams(vmem_limit_bytes=vmem * MIB),
        cost_estimate=cost(us),
    )(*scalars, *(keep(array) if place == THERE else array for array, place in args))


def attend_kernel(given, result):
    first, second, weight, bias = given
    query, key, value, mixed_first, mixed_second = result
    bias_wide = bias()[...].astype(F32)
    rows = first.ref.shape[0]
    width = query.ref.shape[1]
    weight = weight()
    for half, part in enumerate((first, second)):
        block = pl.ds(half * rows, rows)
        part = part()[...]
        query.ref[block, :] = ((dot(part, weight[0]) + bias_wide[0:1, :]) * 0.125).astype(BF16)
        key.ref[block, :] = dot(part, weight[1]).astype(BF16)
        value.ref[block, :] = (dot(part, weight[2]) + bias_wide[1:2, :]).astype(BF16)
    for item in (query, key, value):
        item.send()
    low_half = lax.broadcasted_iota(jnp.int32, (rows, 128), 1) < HEAD_SIZE
    for half, mixed in enumerate((mixed_second, mixed_first)):
        block = pl.ds((1 - half) * rows, rows)
        for pair in range(width // 128):
            cols = pl.ds(pair * 128, 128)
            q_pair = query.ref[block, cols]
            k_pair = key.ref[:, cols]
            v_pair = value.ref[:, cols]
            outs = []
            for side in range(2):
                keep = low_half if side == 0 else ~low_half
                scores = dot_t(jnp.where(keep, q_pair, jnp.zeros_like(q_pair)), k_pair)
                weights = jnp.exp(scores - jnp.max(scores, -1, keepdims=True))
                total = jnp.sum(weights, -1, keepdims=True)
                probs = (weights * (1.0 / total)).astype(BF16)
                outs.append(dot(probs, v_pair))
            mixed.ref[:, cols] = jnp.where(low_half, outs[0], outs[1]).astype(BF16)


def attend(first, second, weight, bias, own=False):
    rows, width = first.shape[0], weight.shape[2]
    args = [(first, THERE if own else HERE), (second, HERE), (weight, THERE), (bias, THERE)]
    outs = [((2 * rows, width), BF16, THERE)] * 3 + [((rows, width), BF16, HERE)] * 2
    return call(attend_kernel, args, outs, VM[0], COSTS["attend"])


def attend_back_kernel(given, result, key_sum, value_sum):
    query, key, value, grad_first, grad_second = given
    query, key, value = query(), key(), value()
    near, far = (item.ref for item in result)
    rows = near.shape[1]
    width = near.shape[2]
    low_half = lax.broadcasted_iota(jnp.int32, (rows, 128), 1) < HEAD_SIZE
    low_all = lax.broadcasted_iota(jnp.int32, (2 * rows, 128), 1) < HEAD_SIZE
    for pair in range(width // 128):
        cols = pl.ds(pair * 128, 128)
        k_pair = key[:, cols]
        v_pair = value[:, cols]
        for half, (grads, out) in enumerate(((grad_first(), near), (grad_second(), far))):
            q_pair = query[pl.ds(half * rows, rows), cols]
            g_pair = grads[:, cols]
            dq, dk, dv = [], [], []
            for side in range(2):
                keep = low_half if side == 0 else ~low_half
                scores = dot_t(jnp.where(keep, q_pair, jnp.zeros_like(q_pair)), k_pair)
                weights = jnp.exp(scores - jnp.max(scores, -1, keepdims=True))
                total = jnp.sum(weights, -1, keepdims=True)
                probs = weights * (1.0 / total)
                grad_probs = dot_t(jnp.where(keep, g_pair, jnp.zeros_like(g_pair)), v_pair)
                inner = probs * grad_probs
                grad_scores = (inner - probs * jnp.sum(inner, -1, keepdims=True)).astype(BF16)
                dv.append(dot_l(probs.astype(BF16), g_pair))
                dq.append(dot(grad_scores, k_pair))
                dk.append(dot_l(grad_scores, q_pair))
            out[0, :, cols] = (jnp.where(low_half, dq[0], dq[1]).astype(BF16).astype(F32) * 0.125).astype(BF16)
            dk_pair = jnp.where(low_all, dk[0], dk[1])
            dv_pair = jnp.where(low_all, dv[0], dv[1])
            if half == 0:
                key_sum[...] = dk_pair
                value_sum[...] = dv_pair
        for i, (part, last) in enumerate(((key_sum, dk_pair), (value_sum, dv_pair))):
            total = (part[...] + last).astype(BF16)
            near[1 + i, :, cols] = total[:rows]
            far[1 + i, :, cols] = total[rows:]


def attend_back(query, key, value, grad_first, grad_second):
    length, width = query.shape
    args = [(query, THERE), (key, THERE), (value, THERE), (grad_first, HERE), (grad_second, HERE)]
    outs = [((3, length // 2, width), BF16, HERE)] * 2
    return call(attend_back_kernel, args, outs, VM[1], COSTS["attend_back"], [pltpu.VMEM((length, 128), F32), pltpu.VMEM((length, 128), F32)])


def mix_out_kernel(given, result):
    mix, mix_peer, weight, weight_peer = given
    out = dot(mix()[...], weight()[...]) + dot(mix_peer()[...], weight_peer()[...])
    result[0].ref[...] = out
    result[1].ref[...] = out.astype(BF16)


def mix_out(mix, mix_peer, weight, weight_peer):
    args = [(mix, HERE), (mix_peer, HERE), (weight, HERE), (weight_peer, HERE)]
    dims = (mix.shape[0], weight.shape[1])
    return call(mix_out_kernel, args, [(dims, F32, HERE), (dims, BF16, HERE)], 4, COSTS["mix_out"])


def center_scale(values):
    center = values - jnp.mean(values, -1, keepdims=True)
    spread = jnp.mean(center * center, -1, keepdims=True)
    scale = lax.rsqrt(spread + EPSILON)
    return center * scale, scale


def norm_back(grad, unit, scale, gain):
    grad_unit = grad * gain
    return scale * (
        grad_unit
        - jnp.mean(grad_unit, -1, keepdims=True)
        - unit * jnp.mean(grad_unit * unit, -1, keepdims=True)
    )


def gate(pre):
    cdf = 0.5 * (1.0 + lax.erf(pre * np.float32(np.sqrt(0.5))))
    density = np.float32(1 / np.sqrt(2 * np.pi)) * jnp.exp(-0.5 * pre * pre)
    return pre * cdf, cdf + pre * density


def feed_kernel(own, given, result):
    tok, low, far, out_bias, gain, shift, bias, bias_peer = (item()[...].astype(F32) for item in given[:8])
    weights = given[8:]
    if own:
        first, wide, result = result[0], result[1], result[2:]
    normed, act, act_peer, slope, slope_peer, out = result
    first_sum = tok + low + far + out_bias
    unit, _ = center_scale(first_sum)
    value = unit * gain + shift
    if own:
        first.ref[...] = first_sum
        first.send()
        wide.ref[...] = value
    normed.ref[...] = value.astype(BF16)
    normed.send()
    step = 256
    for weight, bias_of, act_of, slope_of in ((weights[0], bias, act, slope), (weights[1], bias_peer, act_peer, slope_peer)):
        for start in range(0, act_of.ref.shape[1], step):
            cols = pl.ds(start, step)
            pre = dot(normed.ref[...], weight()[:, cols]) + bias_of[:, start : start + step]
            act_of.ref[:, cols], slope_of.ref[:, cols] = (
                part.astype(kind) for part, kind in zip(gate(pre), (BF16, F32))
            )
        act_of.send()
        slope_of.send()
    total = dot(act.ref[...], weights[2]()[...]) + dot(act_peer.ref[...], weights[3]()[...])
    out.ref[...] = total.astype(out.ref.dtype)


def feed(own, tok, low, far, out_bias, gain, shift, bias, bias_peer, weights):
    rows, model = tok.shape
    hidden = weights[0].shape[1]
    outs = [((rows, model), F32, THERE), ((rows, model), F32, HERE)] if own else []
    outs += [((rows, model), BF16, HERE), ((rows, hidden), BF16, THERE), ((rows, hidden), BF16, HERE)]
    outs += [((rows, hidden), F32, THERE)] * 2
    outs.append(((rows, model), F32 if own else BF16, HERE))
    args = [(v, HERE) for v in (tok, low, far, out_bias, gain, shift, bias, bias_peer, *weights)]
    return call(functools.partial(feed_kernel, own), args, outs, VM[2], COSTS["feed"])


def second_parts(given):
    wide, feed_sum, far, down_bias, gain, shift, cot = (item()[...].astype(F32) for item in given)
    unit, scale = center_scale(wide + feed_sum + far + down_bias)
    return unit, scale, gain, shift, cot


def second_grad_kernel(given, result):
    unit, scale, gain, _, cot = second_parts(given)
    result[0].ref[...] = norm_back(cot, unit, scale, gain).astype(BF16)


def second_rest_kernel(given, result):
    unit, scale, gain, shift, cot = second_parts(given)
    layer_out, grad, sums = result
    layer_out.ref[...] = (unit * gain + shift).astype(BF16)
    layer_out.send()
    grad_second = norm_back(cot, unit, scale, gain)
    grad.ref[...] = grad_second
    grad.send()
    sums.ref[...] = jnp.zeros_like(sums.ref)
    sums.ref[3:4, :] = jnp.sum(cot * unit, 0, keepdims=True)
    sums.ref[4:5, :] = jnp.sum(cot, 0, keepdims=True)
    sums.ref[5:6, :] = jnp.sum(grad_second, 0, keepdims=True)


def second_grad(*values):
    return call(second_grad_kernel, [(v, HERE) for v in values], [(values[0].shape, BF16, HERE)], 6, COSTS["second_grad"])[0]


def second_rest(*values):
    dims = values[0].shape
    outs = [(dims, BF16, THERE), (dims, F32, THERE), ((8, dims[1]), F32, HERE)]
    return call(second_rest_kernel, [(v, HERE) for v in values], outs, 8, COSTS["second_rest"])


def feed_back_kernel(given, result):
    grad, slope, slope_peer, up, up_peer, down, down_peer, *more = given
    pre, pre_peer, out = result
    step = 256
    for slope_of, pre_of, weight in ((slope, pre, down), (slope_peer, pre_peer, down_peer)):
        for first in range(0, pre.ref.shape[1], step):
            cols = pl.ds(first, step)
            grad_act = dot_t(grad()[...], weight()[cols, :])
            pre_of.ref[:, cols] = (slope_of()[:, cols] * grad_act).astype(BF16)
        pre_of.send()
    total = dot_t(pre.ref[...], up()[...]) + dot_t(pre_peer.ref[...], up_peer()[...])
    for part in more:
        total += part()[...]
    out.ref[...] = total.astype(out.ref.dtype)


def feed_back(grad, slope, slope_peer, weights, wide=None):
    own = wide is not None
    rows, model = grad.shape
    hidden = slope.shape[1]
    outs = [((rows, hidden), BF16, THERE), ((rows, hidden), BF16, HERE)]
    outs.append(((rows, model), F32, THERE) if own else ((rows, model), BF16, HERE))
    args = [(grad, HERE), (slope, THERE), (slope_peer, THERE)] + [(v, HERE) for v in weights] + [(wide, THERE)] * own
    return call(feed_back_kernel, args, outs, VM[3], COSTS["feed_back"])


def summed(left, right):
    total = dot_l(left[0], right[0])
    for a, b in zip(left[1:], right[1:]):
        total += dot_l(a, b)
    return total


def add_products(out, half, left, right, fresh):
    chunks, tall = out.shape[0], out.shape[1] // 2
    rows = pl.ds(half * tall, tall)
    step = 256
    left = [part()[...] for part in left]
    for first in range(0, out.shape[2], step):
        cols = pl.ds(first, step)
        block = summed(left, [part()[:, cols] for part in right]).reshape(chunks, tall, step)
        if fresh:
            out[:, rows, cols] = block
        else:
            out[:, rows, cols] += block


def near_grads_kernel(given, result):
    out, total = (item.ref for item in result)
    add_products(out, 0, given[:2], given[2:4], True)
    left, right = given[4:5], given[5:]
    add_products(out, 1, left, right, True)
    total[...] = dot_l(jnp.ones((right[0].ref.shape[0], 8), BF16), right[0]()[...])


def near_grads(args, vmem):
    wide, tall = args[2][0].shape[1], args[0][0].shape[1] // RING
    outs = [((RING, 2 * tall, wide), F32, HERE), ((8, wide), F32, HERE)]
    return call(near_grads_kernel, args, outs, vmem, COSTS["near_grads"])


def far_grads_kernel(half, given, result, index):
    grads, *given = given
    parts = 2 + half
    left, right, more = given[:parts], given[parts : 2 * parts], given[2 * parts :]
    out, moving = result[0].ref, result[-1].ref
    add_products(out, half, left, right, False)
    if half:
        ones = jnp.ones((right[0].ref.shape[0], 8), BF16)
        result[1].ref[...] = more[0]()[...] + summed([ones] * parts, [part()[...] for part in right])
    tall = moving.shape[0]
    moving[...] = out[index[out.shape[0] // 2], pl.ds(half * tall, tall)].astype(BF16)


def far_grads(half, grads, args, index, vmem, total=None):
    wide, tall = grads.shape[2], grads.shape[1] // 2
    more = [(total, HERE)] if half else []
    outs = [(grads.shape, F32, HERE)] + [((8, wide), F32, HERE)] * half + [((tall, wide), BF16, HERE)]
    body = functools.partial(far_grads_kernel, half)
    return call(body, [(grads, HERE), *args, *more], outs, vmem, COSTS["weight_grad"], index=index, aliases={0: 0})


def first_back_kernel(given, result):
    first, gain, near, far_back, weight, weight_peer, sums_second = given
    grad, grad_low, sent, heads, sums = result
    unit, scale = center_scale(first()[...])
    grad_normed = near()[...] + far_back()[...].astype(F32)
    grad_first = norm_back(grad_normed, unit, scale, gain()[...].astype(F32))
    grad.ref[...] = grad_first
    grad.send()
    low = grad_first.astype(BF16)
    grad_low.ref[...] = low
    width = heads.ref.shape[1]
    sent.ref[:, width:] = low
    heads.ref[...] = dot_t(low, weight()[...]).astype(BF16)
    sent.ref[:, :width] = dot_t(low, weight_peer()[...]).astype(BF16)
    sums.ref[...] = sums_second()[...]
    sums.ref[0:1, :] = jnp.sum(grad_normed * unit, 0, keepdims=True)
    sums.ref[1:2, :] = jnp.sum(grad_normed, 0, keepdims=True)
    sums.ref[2:3, :] = jnp.sum(grad_first, 0, keepdims=True)


def first_back(first, gain, near, far_back, weight, weight_peer, sums):
    dims, width = first.shape, weight.shape[0]
    args = [(first, THERE), (gain, HERE), (near, THERE)]
    args += [(v, HERE) for v in (far_back, weight, weight_peer, sums)]
    outs = [(dims, F32, THERE), (dims, BF16, HERE)]
    outs += [((dims[0], width + dims[1]), BF16, HERE), ((dims[0], width), BF16, HERE), (sums.shape, F32, HERE)]
    return call(first_back_kernel, args, outs, VM[5], COSTS["first_back"])


def heads_back_kernel(given, result):
    grad, weight, weight_peer = given
    sent, heads = (item.ref for item in result)
    low = grad()[...]
    width = heads.shape[1]
    sent[:, width:] = low
    heads[...] = dot_t(low, weight()[...]).astype(BF16)
    sent[:, :width] = dot_t(low, weight_peer()[...]).astype(BF16)


def heads_back(grad, weight, weight_peer):
    rows, model = grad.shape
    width = weight.shape[0]
    outs = [((rows, width + model), BF16, HERE), ((rows, width), BF16, HERE)]
    return call(heads_back_kernel, [(grad, HERE), (weight, HERE), (weight_peer, HERE)], outs, 4, COSTS["heads_back"])


def proj_back_kernel(given, result):
    near, far, weight, weight_peer = (item() for item in given)
    total = dot_t(near[0], weight[0]) + dot_t(far[0], weight_peer[0])
    for i in (1, 2):
        total += dot_t(near[i], weight[i]) + dot_t(far[i], weight_peer[i])
    result[0].ref[...] = total.astype(result[0].ref.dtype)


def proj_back(near, far, weight, weight_peer, kind, space):
    args = [(v, HERE) for v in (near, far, weight, weight_peer)]
    return call(proj_back_kernel, args, [((near.shape[1], weight.shape[1]), kind, space)], VM[7], COSTS["proj_back"])[0]


def mixed_grad_kernel(given, result, index, total):
    toks, nears, mixes, grads = given[:4], given[4:8], given[8:12], given[12:]
    out, bias, *moving = (item.ref for item in result)
    width = total.shape[1]
    model = total.shape[0] // 3
    chunks = out.shape[0]
    share = width // chunks
    tall = out.shape[1] - model // width * share
    mixed = [part()[...] for part in mixes]
    for j in range(model // width):
        block = summed(mixed, [part()[:, pl.ds(part.ref.shape[1] - model + j * width, width)] for part in grads])
        out[:, pl.ds(tall + j * share, share), :] = block.reshape(chunks, share, width)
    lefts = [part()[...] for part in toks]
    ones = [jnp.ones((lefts[0].shape[0], 8), BF16)] * 4
    for j in range(3):
        right = [part()[j] for part in nears]
        total[pl.ds(j * model, model), :] = summed(lefts, right)
        if j != 1:
            bias[:, pl.ds(j // 2 * width, width)] = summed(ones, right)
    for i in range(chunks):
        out[i, pl.ds(0, tall), :] = total[pl.ds(i * tall, tall), :]
    half = out.shape[1] // 2
    for i, part in enumerate(moving):
        part[...] = out[index[chunks // 2], pl.ds(i * half, half)].astype(BF16)


def mixed_grad(toks, nears, mixes, grads, index, vmem):
    model, width = toks[0].shape[1], mixes[0].shape[1]
    tall = 4 * model // RING
    outs = [((RING, tall, width), F32, HERE), ((8, 2 * width), F32, HERE)] + [((tall // 2, width), BF16, HERE)] * 2
    args = [(v, HERE) for v in (*toks, *nears, *mixes, *grads)]
    return call(mixed_grad_kernel, args, outs, vmem, COSTS["mixed_grad"], [pltpu.VMEM((3 * model, width), F32)], index)


def token_grad_kernel(given, result):
    grad, near, far = given
    result[0].ref[...] = grad()[...] + near()[...] + far()[...].astype(F32)


def token_sum(grad, near, far):
    args = [(grad, THERE), (near, THERE), (far, HERE)]
    return call(token_grad_kernel, args, [(grad.shape, F32, THERE)], 8, COSTS["token_sum"])[0]


def ring_step_kernel(places, given, result, index):
    grad = given[0].ref
    for side, (place, arrived, moving) in enumerate(zip(places, given[1:], result)):
        rows = arrived.ref.shape[0]
        first = side * (grad.shape[1] - rows)
        own = grad[index[place]]
        if rows < grad.shape[1]:
            moving.ref[...] = own.astype(BF16)
        block = pl.ds(first, rows)
        moving.ref[block, :] = (grad[index[place], block] + arrived()[...].astype(F32)).astype(BF16)


def ring_last_kernel(given, result, index):
    grad, ahead, behind = given
    total = grad.ref[index[0]] + ahead()[...].astype(F32) + behind()[...].astype(F32)
    result[0].ref[...] = total
    result[1].ref[...] = total.astype(BF16)


def ring_step(grad, arrived, index, places):
    args = [(v, HERE) for v in (grad, *arrived)]
    outs = [(grad.shape[1:], BF16, HERE)] * 2
    return call(functools.partial(ring_step_kernel, places), args, outs, 3, COSTS["ring"], index=index)


def ring_last(grad, arrived, index):
    args = [(v, HERE) for v in (grad, *arrived)]
    outs = [(grad.shape[1:], kind, HERE) for kind in (F32, BF16)]
    return call(ring_last_kernel, args, outs, 2, COSTS["ring"], index=index)


def place_kernel(bands, order, given, result, index, *scratch):
    wides, semaphores = scratch[:-1], scratch[-1]
    copies = []
    for i, place in enumerate(order):
        parts = given[i:] if i == len(order) - 1 else given[i : i + 1]
        chunk = jnp.concatenate([part()[...] for part in parts], 0).astype(F32)
        for j, ((first, rows, columns), wide, out) in enumerate(zip(bands, wides, result)):
            width = chunk.shape[1]
            for k in range(columns // width):
                wide[i, :, pl.ds(k * width, width)] = chunk[first + k * rows : first + (k + 1) * rows]
            target = pl.ds(pl.multiple_of(index[place] * rows, 8), rows)
            copies.append(pltpu.make_async_copy(wide.at[i], out.at[target], semaphores.at[i, j]))
            copies[-1].start()
    for copy in copies:
        copy.wait()


def place(chunks, held, index, bands, order):
    there = pl.BlockSpec(memory_space=pltpu.HBM)
    count, results, parts = len(chunks), len(bands), len(order)
    held = held or ()

    def kernel(index, *refs):
        given, refs = refs[:count], refs[count + len(held) :]
        place_kernel(bands, order, [Given(ref) for ref in given], refs[:results], index, *refs[results:])

    scratch = [pltpu.VMEM((parts, rows, columns), F32) for _, rows, columns in bands]
    return pl.pallas_call(
        kernel,
        out_shape=tuple(pltpu.HBM((RING * rows, columns), F32) for _, rows, columns in bands),
        in_specs=[pl.BlockSpec(memory_space=pltpu.SMEM)]
        + [pl.BlockSpec(memory_space=pltpu.VMEM)] * count
        + [there] * len(held),
        out_specs=tuple(there for _ in bands),
        scratch_shapes=scratch + [pltpu.SemaphoreType.DMA((parts, results))],
        input_output_aliases={1 + count + i: i for i in range(len(held))},
        compiler_params=pltpu.CompilerParams(vmem_limit_bytes=8 * MIB),
        cost_estimate=cost(COSTS["place"]),
    )(index, *chunks, *(keep(v) for v in held))


def add_kernel(given, result):
    total = given[0]()[...] + given[1]()[...]
    result[0].ref[...] = total


def add(a, b):
    return call(add_kernel, [(a, HERE), (b, HERE)], [(a.shape, a.dtype, HERE)], 2, COSTS["add"])[0]


def add_rows_kernel(given, result):
    a, b, hidden, wide = (item() for item in given)
    out = result[0].ref
    out[...] = a[...] + b[...]
    out[6:7, :] = hidden[0:1, :]
    out[7:8, : wide.shape[1]] = wide[0:1, :]


def add_rows(a, b, hidden, wide):
    return call(add_rows_kernel, [(v, HERE) for v in (a, b, hidden, wide)], [(a.shape, F32, HERE)], 2, COSTS["add"])[0]


def swap(values, bit, tensor):
    return lax.ppermute(values, "tensor", [(i, i ^ bit) for i in range(tensor)])


class Line:
    def __init__(self):
        self.last = None

    def run(self, body, *args):
        if self.last is not None:
            args, _ = lax.optimization_barrier((args, self.last))
        out = body(*args)
        self.last = jax.tree.leaves(out)[-1]
        return out

    def land(self, values):
        return lax.optimization_barrier((values, self.last))[0]

    def settle(self, *values):
        self.last = lax.optimization_barrier((values, self.last))[0]
        return self.last if len(values) > 1 else self.last[0]


def ring_order(dp):
    return list(range(0, dp, 2)) + list(range(dp - 1, 0, -2))


class Ring:
    def __init__(self, line, dp, index, bands):
        self.bands = bands
        order = ring_order(dp)
        self.ways = [[(order[i], order[(i + way) % dp]) for i in range(dp)] for way in (1, -1)]
        self.line, self.dp, self.index = line, dp, index
        self.step, self.half = 0, dp // 2
        self.flying, self.outs = [], None

    def send(self, *moving):
        for part in moving:
            self.flying.append(lax.ppermute(part, "dp", self.ways[len(self.flying)]))

    def tick(self):
        self.step += 1
        step, half, run = self.step, self.half, self.line.run
        arrived, self.flying = tuple(self.flying), []
        if step < half:
            places = (half - step, self.dp + step - half)
            self.send(*run(functools.partial(ring_step, places=places), self.grad, arrived, self.index))
        elif step == half:
            self.total, moving = run(ring_last, self.grad, arrived, self.index)
            self.send(moving, moving)
        else:
            step -= half
            arrived = self.line.settle(*arrived)
            if step < half - 1:
                self.send(*arrived)
            elif step < half:
                rows = arrived[0].shape[0] // 2
                self.send(arrived[0][:rows], arrived[1][rows:])
            order = (self.dp - step, step) if step < half else (step,)
            if step == 1:
                arrived, order = (self.total, *arrived), (0, *order)
            self.put(arrived, order)

    def put(self, chunks, order):
        body = functools.partial(place, bands=self.bands, order=order)
        self.outs = self.line.run(body, chunks, self.outs, self.index)


def on_device(
    dp,
    tensor,
    tokens,
    qkv_weight,
    qv_bias,
    out_weight,
    out_bias,
    norm1_gain,
    norm1_bias,
    up_weight,
    up_bias,
    down_weight,
    down_bias,
    norm2_gain,
    norm2_bias,
    cotangent,
):
    core = functools.partial(swap, bit=1, tensor=tensor)
    chip = functools.partial(swap, bit=2, tensor=tensor)
    rows, model = tokens.shape
    width = qkv_weight.shape[2]
    hidden = up_weight.shape[1]
    ring = dp == RING
    room = 8 if ring else 48
    line = Line()
    run, land, settle = line.run, line.land, line.settle

    def row(values):
        return values.reshape(1, -1)

    index = jnp.arange(RING, dtype=jnp.int32)
    if ring:
        turns = np.zeros((dp, dp), np.int32)
        for at, device in enumerate(ring_order(dp)):
            turns[device] = (at + np.arange(dp)) % dp
        index = lax.dynamic_index_in_dim(jnp.asarray(turns), lax.axis_index("dp"), 0, keepdims=False)
        line.last = index
    out_bias, down_bias = row(out_bias), row(down_bias)
    gain1, shift1, gain2, shift2 = (row(v) for v in (norm1_gain, norm1_bias, norm2_gain, norm2_bias))
    tok_a = tokens
    tok_c = chip(tok_a)
    tok_b = core(tok_a)
    out_peer, up_peer = core(out_weight), core(up_weight)
    q_ab, k_ab, v_ab, mix_a, mix_b = run(functools.partial(attend, own=True), tok_a, tok_b, qkv_weight, qv_bias)
    mix_b_peer = core(mix_b)
    out_peer, up_peer = settle(out_peer, up_peer)
    part_a, low_a = run(mix_out, mix_a, mix_b_peer, out_weight, out_peer)
    far_c = chip(low_a)
    down_peer = core(land(down_weight))
    tok_c = settle(tok_c)
    tok_d = core(tok_c)
    q_cd, k_cd, v_cd, mix_c, mix_d = run(attend, tok_c, tok_d, qkv_weight, qv_bias)
    part_c, low_c = run(mix_out, mix_c, core(mix_d), out_weight, out_peer)
    far_a = chip(low_c)
    up_bias_peer, down_peer = settle(core(land(up_bias)), down_peer)
    up_bias, up_bias_peer = row(up_bias), row(up_bias_peer)
    weights = (up_weight, up_peer, down_weight, down_peer)
    nrm_c, act_c, act_peer_c, slope_c, slope_peer_c, feed_c = run(
        functools.partial(feed, False), tok_c, part_c, far_c, out_bias, gain1, shift1, up_bias, up_bias_peer, weights
    )
    far_feed = chip(feed_c)
    act_d, nrm_d = core(act_peer_c), core(nrm_c)
    first_a, wide_a, nrm_a, act_a, act_peer_a, slope_a, slope_peer_a, feed_a = run(
        functools.partial(feed, True), tok_a, part_a, far_a, out_bias, gain1, shift1, up_bias, up_bias_peer, weights
    )
    act_d, nrm_d = settle(act_d, nrm_d)
    act_b, nrm_b = core(act_peer_a), core(nrm_a)
    second = (wide_a, feed_a, land(far_feed), down_bias, gain2, shift2, cotangent)
    gs_a = run(second_grad, *second)
    gs_c = chip(gs_a)
    layer_out, grad_second, sums = run(second_rest, *second)
    act_b, nrm_b = settle(act_b, nrm_b)
    qkv_peer = core(land(qkv_weight))
    gs_b = core(gs_a)
    gp_a, gp_peer_a, back_a = run(
        feed_back, gs_a, slope_a, slope_peer_a, weights, grad_second
    )
    gs_b, qkv_peer = settle(gs_b, qkv_peer)
    gp_b = core(gp_peer_a)

    def add_near(*values):
        return near_grads(list(zip(values, (THERE, HERE, HERE, HERE, HERE, THERE))), room)

    grads, up_sum = run(add_near, act_a, act_b, gs_a, gs_b, nrm_a, gp_a)
    gs_c = settle(gs_c)
    gs_d = core(gs_c)
    gp_c, gp_peer_c, back_c = run(
        feed_back, gs_c, slope_c, slope_peer_c, weights
    )
    far_back = chip(back_c)
    gp_d = core(gp_peer_c)

    half, tall, share = model // RING, 3 * model // RING, width // RING
    ring_feed, ring_mixed = (
        Ring(line, dp, index, bands) if ring else None
        for bands in (((0, half, model), (half, half, hidden)), ((0, tall, width), (tall, share, model)))
    )

    def tick(*items):
        for item in items:
            if ring:
                item.tick()

    def send(item, *moving):
        if ring:
            item.send(*moving)

    def add_far(half, grads, left, right, index, total=None):
        places = ((THERE, HERE), (HERE, HERE)) if half == 0 else ((HERE,) * 3, (HERE, THERE, HERE))
        return far_grads(half, grads, [*zip(left, places[0]), *zip(right, places[1])], index, room, total)

    grads, moving = run(functools.partial(add_far, 0), grads, (act_c, act_d), (gs_c, gs_d), index)
    send(ring_feed, moving)
    grads, up_sum, moving = run(
        functools.partial(add_far, 1), grads, (nrm_b, nrm_c, nrm_d), (gp_b, gp_c, gp_d), index, up_sum
    )
    send(ring_feed, moving)
    if ring:
        ring_feed.grad = grads
    far_back = settle(far_back)
    grad_first, gf_a, sent_a, gh_a, sums = run(
        first_back, first_a, gain1, back_a, far_back, out_weight, out_peer, sums
    )
    gf_c = chip(gf_a)
    back_b = core(sent_a)
    tick(ring_feed)
    back_b = settle(back_b)
    flying = core(sums)
    gr_a, gr_b = run(attend_back, q_ab, k_ab, v_ab, gh_a, back_b)
    far_gr_b = core(gr_b)
    tick(ring_feed)
    gf_c = settle(gf_c)
    far_gr_b, flying = settle(far_gr_b, flying)
    sent_c, gh_c = run(heads_back, gf_c, out_weight, out_peer)
    back_d = settle(core(sent_c))
    gr_c, gr_d = run(attend_back, q_cd, k_cd, v_cd, gh_c, back_d)
    grad_mixed, qv_sum, *moving = run(
        functools.partial(mixed_grad, vmem=room),
        (tok_a, tok_b, tok_c, tok_d),
        (gr_a, gr_b, gr_c, gr_d),
        (mix_a, mix_b, mix_c, mix_d),
        (gf_a, back_b, gf_c, back_d),
        index,
    )
    send(ring_mixed, *moving)
    if ring:
        ring_mixed.grad = grad_mixed
    tick(ring_feed)
    sums = run(add, sums, flying)
    flying = chip(sums)
    tick(ring_mixed)
    flying = settle(flying)
    sums = run(add_rows, sums, flying, up_sum, qv_sum)
    far_gr_d = core(land(gr_d))
    tick(ring_feed)
    far_gr_d = settle(far_gr_d)
    bits = [1 << i for i in range(dp.bit_length() - 1)]

    def hop(values):
        bit = bits.pop(0)
        return lax.ppermute(values, "dp", [(i, i ^ bit) for i in range(dp)])

    flying = hop(sums)
    rows_c = run(functools.partial(proj_back, kind=BF16, space=HERE), gr_c, far_gr_d, qkv_weight, qkv_peer)
    tick(ring_mixed)
    rows_a = run(functools.partial(proj_back, kind=F32, space=THERE), gr_a, far_gr_b, qkv_weight, qkv_peer)
    sums = run(add, sums, flying)
    flying = hop(sums)
    tick(ring_mixed)
    sums = run(add, sums, flying)
    flying = hop(sums)
    tick(ring_feed, ring_mixed)
    sums = run(add, sums, flying)
    while bits:
        sums = run(add, sums, hop(sums))
    far_rows = chip(land(rows_c))
    tick(ring_feed, ring_mixed, ring_mixed, ring_feed)
    token_grad = run(token_sum, grad_first, rows_a, land(far_rows))
    if ring:
        tick(ring_mixed, ring_feed, ring_mixed)
        (grad_down, grad_up), (grad_qkv, grad_out) = ring_feed.outs, ring_mixed.outs
    else:
        grads, grad_mixed = lax.psum((grads, grad_mixed), "dp")
        grad_down, grad_up = grads[:, :half], grads[:, half:]
        grad_qkv = grad_mixed[:, :tall]
        grad_out = grad_mixed[:, tall:].reshape(RING, model // width, share, width).swapaxes(1, 2)
    return (
        layer_out,
        token_grad,
        grad_qkv.reshape(qkv_weight.shape),
        sums[7, : 2 * width].reshape(2, width),
        grad_out.reshape(out_weight.shape),
        sums[2],
        sums[0],
        sums[1],
        grad_up.reshape(up_weight.shape),
        sums[6],
        grad_down.reshape(down_weight.shape),
        sums[5],
        sums[3],
        sums[4],
    )


def solution(mesh):
    dp, tensor = mesh.shape["dp"], mesh.shape["tensor"]
    rows = P(("dp", "tensor"), None)
    placed = (
        rows,
        P(None, None, "tensor"),
        P(None, "tensor"),
        P("tensor", None),
        P(),
        P(),
        P(),
        P(None, "tensor"),
        P("tensor"),
        P("tensor", None),
        P(),
        P(),
        P(),
        rows,
    )
    return jax.shard_map(
        functools.partial(on_device, dp, tensor),
        mesh=mesh,
        in_specs=placed,
        out_specs=(rows, rows) + placed[1:13],
        check_vma=False,
    )
```

```python
import functools

import jax
import jax.numpy as jnp
import numpy as np
from jax import lax
from jax.experimental import pallas as pl
from jax.experimental.pallas import tpu as pltpu
from jax.sharding import PartitionSpec as P

HEAD_SIZE = 64
LENGTH = 512
EPSILON = 1e-05
BF16 = jnp.bfloat16
F32 = jnp.float32
RING = 8
MIB = 2**20


def dot(a, b):
    return jnp.dot(a, b, preferred_element_type=F32)


def dot_t(a, b):
    return lax.dot_general(a, b, (((1,), (1,)), ((), ())), preferred_element_type=F32)


def dot_l(a, b):
    return lax.dot_general(a, b, (((0,), (0,)), ((), ())), preferred_element_type=F32)


class Given:
    def __init__(self, ref, copy=None):
        self.ref, self.copy = ref, copy

    def __call__(self):
        if self.copy is not None:
            self.copy.wait()
            self.copy = None
        return self.ref


class Result:
    def __init__(self, ref, copy=None):
        self.ref, self.copy, self.sent = ref, copy, False

    def send(self):
        if self.copy is not None and not self.sent:
            self.copy.start()
            self.sent = True

    def finish(self):
        self.send()
        if self.copy is not None:
            self.copy.wait()


VM = (6, 6, 8, 8, 8, 8, 8, 4)
HERE, THERE = "vmem", "hbm"


COSTS = {
    "attend": 18.4,
    "attend_back": 0.13,
    "mix_out": 2.4,
    "feed": 0.8,
    "second_grad": 4.0,
    "second_rest": 0.6,
    "feed_back": 22.0,
    "near_grads": 0.64,
    "weight_grad": 0.64,
    "first_back": 0.4,
    "heads_back": 1.2,
    "proj_back": 2.4,
    "mixed_grad": 0.05,
    "token_sum": 0.4,
    "add": 1.0,
    "place": 0.16,
    "feed_step1": 2.8,
    "feed_step2": 2.8,
    "feed_step3": 0.02,
    "feed_step4": 0.02,
    "mixed_step1": 0.02,
    "mixed_step2": 0.02,
    "mixed_step3": 0.02,
    "mixed_step4": 2.8,
    "attend_back_c": 0.13,
    "proj_back_c": 2.4,
    "add_rows": 1.0,
}


def cost(us):
    return pl.CostEstimate(flops=int(us * 1e9), bytes_accessed=1024, transcendentals=0)


def keep(array):
    return pltpu.with_memory_space_constraint(array, pltpu.HBM)


def call(body, args, outs, vmem, us, scratch=(), index=None, aliases=None):
    spaces = {HERE: pltpu.VMEM, THERE: pltpu.HBM}
    far_in = [i for i, (_, place) in enumerate(args) if place == THERE]
    far_out = [i for i, (_, _, place) in enumerate(outs) if place == THERE]
    scalars = [] if index is None else [index]

    def kernel(*refs):
        scalar, refs = refs[: len(scalars)], refs[len(scalars) :]
        given, refs = list(refs[: len(args)]), refs[len(args) :]
        result, refs = list(refs[: len(outs)]), refs[len(outs) :]
        slots_in, refs = refs[: len(far_in)], refs[len(far_in) :]
        slots_out, refs = refs[: len(far_out)], refs[len(far_out) :]
        if far_in:
            done_in, refs = refs[0], refs[1:]
        if far_out:
            done_out, refs = refs[0], refs[1:]
        given = [Given(ref) for ref in given]
        for slot, i in enumerate(far_in):
            copy = pltpu.make_async_copy(given[i].ref, slots_in[slot], done_in.at[slot])
            copy.start()
            given[i] = Given(slots_in[slot], copy)
        result = [Result(ref) for ref in result]
        for slot, i in enumerate(far_out):
            copy = pltpu.make_async_copy(slots_out[slot], result[i].ref, done_out.at[slot])
            result[i] = Result(slots_out[slot], copy)
        body(given, result, *scalar, *refs)
        for item in given:
            item()
        for item in result:
            item.send()
        for item in result:
            item.finish()

    room = [pltpu.VMEM(args[i][0].shape, args[i][0].dtype) for i in far_in]
    room += [pltpu.VMEM(outs[i][0], outs[i][1]) for i in far_out]
    room += [pltpu.SemaphoreType.DMA((len(far),)) for far in (far_in, far_out) if far]
    return pl.pallas_call(
        kernel,
        out_shape=tuple(
            (pltpu.HBM if place == THERE else jax.ShapeDtypeStruct)(dims, kind) for dims, kind, place in outs
        ),
        in_specs=[pl.BlockSpec(memory_space=pltpu.SMEM)] * len(scalars)
        + [pl.BlockSpec(memory_space=spaces[place]) for _, place in args],
        out_specs=tuple(pl.BlockSpec(memory_space=spaces[place]) for _, _, place in outs),
        scratch_shapes=room + list(scratch),
        input_output_aliases={len(scalars) + i: o for i, o in (aliases or {}).items()},
        compiler_params=pltpu.CompilerParams(vmem_limit_bytes=vmem * MIB),
        cost_estimate=cost(us),
    )(*scalars, *(keep(array) if place == THERE else array for array, place in args))


def attend_kernel(given, result):
    first, second, weight, bias = given
    query, key, value, mixed_first, mixed_second = result
    bias_wide = bias()[...].astype(F32)
    rows = first.ref.shape[0]
    width = query.ref.shape[1]
    weight = weight()
    for half, part in enumerate((first, second)):
        block = pl.ds(half * rows, rows)
        part = part()[...]
        query.ref[block, :] = ((dot(part, weight[0]) + bias_wide[0:1, :]) * 0.125).astype(BF16)
        key.ref[block, :] = dot(part, weight[1]).astype(BF16)
        value.ref[block, :] = (dot(part, weight[2]) + bias_wide[1:2, :]).astype(BF16)
    for item in (query, key, value):
        item.send()
    low_half = lax.broadcasted_iota(jnp.int32, (rows, 128), 1) < HEAD_SIZE
    for half, mixed in enumerate((mixed_second, mixed_first)):
        block = pl.ds((1 - half) * rows, rows)
        for pair in range(width // 128):
            cols = pl.ds(pair * 128, 128)
            q_pair = query.ref[block, cols]
            k_pair = key.ref[:, cols]
            v_pair = value.ref[:, cols]
            outs = []
            for side in range(2):
                keep = low_half if side == 0 else ~low_half
                scores = dot_t(jnp.where(keep, q_pair, jnp.zeros_like(q_pair)), k_pair)
                weights = jnp.exp(scores - jnp.max(scores, -1, keepdims=True))
                total = jnp.sum(weights, -1, keepdims=True)
                probs = (weights * (1.0 / total)).astype(BF16)
                outs.append(dot(probs, v_pair))
            mixed.ref[:, cols] = jnp.where(low_half, outs[0], outs[1]).astype(BF16)


def attend(first, second, weight, bias, own=False):
    rows, width = first.shape[0], weight.shape[2]
    args = [(first, THERE if own else HERE), (second, HERE), (weight, THERE), (bias, THERE)]
    outs = [((2 * rows, width), BF16, THERE)] * 3 + [((rows, width), BF16, HERE)] * 2
    return call(attend_kernel, args, outs, VM[0], COSTS["attend"])


def attend_back_kernel(given, result, key_sum, value_sum):
    query, key, value, grad_first, grad_second = given
    query, key, value = query(), key(), value()
    near, far = (item.ref for item in result)
    rows = near.shape[1]
    width = near.shape[2]
    low_half = lax.broadcasted_iota(jnp.int32, (rows, 128), 1) < HEAD_SIZE
    low_all = lax.broadcasted_iota(jnp.int32, (2 * rows, 128), 1) < HEAD_SIZE
    for pair in range(width // 128):
        cols = pl.ds(pair * 128, 128)
        k_pair = key[:, cols]
        v_pair = value[:, cols]
        for half, (grads, out) in enumerate(((grad_first(), near), (grad_second(), far))):
            q_pair = query[pl.ds(half * rows, rows), cols]
            g_pair = grads[:, cols]
            dq, dk, dv = [], [], []
            for side in range(2):
                keep = low_half if side == 0 else ~low_half
                scores = dot_t(jnp.where(keep, q_pair, jnp.zeros_like(q_pair)), k_pair)
                weights = jnp.exp(scores - jnp.max(scores, -1, keepdims=True))
                total = jnp.sum(weights, -1, keepdims=True)
                probs = weights * (1.0 / total)
                grad_probs = dot_t(jnp.where(keep, g_pair, jnp.zeros_like(g_pair)), v_pair)
                inner = probs * grad_probs
                grad_scores = (inner - probs * jnp.sum(inner, -1, keepdims=True)).astype(BF16)
                dv.append(dot_l(probs.astype(BF16), g_pair))
                dq.append(dot(grad_scores, k_pair))
                dk.append(dot_l(grad_scores, q_pair))
            out[0, :, cols] = (jnp.where(low_half, dq[0], dq[1]).astype(BF16).astype(F32) * 0.125).astype(BF16)
            dk_pair = jnp.where(low_all, dk[0], dk[1])
            dv_pair = jnp.where(low_all, dv[0], dv[1])
            if half == 0:
                key_sum[...] = dk_pair
                value_sum[...] = dv_pair
        for i, (part, last) in enumerate(((key_sum, dk_pair), (value_sum, dv_pair))):
            total = (part[...] + last).astype(BF16)
            near[1 + i, :, cols] = total[:rows]
            far[1 + i, :, cols] = total[rows:]


def attend_back(query, key, value, grad_first, grad_second, name):
    length, width = query.shape
    args = [(query, THERE), (key, THERE), (value, THERE), (grad_first, HERE), (grad_second, HERE)]
    outs = [((3, length // 2, width), BF16, HERE)] * 2
    return call(attend_back_kernel, args, outs, VM[1], COSTS[name], [pltpu.VMEM((length, 128), F32), pltpu.VMEM((length, 128), F32)])


def mix_out_kernel(given, result):
    mix, mix_peer, weight, weight_peer = given
    out = dot(mix()[...], weight()[...]) + dot(mix_peer()[...], weight_peer()[...])
    result[0].ref[...] = out
    result[1].ref[...] = out.astype(BF16)


def mix_out(mix, mix_peer, weight, weight_peer):
    args = [(mix, HERE), (mix_peer, HERE), (weight, HERE), (weight_peer, HERE)]
    dims = (mix.shape[0], weight.shape[1])
    return call(mix_out_kernel, args, [(dims, F32, HERE), (dims, BF16, HERE)], 4, COSTS["mix_out"])


def center_scale(values):
    center = values - jnp.mean(values, -1, keepdims=True)
    spread = jnp.mean(center * center, -1, keepdims=True)
    scale = lax.rsqrt(spread + EPSILON)
    return center * scale, scale


def norm_back(grad, unit, scale, gain):
    grad_unit = grad * gain
    return scale * (
        grad_unit
        - jnp.mean(grad_unit, -1, keepdims=True)
        - unit * jnp.mean(grad_unit * unit, -1, keepdims=True)
    )


def gate(pre):
    cdf = 0.5 * (1.0 + lax.erf(pre * np.float32(np.sqrt(0.5))))
    density = np.float32(1 / np.sqrt(2 * np.pi)) * jnp.exp(-0.5 * pre * pre)
    return pre * cdf, cdf + pre * density


def feed_kernel(own, given, result):
    tok, low, far, out_bias, gain, shift, bias, bias_peer = (item()[...].astype(F32) for item in given[:8])
    weights = given[8:]
    if own:
        first, wide, result = result[0], result[1], result[2:]
    normed, act, act_peer, slope, slope_peer, out = result
    first_sum = tok + low + far + out_bias
    unit, _ = center_scale(first_sum)
    value = unit * gain + shift
    if own:
        first.ref[...] = first_sum
        first.send()
        wide.ref[...] = value
    normed.ref[...] = value.astype(BF16)
    normed.send()
    step = 256
    for weight, bias_of, act_of, slope_of in ((weights[0], bias, act, slope), (weights[1], bias_peer, act_peer, slope_peer)):
        for start in range(0, act_of.ref.shape[1], step):
            cols = pl.ds(start, step)
            pre = dot(normed.ref[...], weight()[:, cols]) + bias_of[:, start : start + step]
            act_of.ref[:, cols], slope_of.ref[:, cols] = (
                part.astype(kind) for part, kind in zip(gate(pre), (BF16, F32))
            )
        act_of.send()
        slope_of.send()
    total = dot(act.ref[...], weights[2]()[...]) + dot(act_peer.ref[...], weights[3]()[...])
    out.ref[...] = total.astype(out.ref.dtype)


def feed(own, tok, low, far, out_bias, gain, shift, bias, bias_peer, weights):
    rows, model = tok.shape
    hidden = weights[0].shape[1]
    outs = [((rows, model), F32, THERE), ((rows, model), F32, HERE)] if own else []
    outs += [((rows, model), BF16, HERE), ((rows, hidden), BF16, THERE), ((rows, hidden), BF16, HERE)]
    outs += [((rows, hidden), F32, THERE)] * 2
    outs.append(((rows, model), F32 if own else BF16, HERE))
    args = [(v, HERE) for v in (tok, low, far, out_bias, gain, shift, bias, bias_peer, *weights)]
    return call(functools.partial(feed_kernel, own), args, outs, VM[2], COSTS["feed"])


def second_parts(given):
    wide, feed_sum, far, down_bias, gain, shift, cot = (item()[...].astype(F32) for item in given)
    unit, scale = center_scale(wide + feed_sum + far + down_bias)
    return unit, scale, gain, shift, cot


def second_grad_kernel(given, result):
    unit, scale, gain, _, cot = second_parts(given)
    result[0].ref[...] = norm_back(cot, unit, scale, gain).astype(BF16)


def second_rest_kernel(given, result):
    unit, scale, gain, shift, cot = second_parts(given)
    layer_out, grad, sums = result
    layer_out.ref[...] = (unit * gain + shift).astype(BF16)
    layer_out.send()
    grad_second = norm_back(cot, unit, scale, gain)
    grad.ref[...] = grad_second
    grad.send()
    sums.ref[...] = jnp.zeros_like(sums.ref)
    sums.ref[3:4, :] = jnp.sum(cot * unit, 0, keepdims=True)
    sums.ref[4:5, :] = jnp.sum(cot, 0, keepdims=True)
    sums.ref[5:6, :] = jnp.sum(grad_second, 0, keepdims=True)


def second_grad(*values):
    return call(second_grad_kernel, [(v, HERE) for v in values], [(values[0].shape, BF16, HERE)], 6, COSTS["second_grad"])[0]


def second_rest(*values):
    dims = values[0].shape
    outs = [(dims, BF16, THERE), (dims, F32, THERE), ((8, dims[1]), F32, HERE)]
    return call(second_rest_kernel, [(v, HERE) for v in values], outs, 8, COSTS["second_rest"])


def feed_back_kernel(given, result):
    grad, slope, slope_peer, up, up_peer, down, down_peer, *more = given
    pre, pre_peer, out = result
    step = 256
    for slope_of, pre_of, weight in ((slope, pre, down), (slope_peer, pre_peer, down_peer)):
        for first in range(0, pre.ref.shape[1], step):
            cols = pl.ds(first, step)
            grad_act = dot_t(grad()[...], weight()[cols, :])
            pre_of.ref[:, cols] = (slope_of()[:, cols] * grad_act).astype(BF16)
        pre_of.send()
    total = dot_t(pre.ref[...], up()[...]) + dot_t(pre_peer.ref[...], up_peer()[...])
    for part in more:
        total += part()[...]
    out.ref[...] = total.astype(out.ref.dtype)


def feed_back(grad, slope, slope_peer, weights, wide=None):
    own = wide is not None
    rows, model = grad.shape
    hidden = slope.shape[1]
    outs = [((rows, hidden), BF16, THERE), ((rows, hidden), BF16, HERE)]
    outs.append(((rows, model), F32, THERE) if own else ((rows, model), BF16, HERE))
    args = [(grad, HERE), (slope, THERE), (slope_peer, THERE)] + [(v, HERE) for v in weights] + [(wide, THERE)] * own
    return call(feed_back_kernel, args, outs, VM[3], COSTS["feed_back"])


def summed(left, right):
    total = dot_l(left[0], right[0])
    for a, b in zip(left[1:], right[1:]):
        total += dot_l(a, b)
    return total


def add_products(out, half, left, right, fresh):
    chunks, tall = out.shape[0], out.shape[1] // 2
    rows = pl.ds(half * tall, tall)
    step = 256
    left = [part()[...] for part in left]
    for first in range(0, out.shape[2], step):
        cols = pl.ds(first, step)
        block = summed(left, [part()[:, cols] for part in right]).reshape(chunks, tall, step)
        if fresh:
            out[:, rows, cols] = block
        else:
            out[:, rows, cols] += block


def near_grads_kernel(given, result):
    out, total = (item.ref for item in result)
    add_products(out, 0, given[:2], given[2:4], True)
    left, right = given[4:5], given[5:]
    add_products(out, 1, left, right, True)
    total[...] = dot_l(jnp.ones((right[0].ref.shape[0], 8), BF16), right[0]()[...])


def near_grads(args, vmem):
    wide, tall = args[2][0].shape[1], args[0][0].shape[1] // RING
    outs = [((RING, 2 * tall, wide), F32, HERE), ((8, wide), F32, HERE)]
    return call(near_grads_kernel, args, outs, vmem, COSTS["near_grads"])


def far_grads_kernel(half, given, result, index):
    grads, *given = given
    parts = 2 + half
    left, right, more = given[:parts], given[parts : 2 * parts], given[2 * parts :]
    out, moving = result[0].ref, result[-1].ref
    add_products(out, half, left, right, False)
    if half:
        ones = jnp.ones((right[0].ref.shape[0], 8), BF16)
        result[1].ref[...] = more[0]()[...] + summed([ones] * parts, [part()[...] for part in right])
    tall = moving.shape[0]
    moving[...] = out[index[out.shape[0] // 2], pl.ds(half * tall, tall)].astype(BF16)


def far_grads(half, grads, args, index, vmem, total=None):
    wide, tall = grads.shape[2], grads.shape[1] // 2
    more = [(total, HERE)] if half else []
    outs = [(grads.shape, F32, HERE)] + [((8, wide), F32, HERE)] * half + [((tall, wide), BF16, HERE)]
    body = functools.partial(far_grads_kernel, half)
    return call(body, [(grads, HERE), *args, *more], outs, vmem, COSTS["weight_grad"], index=index, aliases={0: 0})


def first_back_kernel(given, result):
    first, gain, near, far_back, weight, weight_peer, sums_second = given
    grad, grad_low, sent, heads, sums = result
    unit, scale = center_scale(first()[...])
    grad_normed = near()[...] + far_back()[...].astype(F32)
    grad_first = norm_back(grad_normed, unit, scale, gain()[...].astype(F32))
    grad.ref[...] = grad_first
    grad.send()
    low = grad_first.astype(BF16)
    grad_low.ref[...] = low
    width = heads.ref.shape[1]
    sent.ref[:, width:] = low
    heads.ref[...] = dot_t(low, weight()[...]).astype(BF16)
    sent.ref[:, :width] = dot_t(low, weight_peer()[...]).astype(BF16)
    sums.ref[...] = sums_second()[...]
    sums.ref[0:1, :] = jnp.sum(grad_normed * unit, 0, keepdims=True)
    sums.ref[1:2, :] = jnp.sum(grad_normed, 0, keepdims=True)
    sums.ref[2:3, :] = jnp.sum(grad_first, 0, keepdims=True)


def first_back(first, gain, near, far_back, weight, weight_peer, sums):
    dims, width = first.shape, weight.shape[0]
    args = [(first, THERE), (gain, HERE), (near, THERE)]
    args += [(v, HERE) for v in (far_back, weight, weight_peer, sums)]
    outs = [(dims, F32, THERE), (dims, BF16, HERE)]
    outs += [((dims[0], width + dims[1]), BF16, HERE), ((dims[0], width), BF16, HERE), (sums.shape, F32, HERE)]
    return call(first_back_kernel, args, outs, VM[5], COSTS["first_back"])


def heads_back_kernel(given, result):
    grad, weight, weight_peer = given
    sent, heads = (item.ref for item in result)
    low = grad()[...]
    width = heads.shape[1]
    sent[:, width:] = low
    heads[...] = dot_t(low, weight()[...]).astype(BF16)
    sent[:, :width] = dot_t(low, weight_peer()[...]).astype(BF16)


def heads_back(grad, weight, weight_peer):
    rows, model = grad.shape
    width = weight.shape[0]
    outs = [((rows, width + model), BF16, HERE), ((rows, width), BF16, HERE)]
    return call(heads_back_kernel, [(grad, HERE), (weight, HERE), (weight_peer, HERE)], outs, 4, COSTS["heads_back"])


def proj_back_kernel(given, result):
    near, far, weight, weight_peer = (item() for item in given)
    total = dot_t(near[0], weight[0]) + dot_t(far[0], weight_peer[0])
    for i in (1, 2):
        total += dot_t(near[i], weight[i]) + dot_t(far[i], weight_peer[i])
    result[0].ref[...] = total.astype(result[0].ref.dtype)


def proj_back(near, far, weight, weight_peer, kind, space):
    args = [(v, HERE) for v in (near, far, weight, weight_peer)]
    return call(proj_back_kernel, args, [((near.shape[1], weight.shape[1]), kind, space)], VM[7], COSTS["proj_back" if kind == F32 else "proj_back_c"])[0]


def mixed_grad_kernel(given, result, index, total):
    toks, nears, mixes, grads = given[:4], given[4:8], given[8:12], given[12:]
    out, bias, *moving = (item.ref for item in result)
    width = total.shape[1]
    model = total.shape[0] // 3
    chunks = out.shape[0]
    share = width // chunks
    tall = out.shape[1] - model // width * share
    mixed = [part()[...] for part in mixes]
    for j in range(model // width):
        block = summed(mixed, [part()[:, pl.ds(part.ref.shape[1] - model + j * width, width)] for part in grads])
        out[:, pl.ds(tall + j * share, share), :] = block.reshape(chunks, share, width)
    lefts = [part()[...] for part in toks]
    ones = [jnp.ones((lefts[0].shape[0], 8), BF16)] * 4
    for j in range(3):
        right = [part()[j] for part in nears]
        total[pl.ds(j * model, model), :] = summed(lefts, right)
        if j != 1:
            bias[:, pl.ds(j // 2 * width, width)] = summed(ones, right)
    for i in range(chunks):
        out[i, pl.ds(0, tall), :] = total[pl.ds(i * tall, tall), :]
    half = out.shape[1] // 2
    for i, part in enumerate(moving):
        part[...] = out[index[chunks // 2], pl.ds(i * half, half)].astype(BF16)


def mixed_grad(toks, nears, mixes, grads, index, vmem):
    model, width = toks[0].shape[1], mixes[0].shape[1]
    tall = 4 * model // RING
    outs = [((RING, tall, width), F32, HERE), ((8, 2 * width), F32, HERE)] + [((tall // 2, width), BF16, HERE)] * 2
    args = [(v, HERE) for v in (*toks, *nears, *mixes, *grads)]
    return call(mixed_grad_kernel, args, outs, vmem, COSTS["mixed_grad"], [pltpu.VMEM((3 * model, width), F32)], index)


def token_grad_kernel(given, result):
    grad, near, far = given
    result[0].ref[...] = grad()[...] + near()[...] + far()[...].astype(F32)


def token_sum(grad, near, far):
    args = [(grad, THERE), (near, THERE), (far, HERE)]
    return call(token_grad_kernel, args, [(grad.shape, F32, THERE)], 8, COSTS["token_sum"])[0]


def ring_step_kernel(places, given, result, index):
    grad = given[0].ref
    for side, (place, arrived, moving) in enumerate(zip(places, given[1:], result)):
        rows = arrived.ref.shape[0]
        first = side * (grad.shape[1] - rows)
        own = grad[index[place]]
        if rows < grad.shape[1]:
            moving.ref[...] = own.astype(BF16)
        block = pl.ds(first, rows)
        moving.ref[block, :] = (grad[index[place], block] + arrived()[...].astype(F32)).astype(BF16)


def ring_last_kernel(given, result, index):
    grad, ahead, behind = given
    total = grad.ref[index[0]] + ahead()[...].astype(F32) + behind()[...].astype(F32)
    result[0].ref[...] = total
    result[1].ref[...] = total.astype(BF16)


def ring_step(grad, arrived, index, places, us):
    args = [(v, HERE) for v in (grad, *arrived)]
    outs = [(grad.shape[1:], BF16, HERE)] * 2
    return call(functools.partial(ring_step_kernel, places), args, outs, 3, us, index=index)


def ring_last(grad, arrived, index, us):
    args = [(v, HERE) for v in (grad, *arrived)]
    outs = [(grad.shape[1:], kind, HERE) for kind in (F32, BF16)]
    return call(ring_last_kernel, args, outs, 2, us, index=index)


def place_kernel(bands, order, given, result, index, *scratch):
    wides, semaphores = scratch[:-1], scratch[-1]
    copies = []
    for i, place in enumerate(order):
        parts = given[i:] if i == len(order) - 1 else given[i : i + 1]
        chunk = jnp.concatenate([part()[...] for part in parts], 0).astype(F32)
        for j, ((first, rows, columns), wide, out) in enumerate(zip(bands, wides, result)):
            width = chunk.shape[1]
            for k in range(columns // width):
                wide[i, :, pl.ds(k * width, width)] = chunk[first + k * rows : first + (k + 1) * rows]
            target = pl.ds(pl.multiple_of(index[place] * rows, 8), rows)
            copies.append(pltpu.make_async_copy(wide.at[i], out.at[target], semaphores.at[i, j]))
            copies[-1].start()
    for copy in copies:
        copy.wait()


def place(chunks, held, index, bands, order):
    there = pl.BlockSpec(memory_space=pltpu.HBM)
    count, results, parts = len(chunks), len(bands), len(order)
    held = held or ()

    def kernel(index, *refs):
        given, refs = refs[:count], refs[count + len(held) :]
        place_kernel(bands, order, [Given(ref) for ref in given], refs[:results], index, *refs[results:])

    scratch = [pltpu.VMEM((parts, rows, columns), F32) for _, rows, columns in bands]
    return pl.pallas_call(
        kernel,
        out_shape=tuple(pltpu.HBM((RING * rows, columns), F32) for _, rows, columns in bands),
        in_specs=[pl.BlockSpec(memory_space=pltpu.SMEM)]
        + [pl.BlockSpec(memory_space=pltpu.VMEM)] * count
        + [there] * len(held),
        out_specs=tuple(there for _ in bands),
        scratch_shapes=scratch + [pltpu.SemaphoreType.DMA((parts, results))],
        input_output_aliases={1 + count + i: i for i in range(len(held))},
        compiler_params=pltpu.CompilerParams(vmem_limit_bytes=8 * MIB),
        cost_estimate=cost(COSTS["place"]),
    )(index, *chunks, *(keep(v) for v in held))


def add_kernel(given, result):
    total = given[0]()[...] + given[1]()[...]
    result[0].ref[...] = total


def add(a, b):
    return call(add_kernel, [(a, HERE), (b, HERE)], [(a.shape, a.dtype, HERE)], 2, COSTS["add"])[0]


def add_rows_kernel(given, result):
    a, b, hidden, wide = (item() for item in given)
    out = result[0].ref
    out[...] = a[...] + b[...]
    out[6:7, :] = hidden[0:1, :]
    out[7:8, : wide.shape[1]] = wide[0:1, :]


def add_rows(a, b, hidden, wide):
    return call(add_rows_kernel, [(v, HERE) for v in (a, b, hidden, wide)], [(a.shape, F32, HERE)], 2, COSTS["add_rows"])[0]


def swap(values, bit, tensor):
    return lax.ppermute(values, "tensor", [(i, i ^ bit) for i in range(tensor)])


class Line:
    def __init__(self):
        self.last = None

    def run(self, body, *args):
        if self.last is not None:
            args, _ = lax.optimization_barrier((args, self.last))
        out = body(*args)
        self.last = jax.tree.leaves(out)[-1]
        return out

    def land(self, values):
        return lax.optimization_barrier((values, self.last))[0]

    def settle(self, *values):
        self.last = lax.optimization_barrier((values, self.last))[0]
        return self.last if len(values) > 1 else self.last[0]


def ring_order(dp):
    return list(range(0, dp, 2)) + list(range(dp - 1, 0, -2))


class Ring:
    def __init__(self, line, dp, index, bands, name):
        self.bands, self.name = bands, name
        order = ring_order(dp)
        self.ways = [[(order[i], order[(i + way) % dp]) for i in range(dp)] for way in (1, -1)]
        self.line, self.dp, self.index = line, dp, index
        self.step, self.half = 0, dp // 2
        self.flying, self.outs = [], None

    def send(self, *moving):
        for part in moving:
            self.flying.append(lax.ppermute(part, "dp", self.ways[len(self.flying)]))

    def tick(self):
        self.step += 1
        step, half, run = self.step, self.half, self.line.run
        arrived, self.flying = tuple(self.flying), []
        if step < half:
            places = (half - step, self.dp + step - half)
            self.send(*run(functools.partial(ring_step, places=places, us=COSTS[self.name + str(step)]), self.grad, arrived, self.index))
        elif step == half:
            self.total, moving = run(functools.partial(ring_last, us=COSTS[self.name + str(step)]), self.grad, arrived, self.index)
            self.send(moving, moving)
        else:
            step -= half
            arrived = self.line.settle(*arrived)
            if step < half - 1:
                self.send(*arrived)
            elif step < half:
                rows = arrived[0].shape[0] // 2
                self.send(arrived[0][:rows], arrived[1][rows:])
            order = (self.dp - step, step) if step < half else (step,)
            if step == 1:
                arrived, order = (self.total, *arrived), (0, *order)
            self.put(arrived, order)

    def put(self, chunks, order):
        body = functools.partial(place, bands=self.bands, order=order)
        self.outs = self.line.run(body, chunks, self.outs, self.index)


def on_device(
    dp,
    tensor,
    tokens,
    qkv_weight,
    qv_bias,
    out_weight,
    out_bias,
    norm1_gain,
    norm1_bias,
    up_weight,
    up_bias,
    down_weight,
    down_bias,
    norm2_gain,
    norm2_bias,
    cotangent,
):
    core = functools.partial(swap, bit=1, tensor=tensor)
    chip = functools.partial(swap, bit=2, tensor=tensor)
    rows, model = tokens.shape
    width = qkv_weight.shape[2]
    hidden = up_weight.shape[1]
    ring = dp == RING
    room = 8 if ring else 48
    line = Line()
    run, land, settle = line.run, line.land, line.settle

    def row(values):
        return values.reshape(1, -1)

    index = jnp.arange(RING, dtype=jnp.int32)
    if ring:
        turns = np.zeros((dp, dp), np.int32)
        for at, device in enumerate(ring_order(dp)):
            turns[device] = (at + np.arange(dp)) % dp
        index = lax.dynamic_index_in_dim(jnp.asarray(turns), lax.axis_index("dp"), 0, keepdims=False)
        line.last = index
    out_bias, down_bias = row(out_bias), row(down_bias)
    gain1, shift1, gain2, shift2 = (row(v) for v in (norm1_gain, norm1_bias, norm2_gain, norm2_bias))
    tok_a = tokens
    tok_c = chip(tok_a)
    tok_b = core(tok_a)
    out_peer, up_peer = core(out_weight), core(up_weight)
    q_ab, k_ab, v_ab, mix_a, mix_b = run(functools.partial(attend, own=True), tok_a, tok_b, qkv_weight, qv_bias)
    mix_b_peer = core(mix_b)
    out_peer, up_peer = settle(out_peer, up_peer)
    part_a, low_a = run(mix_out, mix_a, mix_b_peer, out_weight, out_peer)
    far_c = chip(low_a)
    down_peer = core(land(down_weight))
    tok_c = settle(tok_c)
    tok_d = core(tok_c)
    q_cd, k_cd, v_cd, mix_c, mix_d = run(attend, tok_c, tok_d, qkv_weight, qv_bias)
    part_c, low_c = run(mix_out, mix_c, core(mix_d), out_weight, out_peer)
    far_a = chip(low_c)
    up_bias_peer, down_peer = settle(core(land(up_bias)), down_peer)
    up_bias, up_bias_peer = row(up_bias), row(up_bias_peer)
    weights = (up_weight, up_peer, down_weight, down_peer)
    nrm_c, act_c, act_peer_c, slope_c, slope_peer_c, feed_c = run(
        functools.partial(feed, False), tok_c, part_c, far_c, out_bias, gain1, shift1, up_bias, up_bias_peer, weights
    )
    far_feed = chip(feed_c)
    act_d, nrm_d = core(act_peer_c), core(nrm_c)
    first_a, wide_a, nrm_a, act_a, act_peer_a, slope_a, slope_peer_a, feed_a = run(
        functools.partial(feed, True), tok_a, part_a, far_a, out_bias, gain1, shift1, up_bias, up_bias_peer, weights
    )
    act_d, nrm_d = settle(act_d, nrm_d)
    act_b, nrm_b = core(act_peer_a), core(nrm_a)
    second = (wide_a, feed_a, land(far_feed), down_bias, gain2, shift2, cotangent)
    gs_a = run(second_grad, *second)
    gs_c = chip(gs_a)
    layer_out, grad_second, sums = run(second_rest, *second)
    act_b, nrm_b = settle(act_b, nrm_b)
    qkv_peer = core(land(qkv_weight))
    gs_b = core(gs_a)
    gp_a, gp_peer_a, back_a = run(
        feed_back, gs_a, slope_a, slope_peer_a, weights, grad_second
    )
    gs_b, qkv_peer = settle(gs_b, qkv_peer)
    gp_b = core(gp_peer_a)

    def add_near(*values):
        return near_grads(list(zip(values, (THERE, HERE, HERE, HERE, HERE, THERE))), room)

    grads, up_sum = run(add_near, act_a, act_b, gs_a, gs_b, nrm_a, gp_a)
    gs_c = settle(gs_c)
    gs_d = core(gs_c)
    gp_c, gp_peer_c, back_c = run(
        feed_back, gs_c, slope_c, slope_peer_c, weights
    )
    far_back = chip(back_c)
    gp_d = core(gp_peer_c)

    half, tall, share = model // RING, 3 * model // RING, width // RING
    ring_feed, ring_mixed = (
        Ring(line, dp, index, bands, name) if ring else None
        for name, bands in (
            ("feed_step", ((0, half, model), (half, half, hidden))),
            ("mixed_step", ((0, tall, width), (tall, share, model))),
        )
    )

    def tick(*items):
        for item in items:
            if ring:
                item.tick()

    def send(item, *moving):
        if ring:
            item.send(*moving)

    def add_far(half, grads, left, right, index, total=None):
        places = ((THERE, HERE), (HERE, HERE)) if half == 0 else ((HERE,) * 3, (HERE, THERE, HERE))
        return far_grads(half, grads, [*zip(left, places[0]), *zip(right, places[1])], index, room, total)

    grads, moving = run(functools.partial(add_far, 0), grads, (act_c, act_d), (gs_c, gs_d), index)
    send(ring_feed, moving)
    grads, up_sum, moving = run(
        functools.partial(add_far, 1), grads, (nrm_b, nrm_c, nrm_d), (gp_b, gp_c, gp_d), index, up_sum
    )
    send(ring_feed, moving)
    if ring:
        ring_feed.grad = grads
    far_back = settle(far_back)
    grad_first, gf_a, sent_a, gh_a, sums = run(
        first_back, first_a, gain1, back_a, far_back, out_weight, out_peer, sums
    )
    gf_c = chip(gf_a)
    back_b = core(sent_a)
    tick(ring_feed)
    back_b = settle(back_b)
    flying = core(sums)
    gr_a, gr_b = run(functools.partial(attend_back, name="attend_back"), q_ab, k_ab, v_ab, gh_a, back_b)
    far_gr_b = core(gr_b)
    tick(ring_feed)
    gf_c = settle(gf_c)
    far_gr_b, flying = settle(far_gr_b, flying)
    sums = run(add, sums, flying)
    sent_c, gh_c = run(heads_back, gf_c, out_weight, out_peer)
    back_d = settle(core(sent_c))
    flying = chip(sums)
    gr_c, gr_d = run(functools.partial(attend_back, name="attend_back_c"), q_cd, k_cd, v_cd, gh_c, back_d)
    grad_mixed, qv_sum, *moving = run(
        functools.partial(mixed_grad, vmem=room),
        (tok_a, tok_b, tok_c, tok_d),
        (gr_a, gr_b, gr_c, gr_d),
        (mix_a, mix_b, mix_c, mix_d),
        (gf_a, back_b, gf_c, back_d),
        index,
    )
    send(ring_mixed, *moving)
    if ring:
        ring_mixed.grad = grad_mixed
    tick(ring_feed)
    tick(ring_mixed)
    flying = settle(flying)
    sums = run(add_rows, sums, flying, up_sum, qv_sum)
    far_gr_d = core(land(gr_d))
    tick(ring_feed)
    far_gr_d = settle(far_gr_d)
    bits = [1 << i for i in range(dp.bit_length() - 1)]

    def hop(values):
        bit = bits.pop(0)
        return lax.ppermute(values, "dp", [(i, i ^ bit) for i in range(dp)])

    flying = hop(sums)
    rows_c = run(functools.partial(proj_back, kind=BF16, space=HERE), gr_c, far_gr_d, qkv_weight, qkv_peer)
    tick(ring_mixed)
    rows_a = run(functools.partial(proj_back, kind=F32, space=THERE), gr_a, far_gr_b, qkv_weight, qkv_peer)
    sums = run(add, sums, flying)
    flying = hop(sums)
    tick(ring_mixed)
    sums = run(add, sums, flying)
    flying = hop(sums)
    tick(ring_feed, ring_mixed)
    sums = run(add, sums, flying)
    while bits:
        sums = run(add, sums, hop(sums))
    far_rows = chip(land(rows_c))
    tick(ring_feed, ring_mixed, ring_mixed, ring_feed)
    token_grad = run(token_sum, grad_first, rows_a, land(far_rows))
    if ring:
        tick(ring_mixed, ring_feed, ring_mixed)
        (grad_down, grad_up), (grad_qkv, grad_out) = ring_feed.outs, ring_mixed.outs
    else:
        grads, grad_mixed = lax.psum((grads, grad_mixed), "dp")
        grad_down, grad_up = grads[:, :half], grads[:, half:]
        grad_qkv = grad_mixed[:, :tall]
        grad_out = grad_mixed[:, tall:].reshape(RING, model // width, share, width).swapaxes(1, 2)
    return (
        layer_out,
        token_grad,
        grad_qkv.reshape(qkv_weight.shape),
        sums[7, : 2 * width].reshape(2, width),
        grad_out.reshape(out_weight.shape),
        sums[2],
        sums[0],
        sums[1],
        grad_up.reshape(up_weight.shape),
        sums[6],
        grad_down.reshape(down_weight.shape),
        sums[5],
        sums[3],
        sums[4],
    )


def solution(mesh):
    dp, tensor = mesh.shape["dp"], mesh.shape["tensor"]
    rows = P(("dp", "tensor"), None)
    placed = (
        rows,
        P(None, None, "tensor"),
        P(None, "tensor"),
        P("tensor", None),
        P(),
        P(),
        P(),
        P(None, "tensor"),
        P("tensor"),
        P("tensor", None),
        P(),
        P(),
        P(),
        rows,
    )
    return jax.shard_map(
        functools.partial(on_device, dp, tensor),
        mesh=mesh,
        in_specs=placed,
        out_specs=(rows, rows) + placed[1:13],
        check_vma=False,
    )
```

```python
import functools

import jax
import jax.numpy as jnp
import numpy as np
from jax import lax
from jax.experimental import pallas as pl
from jax.experimental.pallas import tpu as pltpu
from jax.sharding import PartitionSpec as P

HEAD_SIZE = 64
LENGTH = 512
EPSILON = 1e-05
BF16 = jnp.bfloat16
F32 = jnp.float32
RING = 8
MIB = 2**20


def dot(a, b):
    return jnp.dot(a, b, preferred_element_type=F32)


def dot_t(a, b):
    return lax.dot_general(a, b, (((1,), (1,)), ((), ())), preferred_element_type=F32)


def dot_l(a, b):
    return lax.dot_general(a, b, (((0,), (0,)), ((), ())), preferred_element_type=F32)


class Given:
    def __init__(self, ref, copy=None):
        self.ref, self.copy = ref, copy

    def __call__(self):
        if self.copy is not None:
            self.copy.wait()
            self.copy = None
        return self.ref


class Result:
    def __init__(self, ref, copy=None):
        self.ref, self.copy, self.sent = ref, copy, False

    def send(self):
        if self.copy is not None and not self.sent:
            self.copy.start()
            self.sent = True

    def finish(self):
        self.send()
        if self.copy is not None:
            self.copy.wait()


VM = (6, 6, 8, 8, 8, 8, 8, 4)
HERE, THERE = "vmem", "hbm"


COSTS = {
    "attend": 18.4,
    "attend_back": 0.13,
    "mix_out": 2.4,
    "feed": 0.8,
    "second_grad": 4.0,
    "second_rest": 0.6,
    "feed_back": 22.0,
    "near_grads": 0.64,
    "weight_grad": 0.64,
    "first_back": 0.4,
    "heads_back": 1.2,
    "proj_back": 2.4,
    "mixed_grad": 0.05,
    "token_sum": 4.0,
    "add": 1.0,
    "join": 0.02,
    "place": 0.4,
    "feed_step1": 2.8,
    "feed_step2": 2.8,
    "feed_step3": 0.02,
    "feed_step4": 0.02,
    "mixed_step1": 0.02,
    "mixed_step2": 0.02,
    "mixed_step3": 0.02,
    "mixed_step4": 2.8,
    "attend_back_c": 0.13,
    "proj_back_c": 2.4,
    "add_rows": 1.0,
    "feed_back_c": 22.0,
}


def cost(us):
    return pl.CostEstimate(flops=int(us * 1e9), bytes_accessed=1024, transcendentals=0)


def keep(array):
    return pltpu.with_memory_space_constraint(array, pltpu.HBM)


def call(body, args, outs, vmem, us, scratch=(), index=None, aliases=None):
    spaces = {HERE: pltpu.VMEM, THERE: pltpu.HBM}
    far_in = [i for i, (_, place) in enumerate(args) if place == THERE]
    far_out = [i for i, (_, _, place) in enumerate(outs) if place == THERE]
    scalars = [] if index is None else [index]

    def kernel(*refs):
        scalar, refs = refs[: len(scalars)], refs[len(scalars) :]
        given, refs = list(refs[: len(args)]), refs[len(args) :]
        result, refs = list(refs[: len(outs)]), refs[len(outs) :]
        slots_in, refs = refs[: len(far_in)], refs[len(far_in) :]
        slots_out, refs = refs[: len(far_out)], refs[len(far_out) :]
        if far_in:
            done_in, refs = refs[0], refs[1:]
        if far_out:
            done_out, refs = refs[0], refs[1:]
        given = [Given(ref) for ref in given]
        for slot, i in enumerate(far_in):
            copy = pltpu.make_async_copy(given[i].ref, slots_in[slot], done_in.at[slot])
            copy.start()
            given[i] = Given(slots_in[slot], copy)
        result = [Result(ref) for ref in result]
        for slot, i in enumerate(far_out):
            copy = pltpu.make_async_copy(slots_out[slot], result[i].ref, done_out.at[slot])
            result[i] = Result(slots_out[slot], copy)
        body(given, result, *scalar, *refs)
        for item in given:
            item()
        for item in result:
            item.send()
        for item in result:
            item.finish()

    room = [pltpu.VMEM(args[i][0].shape, args[i][0].dtype) for i in far_in]
    room += [pltpu.VMEM(outs[i][0], outs[i][1]) for i in far_out]
    room += [pltpu.SemaphoreType.DMA((len(far),)) for far in (far_in, far_out) if far]
    return pl.pallas_call(
        kernel,
        out_shape=tuple(
            (pltpu.HBM if place == THERE else jax.ShapeDtypeStruct)(dims, kind) for dims, kind, place in outs
        ),
        in_specs=[pl.BlockSpec(memory_space=pltpu.SMEM)] * len(scalars)
        + [pl.BlockSpec(memory_space=spaces[place]) for _, place in args],
        out_specs=tuple(pl.BlockSpec(memory_space=spaces[place]) for _, _, place in outs),
        scratch_shapes=room + list(scratch),
        input_output_aliases={len(scalars) + i: o for i, o in (aliases or {}).items()},
        compiler_params=pltpu.CompilerParams(vmem_limit_bytes=vmem * MIB),
        cost_estimate=cost(us),
    )(*scalars, *(keep(array) if place == THERE else array for array, place in args))


def attend_kernel(given, result):
    first, second, weight, bias = given
    query, key, value, mixed_first, mixed_second = result
    bias_wide = bias()[...].astype(F32)
    rows = first.ref.shape[0]
    width = query.ref.shape[1]
    weight = weight()
    for half, part in enumerate((first, second)):
        block = pl.ds(half * rows, rows)
        part = part()[...]
        query.ref[block, :] = ((dot(part, weight[0]) + bias_wide[0:1, :]) * 0.125).astype(BF16)
        key.ref[block, :] = dot(part, weight[1]).astype(BF16)
        value.ref[block, :] = (dot(part, weight[2]) + bias_wide[1:2, :]).astype(BF16)
    for item in (query, key, value):
        item.send()
    low_half = lax.broadcasted_iota(jnp.int32, (rows, 128), 1) < HEAD_SIZE
    for half, mixed in enumerate((mixed_second, mixed_first)):
        block = pl.ds((1 - half) * rows, rows)
        for pair in range(width // 128):
            cols = pl.ds(pair * 128, 128)
            q_pair = query.ref[block, cols]
            k_pair = key.ref[:, cols]
            v_pair = value.ref[:, cols]
            outs = []
            for side in range(2):
                keep = low_half if side == 0 else ~low_half
                scores = dot_t(jnp.where(keep, q_pair, jnp.zeros_like(q_pair)), k_pair)
                weights = jnp.exp(scores - jnp.max(scores, -1, keepdims=True))
                total = jnp.sum(weights, -1, keepdims=True)
                probs = (weights * (1.0 / total)).astype(BF16)
                outs.append(dot(probs, v_pair))
            mixed.ref[:, cols] = jnp.where(low_half, outs[0], outs[1]).astype(BF16)


def attend(first, second, weight, bias, own=False):
    rows, width = first.shape[0], weight.shape[2]
    args = [(first, THERE if own else HERE), (second, HERE), (weight, THERE), (bias, THERE)]
    outs = [((2 * rows, width), BF16, THERE)] * 3 + [((rows, width), BF16, HERE)] * 2
    return call(attend_kernel, args, outs, VM[0], COSTS["attend"])


def attend_back_kernel(given, result, key_sum, value_sum):
    query, key, value, grad_first, grad_second = given
    query, key, value = query(), key(), value()
    near, far = (item.ref for item in result)
    rows = near.shape[1]
    width = near.shape[2]
    low_half = lax.broadcasted_iota(jnp.int32, (rows, 128), 1) < HEAD_SIZE
    low_all = lax.broadcasted_iota(jnp.int32, (2 * rows, 128), 1) < HEAD_SIZE
    for pair in range(width // 128):
        cols = pl.ds(pair * 128, 128)
        k_pair = key[:, cols]
        v_pair = value[:, cols]
        for half, (grads, out) in enumerate(((grad_first(), near), (grad_second(), far))):
            q_pair = query[pl.ds(half * rows, rows), cols]
            g_pair = grads[:, cols]
            dq, dk, dv = [], [], []
            for side in range(2):
                keep = low_half if side == 0 else ~low_half
                scores = dot_t(jnp.where(keep, q_pair, jnp.zeros_like(q_pair)), k_pair)
                weights = jnp.exp(scores - jnp.max(scores, -1, keepdims=True))
                total = jnp.sum(weights, -1, keepdims=True)
                probs = weights * (1.0 / total)
                grad_probs = dot_t(jnp.where(keep, g_pair, jnp.zeros_like(g_pair)), v_pair)
                inner = probs * grad_probs
                grad_scores = (inner - probs * jnp.sum(inner, -1, keepdims=True)).astype(BF16)
                dv.append(dot_l(probs.astype(BF16), g_pair))
                dq.append(dot(grad_scores, k_pair))
                dk.append(dot_l(grad_scores, q_pair))
            out[0, :, cols] = (jnp.where(low_half, dq[0], dq[1]).astype(BF16).astype(F32) * 0.125).astype(BF16)
            dk_pair = jnp.where(low_all, dk[0], dk[1])
            dv_pair = jnp.where(low_all, dv[0], dv[1])
            if half == 0:
                key_sum[...] = dk_pair
                value_sum[...] = dv_pair
        for i, (part, last) in enumerate(((key_sum, dk_pair), (value_sum, dv_pair))):
            total = (part[...] + last).astype(BF16)
            near[1 + i, :, cols] = total[:rows]
            far[1 + i, :, cols] = total[rows:]


def attend_back(query, key, value, grad_first, grad_second, name):
    length, width = query.shape
    args = [(query, THERE), (key, THERE), (value, THERE), (grad_first, HERE), (grad_second, HERE)]
    outs = [((3, length // 2, width), BF16, HERE)] * 2
    return call(attend_back_kernel, args, outs, VM[1], COSTS[name], [pltpu.VMEM((length, 128), F32), pltpu.VMEM((length, 128), F32)])


def mix_out_kernel(given, result):
    mix, mix_peer, weight, weight_peer = given
    out = dot(mix()[...], weight()[...]) + dot(mix_peer()[...], weight_peer()[...])
    result[0].ref[...] = out
    result[1].ref[...] = out.astype(BF16)


def mix_out(mix, mix_peer, weight, weight_peer):
    args = [(mix, HERE), (mix_peer, HERE), (weight, HERE), (weight_peer, HERE)]
    dims = (mix.shape[0], weight.shape[1])
    return call(mix_out_kernel, args, [(dims, F32, HERE), (dims, BF16, HERE)], 4, COSTS["mix_out"])


def center_scale(values):
    center = values - jnp.mean(values, -1, keepdims=True)
    spread = jnp.mean(center * center, -1, keepdims=True)
    scale = lax.rsqrt(spread + EPSILON)
    return center * scale, scale


def norm_back(grad, unit, scale, gain):
    grad_unit = grad * gain
    return scale * (
        grad_unit
        - jnp.mean(grad_unit, -1, keepdims=True)
        - unit * jnp.mean(grad_unit * unit, -1, keepdims=True)
    )


def gate(pre):
    cdf = 0.5 * (1.0 + lax.erf(pre * np.float32(np.sqrt(0.5))))
    density = np.float32(1 / np.sqrt(2 * np.pi)) * jnp.exp(-0.5 * pre * pre)
    return pre * cdf, cdf + pre * density


def put_rows(parts, values):
    first = 0
    for part in parts:
        rows = part.ref.shape[0]
        part.ref[...] = values[first : first + rows].astype(part.ref.dtype)
        first += rows


def feed_kernel(own, given, result):
    tok, low, far, out_bias, gain, shift, bias, bias_peer = (item()[...].astype(F32) for item in given[:8])
    weights = given[8:]
    if own:
        first, wide, result = result[0], result[1], result[2:]
    normed, act, act_peer, slope, slope_peer, *outs = result
    first_sum = tok + low + far + out_bias
    unit, _ = center_scale(first_sum)
    value = unit * gain + shift
    if own:
        first.ref[...] = first_sum
        first.send()
        wide.ref[...] = value
    normed.ref[...] = value.astype(BF16)
    normed.send()
    step = 256
    for weight, bias_of, act_of, slope_of in ((weights[0], bias, act, slope), (weights[1], bias_peer, act_peer, slope_peer)):
        for start in range(0, act_of.ref.shape[1], step):
            cols = pl.ds(start, step)
            pre = dot(normed.ref[...], weight()[:, cols]) + bias_of[:, start : start + step]
            act_of.ref[:, cols], slope_of.ref[:, cols] = (
                part.astype(kind) for part, kind in zip(gate(pre), (BF16, F32))
            )
        act_of.send()
        slope_of.send()
    total = dot(act.ref[...], weights[2]()[...]) + dot(act_peer.ref[...], weights[3]()[...])
    put_rows(outs, total)


def feed(own, tok, low, far, out_bias, gain, shift, bias, bias_peer, weights):
    rows, model = tok.shape
    hidden = weights[0].shape[1]
    outs = [((rows, model), F32, THERE), ((rows, model), F32, HERE)] if own else []
    outs += [((rows, model), BF16, HERE), ((rows, hidden), BF16, THERE), ((rows, hidden), BF16, HERE)]
    outs += [((rows, hidden), F32, THERE)] * 2
    outs += [((rows, model), F32, HERE)] if own else [((rows // 2, model), BF16, HERE)] * 2
    args = [(v, HERE) for v in (tok, low, far, out_bias, gain, shift, bias, bias_peer, *weights)]
    return call(functools.partial(feed_kernel, own), args, outs, VM[2], COSTS["feed"])


def second_parts(given, rows=slice(None)):
    wide, feed_sum, *far, down_bias, gain, shift, cot = given
    far = jnp.concatenate([part()[...] for part in far], 0).astype(F32)
    down_bias, gain, shift = (item()[...].astype(F32) for item in (down_bias, gain, shift))
    unit, scale = center_scale(wide()[rows, :] + feed_sum()[rows, :] + far + down_bias)
    return unit, scale, gain, shift, cot()[rows, :].astype(F32)


def second_grad_kernel(at, given, result):
    out = result[0].ref
    unit, scale, gain, _, cot = second_parts(given, pl.ds(at * out.shape[0], out.shape[0]))
    out[...] = norm_back(cot, unit, scale, gain).astype(BF16)


def second_rest_kernel(given, result):
    unit, scale, gain, shift, cot = second_parts(given)
    layer_out, grad, grad_low, sums = result
    layer_out.ref[...] = (unit * gain + shift).astype(BF16)
    layer_out.send()
    grad_second = norm_back(cot, unit, scale, gain)
    grad.ref[...] = grad_second
    grad.send()
    grad_low.ref[...] = grad_second.astype(BF16)
    sums.ref[...] = jnp.zeros_like(sums.ref)
    sums.ref[3:4, :] = jnp.sum(cot * unit, 0, keepdims=True)
    sums.ref[4:5, :] = jnp.sum(cot, 0, keepdims=True)
    sums.ref[5:6, :] = jnp.sum(grad_second, 0, keepdims=True)


def second_grad(at, wide, feed_sum, far, *more):
    args = [(v, HERE) for v in (wide, feed_sum, far, *more)]
    return call(functools.partial(second_grad_kernel, at), args, [(far.shape, BF16, HERE)], 6, COSTS["second_grad"])[0]


def second_rest(wide, *more):
    dims = wide.shape
    outs = [(dims, BF16, THERE), (dims, F32, THERE), (dims, BF16, HERE), ((8, dims[1]), F32, HERE)]
    return call(second_rest_kernel, [(v, HERE) for v in (wide, *more)], outs, 8, COSTS["second_rest"])


def join_kernel(given, result):
    put_rows(result, jnp.concatenate([part()[...] for part in given], 0))


def join(*parts):
    dims = (sum(part.shape[0] for part in parts), parts[0].shape[1])
    return call(join_kernel, [(v, HERE) for v in parts], [(dims, BF16, HERE)], 3, COSTS["join"])[0]


def feed_back_kernel(given, result):
    grad, slope, slope_peer, up, up_peer, down, down_peer, *more = given
    pre, pre_peer, out = result
    step = 256
    for slope_of, pre_of, weight in ((slope, pre, down), (slope_peer, pre_peer, down_peer)):
        for first in range(0, pre.ref.shape[1], step):
            cols = pl.ds(first, step)
            grad_act = dot_t(grad()[...], weight()[cols, :])
            pre_of.ref[:, cols] = (slope_of()[:, cols] * grad_act).astype(BF16)
        pre_of.send()
    total = dot_t(pre.ref[...], up()[...]) + dot_t(pre_peer.ref[...], up_peer()[...])
    for part in more:
        total += part()[...]
    out.ref[...] = total.astype(out.ref.dtype)


def feed_back(grad, slope, slope_peer, weights, wide=None):
    own = wide is not None
    rows, model = grad.shape
    hidden = slope.shape[1]
    outs = [((rows, hidden), BF16, THERE), ((rows, hidden), BF16, HERE)]
    outs.append(((rows, model), F32, THERE) if own else ((rows, model), BF16, HERE))
    args = [(grad, HERE), (slope, THERE), (slope_peer, THERE)] + [(v, HERE) for v in weights] + [(wide, THERE)] * own
    return call(feed_back_kernel, args, outs, VM[3], COSTS["feed_back" if own else "feed_back_c"])


def summed(left, right):
    total = dot_l(left[0], right[0])
    for a, b in zip(left[1:], right[1:]):
        total += dot_l(a, b)
    return total


def add_products(out, half, left, right, fresh):
    chunks, tall = out.shape[0], out.shape[1] // 2
    rows = pl.ds(half * tall, tall)
    step = 256
    left = [part()[...] for part in left]
    for first in range(0, out.shape[2], step):
        cols = pl.ds(first, step)
        block = summed(left, [part()[:, cols] for part in right]).reshape(chunks, tall, step)
        if fresh:
            out[:, rows, cols] = block
        else:
            out[:, rows, cols] += block


def near_grads_kernel(given, result):
    out, total = (item.ref for item in result)
    add_products(out, 0, given[:2], given[2:4], True)
    left, right = given[4:5], given[5:]
    add_products(out, 1, left, right, True)
    total[...] = dot_l(jnp.ones((right[0].ref.shape[0], 8), BF16), right[0]()[...])


def near_grads(args, vmem):
    wide, tall = args[2][0].shape[1], args[0][0].shape[1] // RING
    outs = [((RING, 2 * tall, wide), F32, HERE), ((8, wide), F32, HERE)]
    return call(near_grads_kernel, args, outs, vmem, COSTS["near_grads"])


def far_grads_kernel(half, given, result, index):
    grads, *given = given
    parts = 2 + half
    left, right, more = given[:parts], given[parts : 2 * parts], given[2 * parts :]
    out, moving = result[0].ref, result[-1].ref
    add_products(out, half, left, right, False)
    if half:
        ones = jnp.ones((right[0].ref.shape[0], 8), BF16)
        result[1].ref[...] = more[0]()[...] + summed([ones] * parts, [part()[...] for part in right])
    tall = moving.shape[0]
    moving[...] = out[index[out.shape[0] // 2], pl.ds(half * tall, tall)].astype(BF16)


def far_grads(half, grads, args, index, vmem, total=None):
    wide, tall = grads.shape[2], grads.shape[1] // 2
    more = [(total, HERE)] if half else []
    outs = [(grads.shape, F32, HERE)] + [((8, wide), F32, HERE)] * half + [((tall, wide), BF16, HERE)]
    body = functools.partial(far_grads_kernel, half)
    return call(body, [(grads, HERE), *args, *more], outs, vmem, COSTS["weight_grad"], index=index, aliases={0: 0})


def first_back_kernel(given, result):
    first, gain, near, far_back, weight, weight_peer, sums_second = given
    grad, grad_low, sent, heads, sums = result
    unit, scale = center_scale(first()[...])
    grad_normed = near()[...] + far_back()[...].astype(F32)
    grad_first = norm_back(grad_normed, unit, scale, gain()[...].astype(F32))
    grad.ref[...] = grad_first
    grad.send()
    low = grad_first.astype(BF16)
    grad_low.ref[...] = low
    width = heads.ref.shape[1]
    sent.ref[:, width:] = low
    heads.ref[...] = dot_t(low, weight()[...]).astype(BF16)
    sent.ref[:, :width] = dot_t(low, weight_peer()[...]).astype(BF16)
    sums.ref[...] = sums_second()[...]
    sums.ref[0:1, :] = jnp.sum(grad_normed * unit, 0, keepdims=True)
    sums.ref[1:2, :] = jnp.sum(grad_normed, 0, keepdims=True)
    sums.ref[2:3, :] = jnp.sum(grad_first, 0, keepdims=True)


def first_back(first, gain, near, far_back, weight, weight_peer, sums):
    dims, width = first.shape, weight.shape[0]
    args = [(first, THERE), (gain, HERE), (near, THERE)]
    args += [(v, HERE) for v in (far_back, weight, weight_peer, sums)]
    outs = [(dims, F32, THERE), (dims, BF16, HERE)]
    outs += [((dims[0], width + dims[1]), BF16, HERE), ((dims[0], width), BF16, HERE), (sums.shape, F32, HERE)]
    return call(first_back_kernel, args, outs, VM[5], COSTS["first_back"])


def heads_back_kernel(given, result):
    grad, weight, weight_peer = given
    sent, heads = (item.ref for item in result)
    low = grad()[...]
    width = heads.shape[1]
    sent[:, width:] = low
    heads[...] = dot_t(low, weight()[...]).astype(BF16)
    sent[:, :width] = dot_t(low, weight_peer()[...]).astype(BF16)


def heads_back(grad, weight, weight_peer):
    rows, model = grad.shape
    width = weight.shape[0]
    outs = [((rows, width + model), BF16, HERE), ((rows, width), BF16, HERE)]
    return call(heads_back_kernel, [(grad, HERE), (weight, HERE), (weight_peer, HERE)], outs, 4, COSTS["heads_back"])


def proj_back_kernel(given, result):
    near, far, weight, weight_peer = (item() for item in given)
    total = dot_t(near[0], weight[0]) + dot_t(far[0], weight_peer[0])
    for i in (1, 2):
        total += dot_t(near[i], weight[i]) + dot_t(far[i], weight_peer[i])
    result[0].ref[...] = total.astype(result[0].ref.dtype)


def proj_back(near, far, weight, weight_peer, kind, space):
    args = [(v, HERE) for v in (near, far, weight, weight_peer)]
    return call(proj_back_kernel, args, [((near.shape[1], weight.shape[1]), kind, space)], VM[7], COSTS["proj_back" if kind == F32 else "proj_back_c"])[0]


def mixed_grad_kernel(given, result, index, total):
    toks, nears, mixes, grads = given[:4], given[4:8], given[8:12], given[12:]
    out, bias, *moving = (item.ref for item in result)
    width = total.shape[1]
    model = total.shape[0] // 3
    chunks = out.shape[0]
    share = width // chunks
    tall = out.shape[1] - model // width * share
    mixed = [part()[...] for part in mixes]
    for j in range(model // width):
        block = summed(mixed, [part()[:, pl.ds(part.ref.shape[1] - model + j * width, width)] for part in grads])
        out[:, pl.ds(tall + j * share, share), :] = block.reshape(chunks, share, width)
    lefts = [part()[...] for part in toks]
    ones = [jnp.ones((lefts[0].shape[0], 8), BF16)] * 4
    for j in range(3):
        right = [part()[j] for part in nears]
        total[pl.ds(j * model, model), :] = summed(lefts, right)
        if j != 1:
            bias[:, pl.ds(j // 2 * width, width)] = summed(ones, right)
    for i in range(chunks):
        out[i, pl.ds(0, tall), :] = total[pl.ds(i * tall, tall), :]
    half = out.shape[1] // 2
    for i, part in enumerate(moving):
        part[...] = out[index[chunks // 2], pl.ds(i * half, half)].astype(BF16)


def mixed_grad(toks, nears, mixes, grads, index, vmem):
    model, width = toks[0].shape[1], mixes[0].shape[1]
    tall = 4 * model // RING
    outs = [((RING, tall, width), F32, HERE), ((8, 2 * width), F32, HERE)] + [((tall // 2, width), BF16, HERE)] * 2
    args = [(v, HERE) for v in (*toks, *nears, *mixes, *grads)]
    return call(mixed_grad_kernel, args, outs, vmem, COSTS["mixed_grad"], [pltpu.VMEM((3 * model, width), F32)], index)


def token_grad_kernel(given, result):
    grad, near, far = given
    result[0].ref[...] = grad()[...] + near()[...] + far()[...].astype(F32)


def token_sum(grad, near, far):
    args = [(grad, THERE), (near, THERE), (far, HERE)]
    return call(token_grad_kernel, args, [(grad.shape, F32, THERE)], 8, COSTS["token_sum"])[0]


def ring_step_kernel(places, given, result, index):
    grad = given[0].ref
    for side, (place, arrived, moving) in enumerate(zip(places, given[1:], result)):
        rows = arrived.ref.shape[0]
        first = side * (grad.shape[1] - rows)
        own = grad[index[place]]
        if rows < grad.shape[1]:
            moving.ref[...] = own.astype(BF16)
        block = pl.ds(first, rows)
        moving.ref[block, :] = (grad[index[place], block] + arrived()[...].astype(F32)).astype(BF16)


def ring_last_kernel(given, result, index):
    grad, ahead, behind = given
    total = grad.ref[index[0]] + ahead()[...].astype(F32) + behind()[...].astype(F32)
    result[0].ref[...] = total
    result[1].ref[...] = total.astype(BF16)


def ring_step(grad, arrived, index, places, us):
    args = [(v, HERE) for v in (grad, *arrived)]
    outs = [(grad.shape[1:], BF16, HERE)] * 2
    return call(functools.partial(ring_step_kernel, places), args, outs, 3, us, index=index)


def ring_last(grad, arrived, index, us):
    args = [(v, HERE) for v in (grad, *arrived)]
    outs = [(grad.shape[1:], kind, HERE) for kind in (F32, BF16)]
    return call(ring_last_kernel, args, outs, 2, us, index=index)


def place_kernel(bands, order, given, result, index, *scratch):
    wides, semaphores = scratch[:-1], scratch[-1]
    copies = []
    for i, place in enumerate(order):
        parts = given[i:] if i == len(order) - 1 else given[i : i + 1]
        chunk = jnp.concatenate([part()[...] for part in parts], 0).astype(F32)
        for j, ((first, rows, columns), wide, out) in enumerate(zip(bands, wides, result)):
            width = chunk.shape[1]
            for k in range(columns // width):
                wide[i, :, pl.ds(k * width, width)] = chunk[first + k * rows : first + (k + 1) * rows]
            target = pl.ds(pl.multiple_of(index[place] * rows, 8), rows)
            copies.append(pltpu.make_async_copy(wide.at[i], out.at[target], semaphores.at[i, j]))
            copies[-1].start()
    for copy in copies:
        copy.wait()


def place(chunks, held, index, bands, order):
    there = pl.BlockSpec(memory_space=pltpu.HBM)
    count, results, parts = len(chunks), len(bands), len(order)
    held = held or ()

    def kernel(index, *refs):
        given, refs = refs[:count], refs[count + len(held) :]
        place_kernel(bands, order, [Given(ref) for ref in given], refs[:results], index, *refs[results:])

    scratch = [pltpu.VMEM((parts, rows, columns), F32) for _, rows, columns in bands]
    return pl.pallas_call(
        kernel,
        out_shape=tuple(pltpu.HBM((RING * rows, columns), F32) for _, rows, columns in bands),
        in_specs=[pl.BlockSpec(memory_space=pltpu.SMEM)]
        + [pl.BlockSpec(memory_space=pltpu.VMEM)] * count
        + [there] * len(held),
        out_specs=tuple(there for _ in bands),
        scratch_shapes=scratch + [pltpu.SemaphoreType.DMA((parts, results))],
        input_output_aliases={1 + count + i: i for i in range(len(held))},
        compiler_params=pltpu.CompilerParams(vmem_limit_bytes=8 * MIB),
        cost_estimate=cost(COSTS["place"]),
    )(index, *chunks, *(keep(v) for v in held))


def add_kernel(given, result):
    total = given[0]()[...] + given[1]()[...]
    result[0].ref[...] = total


def add(a, b):
    return call(add_kernel, [(a, HERE), (b, HERE)], [(a.shape, a.dtype, HERE)], 2, COSTS["add"])[0]


def add_rows_kernel(given, result):
    a, b, hidden, wide = (item() for item in given)
    out = result[0].ref
    out[...] = a[...] + b[...]
    out[6:7, :] = hidden[0:1, :]
    out[7:8, : wide.shape[1]] = wide[0:1, :]


def add_rows(a, b, hidden, wide):
    return call(add_rows_kernel, [(v, HERE) for v in (a, b, hidden, wide)], [(a.shape, F32, HERE)], 2, COSTS["add_rows"])[0]


def swap(values, bit, tensor):
    return lax.ppermute(values, "tensor", [(i, i ^ bit) for i in range(tensor)])


class Line:
    def __init__(self):
        self.last = None

    def run(self, body, *args):
        if self.last is not None:
            args, _ = lax.optimization_barrier((args, self.last))
        out = body(*args)
        self.last = jax.tree.leaves(out)[-1]
        return out

    def land(self, values):
        return lax.optimization_barrier((values, self.last))[0]

    def settle(self, *values):
        self.last = lax.optimization_barrier((values, self.last))[0]
        return self.last if len(values) > 1 else self.last[0]


def ring_order(dp):
    return list(range(0, dp, 2)) + list(range(dp - 1, 0, -2))


class Ring:
    def __init__(self, line, dp, index, bands, name):
        self.bands, self.name = bands, name
        order = ring_order(dp)
        self.ways = [[(order[i], order[(i + way) % dp]) for i in range(dp)] for way in (1, -1)]
        self.line, self.dp, self.index = line, dp, index
        self.step, self.half = 0, dp // 2
        self.flying, self.outs = [], None

    def send(self, *moving):
        for part in moving:
            self.flying.append(lax.ppermute(part, "dp", self.ways[len(self.flying)]))

    def tick(self):
        self.step += 1
        step, half, run = self.step, self.half, self.line.run
        arrived, self.flying = tuple(self.flying), []
        if step < half:
            places = (half - step, self.dp + step - half)
            self.send(*run(functools.partial(ring_step, places=places, us=COSTS[self.name + str(step)]), self.grad, arrived, self.index))
        elif step == half:
            self.total, moving = run(functools.partial(ring_last, us=COSTS[self.name + str(step)]), self.grad, arrived, self.index)
            self.send(moving, moving)
        else:
            step -= half
            arrived = self.line.settle(*arrived)
            if step < half - 1:
                self.send(*arrived)
            elif step < half:
                rows = arrived[0].shape[0] // 2
                self.send(arrived[0][:rows], arrived[1][rows:])
            order = (self.dp - step, step) if step < half else (step,)
            if step == 1:
                arrived, order = (self.total, *arrived), (0, *order)
            self.put(arrived, order)

    def put(self, chunks, order):
        body = functools.partial(place, bands=self.bands, order=order)
        self.outs = self.line.run(body, chunks, self.outs, self.index)


def on_device(
    dp,
    tensor,
    tokens,
    qkv_weight,
    qv_bias,
    out_weight,
    out_bias,
    norm1_gain,
    norm1_bias,
    up_weight,
    up_bias,
    down_weight,
    down_bias,
    norm2_gain,
    norm2_bias,
    cotangent,
):
    core = functools.partial(swap, bit=1, tensor=tensor)
    chip = functools.partial(swap, bit=2, tensor=tensor)
    rows, model = tokens.shape
    width = qkv_weight.shape[2]
    hidden = up_weight.shape[1]
    ring = dp == RING
    room = 8 if ring else 48
    line = Line()
    run, land, settle = line.run, line.land, line.settle

    def row(values):
        return values.reshape(1, -1)

    index = jnp.arange(RING, dtype=jnp.int32)
    if ring:
        turns = np.zeros((dp, dp), np.int32)
        for at, device in enumerate(ring_order(dp)):
            turns[device] = (at + np.arange(dp)) % dp
        index = lax.dynamic_index_in_dim(jnp.asarray(turns), lax.axis_index("dp"), 0, keepdims=False)
        line.last = index
    out_bias, down_bias = row(out_bias), row(down_bias)
    gain1, shift1, gain2, shift2 = (row(v) for v in (norm1_gain, norm1_bias, norm2_gain, norm2_bias))
    tok_a = tokens
    tok_c = chip(tok_a)
    tok_b = core(tok_a)
    out_peer, up_peer = core(out_weight), core(up_weight)
    q_ab, k_ab, v_ab, mix_a, mix_b = run(functools.partial(attend, own=True), tok_a, tok_b, qkv_weight, qv_bias)
    mix_b_peer = core(mix_b)
    out_peer, up_peer = settle(out_peer, up_peer)
    part_a, low_a = run(mix_out, mix_a, mix_b_peer, out_weight, out_peer)
    far_c = chip(low_a)
    down_peer = core(land(down_weight))
    tok_c = settle(tok_c)
    tok_d = core(tok_c)
    q_cd, k_cd, v_cd, mix_c, mix_d = run(attend, tok_c, tok_d, qkv_weight, qv_bias)
    part_c, low_c = run(mix_out, mix_c, core(mix_d), out_weight, out_peer)
    far_a = chip(low_c)
    up_bias_peer, down_peer = settle(core(land(up_bias)), down_peer)
    up_bias, up_bias_peer = row(up_bias), row(up_bias_peer)
    weights = (up_weight, up_peer, down_weight, down_peer)
    nrm_c, act_c, act_peer_c, slope_c, slope_peer_c, *feed_c = run(
        functools.partial(feed, False), tok_c, part_c, far_c, out_bias, gain1, shift1, up_bias, up_bias_peer, weights
    )
    far_feed = [chip(part) for part in feed_c]
    act_d, nrm_d = core(act_peer_c), core(nrm_c)
    first_a, wide_a, nrm_a, act_a, act_peer_a, slope_a, slope_peer_a, feed_a = run(
        functools.partial(feed, True), tok_a, part_a, far_a, out_bias, gain1, shift1, up_bias, up_bias_peer, weights
    )
    act_d, nrm_d = settle(act_d, nrm_d)
    act_b, nrm_b = core(act_peer_a), core(nrm_a)
    second = (down_bias, gain2, shift2, cotangent)
    gs_c = []
    for at in range(2):
        far_feed[at] = settle(far_feed[at])
        gs_c.append(chip(run(functools.partial(second_grad, at), wide_a, feed_a, far_feed[at], *second)))
    layer_out, grad_second, gs_a, sums = run(second_rest, wide_a, feed_a, *far_feed, *second)
    act_b, nrm_b = settle(act_b, nrm_b)
    qkv_peer = core(land(qkv_weight))
    gs_b = core(gs_a)
    gp_a, gp_peer_a, back_a = run(
        feed_back, gs_a, slope_a, slope_peer_a, weights, grad_second
    )
    gs_b, qkv_peer = settle(gs_b, qkv_peer)
    gp_b = core(gp_peer_a)

    def add_near(*values):
        return near_grads(list(zip(values, (THERE, HERE, HERE, HERE, HERE, THERE))), room)

    grads, up_sum = run(add_near, act_a, act_b, gs_a, gs_b, nrm_a, gp_a)
    gs_c = run(join, *settle(*gs_c))
    gs_d = core(gs_c)
    gp_c, gp_peer_c, back_c = run(
        feed_back, gs_c, slope_c, slope_peer_c, weights
    )
    far_back = chip(back_c)
    gp_d = core(gp_peer_c)

    half, tall, share = model // RING, 3 * model // RING, width // RING
    ring_feed, ring_mixed = (
        Ring(line, dp, index, bands, name) if ring else None
        for name, bands in (
            ("feed_step", ((0, half, model), (half, half, hidden))),
            ("mixed_step", ((0, tall, width), (tall, share, model))),
        )
    )

    def tick(*items):
        for item in items:
            if ring:
                item.tick()

    def send(item, *moving):
        if ring:
            item.send(*moving)

    def add_far(half, grads, left, right, index, total=None):
        places = ((THERE, HERE), (HERE, HERE)) if half == 0 else ((HERE,) * 3, (HERE, THERE, HERE))
        return far_grads(half, grads, [*zip(left, places[0]), *zip(right, places[1])], index, room, total)

    grads, moving = run(functools.partial(add_far, 0), grads, (act_c, act_d), (gs_c, gs_d), index)
    send(ring_feed, moving)
    grads, up_sum, moving = run(
        functools.partial(add_far, 1), grads, (nrm_b, nrm_c, nrm_d), (gp_b, gp_c, gp_d), index, up_sum
    )
    send(ring_feed, moving)
    if ring:
        ring_feed.grad = grads
    far_back = settle(far_back)
    grad_first, gf_a, sent_a, gh_a, sums = run(
        first_back, first_a, gain1, back_a, far_back, out_weight, out_peer, sums
    )
    gf_c = chip(gf_a)
    back_b = core(sent_a)
    tick(ring_feed)
    back_b = settle(back_b)
    flying = core(sums)
    gr_a, gr_b = run(functools.partial(attend_back, name="attend_back"), q_ab, k_ab, v_ab, gh_a, back_b)
    far_gr_b = core(gr_b)
    tick(ring_feed)
    gf_c = settle(gf_c)
    far_gr_b, flying = settle(far_gr_b, flying)
    sums = run(add, sums, flying)
    sent_c, gh_c = run(heads_back, gf_c, out_weight, out_peer)
    back_d = settle(core(sent_c))
    flying = chip(sums)
    gr_c, gr_d = run(functools.partial(attend_back, name="attend_back_c"), q_cd, k_cd, v_cd, gh_c, back_d)
    grad_mixed, qv_sum, *moving = run(
        functools.partial(mixed_grad, vmem=room),
        (tok_a, tok_b, tok_c, tok_d),
        (gr_a, gr_b, gr_c, gr_d),
        (mix_a, mix_b, mix_c, mix_d),
        (gf_a, back_b, gf_c, back_d),
        index,
    )
    send(ring_mixed, *moving)
    if ring:
        ring_mixed.grad = grad_mixed
    tick(ring_feed)
    tick(ring_mixed)
    flying = settle(flying)
    sums = run(add_rows, sums, flying, up_sum, qv_sum)
    far_gr_d = core(land(gr_d))
    tick(ring_feed)
    far_gr_d = settle(far_gr_d)
    bits = [1 << i for i in range(dp.bit_length() - 1)]

    def hop(values):
        bit = bits.pop(0)
        return lax.ppermute(values, "dp", [(i, i ^ bit) for i in range(dp)])

    flying = hop(sums)
    rows_c = run(functools.partial(proj_back, kind=BF16, space=HERE), gr_c, far_gr_d, qkv_weight, qkv_peer)
    tick(ring_mixed)
    rows_a = run(functools.partial(proj_back, kind=F32, space=THERE), gr_a, far_gr_b, qkv_weight, qkv_peer)
    sums = run(add, sums, flying)
    flying = hop(sums)
    tick(ring_mixed)
    sums = run(add, sums, flying)
    flying = hop(sums)
    tick(ring_feed, ring_mixed)
    sums = run(add, sums, flying)
    while bits:
        sums = run(add, sums, hop(sums))
    far_rows = chip(land(rows_c))
    tick(ring_feed, ring_mixed, ring_mixed, ring_feed)
    token_grad = run(token_sum, grad_first, rows_a, land(far_rows))
    if ring:
        tick(ring_mixed, ring_feed, ring_mixed)
        (grad_down, grad_up), (grad_qkv, grad_out) = ring_feed.outs, ring_mixed.outs
    else:
        grads, grad_mixed = lax.psum((grads, grad_mixed), "dp")
        grad_down, grad_up = grads[:, :half], grads[:, half:]
        grad_qkv = grad_mixed[:, :tall]
        grad_out = grad_mixed[:, tall:].reshape(RING, model // width, share, width).swapaxes(1, 2)
    return (
        layer_out,
        token_grad,
        grad_qkv.reshape(qkv_weight.shape),
        sums[7, : 2 * width].reshape(2, width),
        grad_out.reshape(out_weight.shape),
        sums[2],
        sums[0],
        sums[1],
        grad_up.reshape(up_weight.shape),
        sums[6],
        grad_down.reshape(down_weight.shape),
        sums[5],
        sums[3],
        sums[4],
    )


def solution(mesh):
    dp, tensor = mesh.shape["dp"], mesh.shape["tensor"]
    rows = P(("dp", "tensor"), None)
    placed = (
        rows,
        P(None, None, "tensor"),
        P(None, "tensor"),
        P("tensor", None),
        P(),
        P(),
        P(),
        P(None, "tensor"),
        P("tensor"),
        P("tensor", None),
        P(),
        P(),
        P(),
        rows,
    )
    return jax.shard_map(
        functools.partial(on_device, dp, tensor),
        mesh=mesh,
        in_specs=placed,
        out_specs=(rows, rows) + placed[1:13],
        check_vma=False,
    )
```
